512 devices in a mesh: dp: 2 (over core), ctx: 32 (over x, z), tp: 8 (over y).
Axes of the slice: x: 4, y: 8, z: 8, core: 2. Of those that a mesh axis runs over, the one named last changes fastest.
Arguments:
- reception_entries: bfloat16 [2, 4096, 2048], P('dp', 'ctx', 'tp'), may hold values from -0.75 to 0.75
- address_entries: bfloat16 [2, 4096, 2048], P('dp', 'ctx', 'tp'), may hold values from -0.1796875 to 0.1796875
- payload_entries: bfloat16 [2, 4096, 2048], P('dp', 'ctx', 'tp'), may hold values from -6 to 6
- minus_logarithm_fade: float32 [2, 4096, 2048], P('dp', 'ctx', 'tp'), may hold values from 0 to 1, as said below
- erasure_axis: bfloat16 [2, 4096, 2048], P('dp', 'ctx', 'tp'), may hold values from -1 to 1, as said below
- inline_step_size: bfloat16 [2, 4096, 2048], P('dp', 'ctx', 'tp'), may hold values from 0.0029907227 to 0.29882812
- current_extra_scale: float32 [2048], P('tp'), may hold values from -8 to 8
- emitted_adjoint: bfloat16 [2, 4096, 2048], P('dp', 'ctx', 'tp'), may hold values from -6 to 6
Outputs:
- grad_receptance: bfloat16 [2, 4096, 2048], P('dp', 'ctx', 'tp')
- grad_key: bfloat16 [2, 4096, 2048], P('dp', 'ctx', 'tp')
- grad_value: bfloat16 [2, 4096, 2048], P('dp', 'ctx', 'tp')
- grad_decay: bfloat16 [2, 4096, 2048], P('dp', 'ctx', 'tp')
- grad_kappa: bfloat16 [2, 4096, 2048], P('dp', 'ctx', 'tp')
- grad_rate: bfloat16 [2, 4096, 2048], P('dp', 'ctx', 'tp')
- grad_bonus: float32 [2048], P('tp')
The draws below stay inside these ranges and needn't reach their ends.
Inputs may be any that keep to these rules, and one draw needn't show every extreme that they name: `minus_logarithm_fade`: Positive. `erasure_axis`: each head's 64 entries at a token have unit Euclidean norm up to bfloat16 rounding.
All inputs are finite; a program needn't handle non-finite values.
Results may differ from the reference program's by a relative error of at most 0.0023.
Values sent between devices are 32-bit elements; how exact they have to be, the bound alone decides.
A program may use at most 128 MiB of HBM per device.

```python
import math
import jax
import jax.numpy as jnp
from jax import lax

EMBEDDING_SIZE = 2048
LANES_PER_GROUP = 64
SPAN = 64
TOK_DEV = 128
TOKENS = 4096
SEQS = 2


def draw_erasure_axis(key, part):
    key = jax.random.fold_in(key, 11)
    streams = jax.random.split(key, 3)
    heads_all = EMBEDDING_SIZE // LANES_PER_GROUP
    directions = jax.random.normal(streams[0], (SEQS, 1, heads_all, 4, LANES_PER_GROUP), jnp.float32)
    directions = directions / jnp.sqrt(jnp.sum(directions * directions, axis=-1, keepdims=True) + 1e-12)
    weights = jax.random.normal(streams[1], (SEQS, TOKENS, heads_all, 4), jnp.float32)
    noise = 0.03 * jax.random.normal(streams[2], (SEQS, TOKENS, heads_all, LANES_PER_GROUP), jnp.float32)
    grouped = noise
    for which in range(4):
        grouped = grouped + weights[..., which:which + 1] * directions[:, :, :, which, :]
    grouped = grouped / jnp.sqrt(jnp.sum(grouped * grouped, axis=-1, keepdims=True) + 1e-12)
    return grouped.reshape(SEQS, TOKENS, EMBEDDING_SIZE).astype(jnp.bfloat16)


def draw_minus_logarithm_fade(key, part):
    key = jax.random.fold_in(key, 23)
    streams = jax.random.split(key, 7)
    heads_all = EMBEDDING_SIZE // LANES_PER_GROUP
    fast_share = 0.5
    fast_heads = jax.random.uniform(streams[0], (SEQS, 1, 1, heads_all, 1)) < fast_share
    slow_rate = jnp.exp(jax.random.uniform(streams[1], (SEQS, 1, 1, heads_all, 1), jnp.float32, jnp.log(0.01), jnp.log(0.1))) / TOKENS
    fast_rate = jnp.exp(jax.random.uniform(streams[2], (SEQS, 1, 1, heads_all, 1), jnp.float32, jnp.log(0.03), jnp.log(0.08)))
    base_rate = jnp.where(fast_heads, fast_rate, slow_rate)
    blocks_all = TOKENS // TOK_DEV
    rough = jnp.exp(jax.random.uniform(streams[3], (SEQS, blocks_all, TOK_DEV, heads_all, LANES_PER_GROUP), jnp.float32, jnp.log(0.5), jnp.log(2.0)))
    device_factor = jnp.exp(jax.random.uniform(streams[4], (SEQS, blocks_all, 1, 1, 1), jnp.float32, jnp.log(0.5), jnp.log(2.0)))
    steady = (base_rate * rough * device_factor).reshape(SEQS, TOKENS, heads_all, LANES_PER_GROUP)
    positions = jax.random.randint(streams[5], (SEQS, 3), 0, TOKENS)
    places = jnp.arange(TOKENS)
    struck = jnp.any(places[None, :, None] == positions[:, None, :], axis=-1)
    amount = jax.random.uniform(streams[6], (SEQS, TOKENS, heads_all, LANES_PER_GROUP), jnp.float32, 0.22, 0.5)
    total = steady + jnp.where(struck[:, :, None, None], amount, 0.0)
    return total.reshape(SEQS, TOKENS, EMBEDDING_SIZE)


def steps_of(own_key, dims, cuts, least, largest):
    loudness, own = 1.0, jax.random.fold_in(own_key, 6)
    for axis_at, parts in cuts:
        steps = jnp.exp(jax.random.uniform(jax.random.fold_in(own, axis_at), (parts,), jnp.float32, least / len(cuts), largest / len(cuts)))
        loudness = loudness * jnp.repeat(steps, dims[axis_at] // parts).reshape([-1 if axis == axis_at else 1 for axis in range(len(dims))])
    return loudness


def scatter_about(stream_key, shape, spread, most, shards=(), dtype=jnp.bfloat16):
    values = spread * jax.random.normal(stream_key, shape, jnp.float32)
    if shards:
        values = values * steps_of(stream_key, shape, shards, -0.22, 0.18)
    return jnp.clip(values, -most, most).astype(dtype)


def setup_inputs(seed: int = 0) -> dict:
    key_list = jax.random.split(jax.random.key(seed), 9)
    reception_entries = scatter_about(key_list[0], (SEQS, TOKENS, EMBEDDING_SIZE), 0.125, 0.75, ((0, 2), (1, 32), (2, 8)))
    address_entries = scatter_about(key_list[1], (SEQS, TOKENS, EMBEDDING_SIZE), 0.03, 0.1796875, ((0, 2), (1, 32), (2, 8)))
    payload_entries = scatter_about(key_list[2], (SEQS, TOKENS, EMBEDDING_SIZE), 1.0, 6.0, ((0, 2), (1, 32), (2, 8)))
    minus_logarithm_fade = draw_minus_logarithm_fade(jax.random.fold_in(key_list[8], 71), 0)
    erasure_axis = draw_erasure_axis(jax.random.fold_in(key_list[8], 71), 0)
    inline_step_size = jnp.clip(jnp.exp(math.log(0.29882812) - 4.6043535 * jax.random.uniform(key_list[5], (SEQS, TOKENS, EMBEDDING_SIZE), jnp.float32) ** steps_of(key_list[5], (SEQS, TOKENS, EMBEDDING_SIZE), ((0, 2), (1, 32), (2, 8)), -0.2, 0.2)), 0.0029907227, 0.29882812).astype(jnp.bfloat16)
    current_extra_scale = scatter_about(key_list[6], (EMBEDDING_SIZE,), 2.0, 8.0, ((0, 8),), jnp.float32)
    emitted_adjoint = scatter_about(key_list[7], (SEQS, TOKENS, EMBEDDING_SIZE), 1.0, 6.0, ((0, 2), (1, 32), (2, 8)))
    return dict(reception_entries=reception_entries, address_entries=address_entries, payload_entries=payload_entries, minus_logarithm_fade=minus_logarithm_fade, erasure_axis=erasure_axis, inline_step_size=inline_step_size, current_extra_scale=current_extra_scale, emitted_adjoint=emitted_adjoint)


def evaluate_recurrence(reception_entries, address_entries, payload_entries, minus_logarithm_fade, erasure_axis, inline_step_size, current_extra_scale):
    seqs_all, tok_all, width_all = reception_entries.shape
    attention_groups_py = width_all // LANES_PER_GROUP
    retain = jnp.exp(-minus_logarithm_fade)
    remove = -erasure_axis
    writes = erasure_axis * inline_step_size
    extra_lines = current_extra_scale.reshape(attention_groups_py, LANES_PER_GROUP)

    def to_heads(values):
        return values.reshape(seqs_all, tok_all // SPAN, SPAN, attention_groups_py, LANES_PER_GROUP).transpose(1, 2, 0, 3, 4)
    streams = tuple((to_heads(argument_tensor) for argument_tensor in (reception_entries, address_entries, payload_entries, retain, remove, writes)))

    def token_step(carried_matrix, stretch_cuts):
        reception_tensor, address_scaled, payload_scaled, kept, removing, writing = stretch_cuts
        removal = jnp.einsum('mzup,mzp->mzu', carried_matrix, removing, precision=lax.Precision.HIGHEST)
        carried_matrix = carried_matrix * kept[:, :, None, :] + removal[..., None] * writing[:, :, None, :] + payload_scaled[..., None] * address_scaled[:, :, None, :]
        extra_share = lax.optimization_barrier(jnp.sum(reception_tensor * extra_lines[None] * address_scaled, axis=-1, keepdims=True)) * payload_scaled
        emitted_entry = jnp.einsum('mzup,mzp->mzu', carried_matrix, reception_tensor, precision=lax.Precision.HIGHEST) + extra_share
        return (carried_matrix, emitted_entry)

    @jax.checkpoint
    def span_scan(carried_matrix, stretch_cuts):
        return lax.scan(token_step, carried_matrix, stretch_cuts)
    starting = jnp.zeros((seqs_all, attention_groups_py, LANES_PER_GROUP, LANES_PER_GROUP), jnp.float32)
    unused, output_collection = lax.scan(span_scan, starting, streams)
    return output_collection.transpose(2, 0, 1, 3, 4).reshape(seqs_all, tok_all, width_all)

def reference(reception_entries, address_entries, payload_entries, minus_logarithm_fade, erasure_axis, inline_step_size, current_extra_scale, emitted_adjoint):
    argument_tensors = tuple((argument_tensor.astype(jnp.float32) for argument_tensor in (reception_entries, address_entries, payload_entries, minus_logarithm_fade, erasure_axis, inline_step_size, current_extra_scale)))
    primal_result, pullback_function = jax.vjp(evaluate_recurrence, *argument_tensors)
    derivative_outcomes = pullback_function(emitted_adjoint.astype(jnp.float32))
    return (derivative_outcomes[0].astype(jnp.bfloat16), derivative_outcomes[1].astype(jnp.bfloat16), derivative_outcomes[2].astype(jnp.bfloat16), derivative_outcomes[3].astype(jnp.bfloat16), derivative_outcomes[4].astype(jnp.bfloat16), derivative_outcomes[5].astype(jnp.bfloat16), derivative_outcomes[6].astype(jnp.float32))
```

```python
import functools

import jax
import jax.numpy as jnp
from jax import lax
from jax.experimental import pallas as pl
from jax.experimental.pallas import tpu as pltpu
from jax.sharding import PartitionSpec as P

HEAD = 64
PAIR = 128
F32 = jnp.float32
BF16 = jnp.bfloat16
MESH = pl.DeviceIdType.MESH
NN = (((1,), (0,)), ((), ()))
NT = (((1,), (1,)), ((), ()))


def split(x):
    high = x.astype(BF16)
    low = (x - high.astype(F32)).astype(BF16)
    return high, low


def mm(x, y, dims=NN):
    return lax.dot_general(x, y, dims, preferred_element_type=F32)


def cat(parts, axis):
    return jnp.concatenate(parts, axis=axis)


def dot3(x, y, dims=NN):
    xh, xl = split(x) if not isinstance(x, tuple) else x
    yh, yl = split(y) if not isinstance(y, tuple) else y
    axis = 0 if dims is NN else 1
    if yh.shape == (PAIR, PAIR):
        wide = cat([cat([yh, yl], 1 - axis)] * 2, axis)
        both = mm(cat([xh, xl], 1), wide, dims)
        return both[:, :PAIR] + both[:, PAIR:]
    return mm(cat([xh, xl], 1), cat([yh, yh], axis), dims) + mm(xh, yl, dims)


def dot2(x, y, dims=NN):
    xh, xl = split(x) if not isinstance(x, tuple) else x
    axis = 0 if dims is NN else 1
    return mm(cat([xh, xl], 1), cat([y, y], axis), dims)


def iotas(rows, cols):
    return (
        lax.broadcasted_iota(jnp.int32, (rows, cols), 0),
        lax.broadcasted_iota(jnp.int32, (rows, cols), 1),
    )


def first_half(shape):
    return (lax.broadcasted_iota(jnp.int32, shape, 1) & (PAIR - 1)) < HEAD


def by_head(stacked):
    half = stacked.shape[0] // 2
    top, bottom = stacked[:half], stacked[half:]
    return jnp.where(first_half(top.shape), top, bottom)


def own_lanes(x):
    mine = first_half(x.shape)
    return jnp.where(mine, x, 0.0), jnp.where(mine, 0.0, x)


def compact(blocks):
    return by_head(blocks)


def spread(x):
    return cat(list(own_lanes(x)), 0)


def turned_lanes(x):
    return pltpu.roll(x, HEAD, 1)


def gram_parts(x):
    high = x.astype(BF16).astype(F32)
    low = x - high
    high_t, low_t = turned_lanes(high), turned_lanes(low)
    mine = first_half(x.shape)
    pick = lambda a, b: jnp.where(mine, a, b).astype(BF16)
    return (
        (pick(high, low_t), pick(high, high_t), pick(low, low_t)),
        (pick(high_t, low), pick(high_t, high), pick(low_t, low)),
    )


def gram(lefts, rights):
    out = []
    for h in (0, 1):
        left = cat([x[h][0] for x in lefts], 0)
        right = [cat([x[h][i] for x in rights], 0) for i in (1, 2)]
        out.append(mm(cat([left, left], 1), cat(right, 1), NT))
    return out


def flip(x):
    return jnp.swapaxes(x, 0, 1)


def prepare(r, k, w, kappa, eta):
    n = w.shape[0]
    row, col = iotas(n, n)
    tri = jnp.where(row >= col, 1.0, 0.0).astype(BF16)
    wh = w.astype(BF16)
    rest = w - wh.astype(F32)
    wm = rest.astype(BF16)
    wl = (rest - wm.astype(F32)).astype(BF16)
    c = mm(cat([tri, tri], 1), cat([wh, wm], 0)) + mm(tri, wl)
    mid = c[n // 2 : n // 2 + 1]
    end = c[n - 1 : n]
    grow = jnp.exp(c - mid)
    fall = jnp.exp(mid - c)
    fall_before = jnp.exp(mid - (c - w))
    beta = kappa * eta
    out = dict(
        end=end,
        grow=grow,
        fall=fall,
        fall_before=fall_before,
        to_start=jnp.exp(-mid),
        to_end=jnp.exp(mid - end),
        beta=beta,
        rs=r * fall,
        ks=k * grow,
        bs=beta * grow,
        asc=-kappa * fall_before,
    )
    out["a0"] = out["asc"] * out["to_start"]
    out["r0"] = out["rs"] * out["to_start"]
    out["bf"] = out["bs"] * out["to_end"]
    out["kf"] = out["ks"] * out["to_end"]
    return out


def inverse(lows):
    n = lows[0].shape[0]
    row, col = iotas(n, n)
    eye = jnp.where(row == col, 1.0, 0.0)
    start = (row >> 4) == (col >> 4)
    d1 = [jnp.where(start, low, 0.0) for low in lows]
    s1 = [split(d) for d in d1]
    d2 = [dot3(s, s) for s in s1]
    s2 = [split(d) for d in d2]
    d4 = [dot3(s, s) for s in s2]
    p4 = [eye + a + b + dot3(s, t) for a, b, s, t in zip(d1, d2, s1, s2)]
    s4 = [split(d) for d in d4]
    d8 = [dot3(s, s) for s in s4]
    p8 = [p + dot3(p, s) for p, s in zip(p4, s4)]
    t = [split(p + dot3(p, d)) for p, d in zip(p8, d8)]
    rest = [jnp.where(start, 0.0, low) for low in lows]
    x1 = [split(dot3(s, r)) for s, r in zip(t, rest)]
    x2 = [split(dot3(s, s)) for s in x1]
    y1 = [a[0].astype(F32) + a[1].astype(F32) + dot3(s, a) for s, a in zip(x1, t)]
    x4 = [split(dot3(s, s)) for s in x2]
    y2 = [y + dot3(s, y) for s, y in zip(x2, y1)]
    return [y + dot3(s, y) for s, y in zip(x4, y2)]


def local_grams(r, k, v, w, kappa, eta, dy, bonus):
    n = w.shape[0]
    q = prepare(r, k, w, kappa, eta)
    q.update(r=r, k=k, v=v, dy=dy, bonus=bonus, vb=v.astype(BF16), dyb=dy.astype(BF16))
    row, col = iotas(n, n)
    pa, pr, pb, pk = [gram_parts(q[name]) for name in ("asc", "rs", "bs", "ks")]
    lower = gram([pa], [pb, pk])
    upper = gram([pb, pk], [pr, pa])
    q["lw"] = [jnp.where(row > col, t[:, :n], 0.0) for t in lower]
    q["lk"] = cat([jnp.where(row > col, t[:, n:], 0.0) for t in lower], 0)
    q["wwt"] = cat([jnp.where(col >= row, t[:n, :n], 0.0) for t in upper], 0)
    q["wkt"] = cat([jnp.where(col >= row, t[n:, :n], 0.0) for t in upper], 0)
    q["lkt"] = cat([jnp.where(col > row, t[n:, n:], 0.0) for t in upper], 0)
    q["z"] = by_head(dot2(q["lk"], q["vb"]))
    q["zd"] = by_head(dot2(q["wwt"], q["dyb"]))
    return q


def local_message(q, t):
    n = q["z"].shape[0]
    eu = by_head(dot3(cat(t, 0), cat([q["a0"], q["z"]], 1)))
    fp = by_head(dot3(cat([flip(x) for x in t], 0), cat([q["bf"], q["zd"]], 1)))
    ml = dot3(flip(q["bf"]), eu)
    row, col = iotas(HEAD, PAIR)
    decay = jnp.where(row == (col & (HEAD - 1)), jnp.exp(-q["end"]), 0.0)
    mt = decay + compact(ml[:, :n])
    lt = compact(ml[:, n:] + dot2(flip(q["kf"]), q["vb"]))
    ht = compact(flip(dot3(flip(q["a0"]), fp[:, n:]) + dot2(flip(q["r0"]), q["dyb"])))
    row, col = iotas(PAIR, PAIR)
    ones = jnp.where((row >> 6) == (col >> 6), 1.0, 0.0).astype(BF16)
    dyv = dot2(q["dy"] * q["v"], ones)
    bonus_part = jnp.sum(dyv * q["r"] * q["k"], axis=0, keepdims=True)
    q.update(eu=eu, fp=fp, ones=ones, dyv=dyv)
    return lt, mt, ht, bonus_part


def exact_parts(x):
    other = turned_lanes(x)
    mine = first_half(x.shape)
    pick = lambda a, b: jnp.where(mine, a, b).astype(BF16)
    return pick(x, 0.0), pick(x, other), pick(other, 0.0), pick(other, x)


def local_rest(q):
    n = q["z"].shape[0]
    eu, fp = q["eu"], q["fp"]
    more = by_head(dot3(q["lkt"], fp))
    kg = q["kf"] + more[:, :n]
    dv = more[:, n:] + by_head(dot2(q["wkt"], q["dyb"]))
    dv = dv + dot2(q["r"] * q["k"] * q["bonus"], q["ones"]) * q["dy"]
    narrow = [*split(eu[:, :n]), *split(fp[:, :n]), *split(kg)]
    narrow += [*exact_parts(q["v"]), *exact_parts(q["dy"])]
    deep = [*split(cat([q["bs"], q["ks"]], 0)), *split(cat([q["rs"], q["asc"]], 0))]
    wide = [eu[:, n:], fp[:, n:], dv, q["dyv"], q["fall"], q["fall_before"], q["grow"]]
    lines = [q["bonus"], q["to_start"], q["to_end"], jnp.exp(-q["end"])]
    return narrow, deep, wide, lines


def final_part(r, k, v, kappa, eta, dy, narrow, deep, wide, lines, st, g):
    n = r.shape[0]
    eh, el, fh, fl, kgh, kgl, *exact = narrow
    by, ry = deep[:2], deep[2:]
    u_own, p_own, dv_own, dyv, fall, fall_before, grow = wide
    bonus, to_start, to_end, decay = lines
    vb, dyb = v.astype(BF16), dy.astype(BF16)
    sb = split(spread(st))
    gb = split(spread(g))
    u = u_own + dot3((eh, el), sb)
    p = p_own + dot3((fh, fl), gb, NT)
    dv = dv_own + dot3((kgh, kgl), gb, NT)
    zero = jnp.zeros((n, PAIR), BF16)
    gv = ((exact[0], exact[1], zero), (exact[2], exact[3], zero))
    gy = ((exact[4], exact[5], zero), (exact[6], exact[7], zero))
    gu, gp = gram_parts(u), gram_parts(p)
    row, col = iotas(2 * n, 2 * n)
    t, s = row & (n - 1), col & (n - 1)
    fwd_mask = t >= s + jnp.where(row >= n, 1, 0)
    bwd_mask = s >= t + jnp.where(col >= n, 1, 0)
    fwd = cat([jnp.where(fwd_mask, m, 0.0) for m in gram([gy, gp], [gu, gv])], 0)
    bwd = cat([jnp.where(bwd_mask, m, 0.0) for m in gram([gu, gv], [gy, gp])], 0)

    def apply(mat, y):
        mh, ml = split(mat)
        both = mm(mh, cat(y, 1))
        return by_head(both[:, :PAIR] + both[:, PAIR:] + mm(ml, y[0]))

    ra = apply(fwd, by)
    bk = apply(bwd, ry)
    uh, ul = split(u)
    ph, pl_ = split(p)
    start = dot3((cat([dyb, ph], 0), cat([zero, pl_], 0)), sb, NT)
    behind = dot3((cat([uh, vb], 0), cat([ul, zero], 0)), gb)
    dr = (ra[:n] + start[:n] * to_start) * fall
    da = (ra[n:] + start[n:] * to_start) * fall_before
    reach = grow * to_end
    final_u = behind[:n] * reach
    final_v = behind[n:] * reach
    db = bk[:n] * grow + final_u
    dk = bk[n:] * grow + final_v
    beta = kappa * eta
    inner = beta * final_u + k * final_v
    through = r * dr - k * dk - beta * db
    behind_a = -kappa * da
    row, col = iotas(n, n)
    from_here = jnp.where(col >= row, 1.0, 0.0).astype(BF16)
    after = jnp.where(col > row, 1.0, 0.0).astype(BF16)
    tail = mm(cat([from_here, from_here], 1), cat(split(through), 0)) + mm(
        cat([after, after], 1), cat(split(behind_a), 0)
    )
    turned = compact(flip(spread(st)))
    anchor = jnp.sum(turned * g, axis=0, keepdims=True) * decay + jnp.sum(
        inner, axis=0, keepdims=True
    )
    return (
        dr + bonus * k * dyv,
        dk + bonus * r * dyv,
        dv,
        -(tail + anchor),
        eta * db - da,
        kappa * db,
    )


def read_tokens(refs, p):
    lanes = slice(PAIR * p, PAIR * p + PAIR)
    return [ref[:, lanes].astype(F32) for ref in refs]


def final_kernel(*refs):
    ins, (state, narrow, deep, wide, done), outs = refs[:6], refs[6:11], refs[11:]
    got = final_part(
        *read_tokens(ins, 1),
        [narrow[i] for i in range(NARROW)],
        [deep[i] for i in range(DEEP)],
        [wide[i] for i in range(WIDE)],
        [state[i : i + 1] for i in range(LINES)],
        state[8:72],
        state[72:136],
    )
    for i, (ref, value) in enumerate(zip(outs, got)):
        ref[:, 0:PAIR] = done[i]
        ref[:, PAIR : 2 * PAIR] = value.astype(ref.dtype)
    for p in (0, 1):
        outs[6][:, PAIR * p : PAIR * p + PAIR] = state[136 + 8 * p : 137 + 8 * p]


ROW = 8
ROWS = 4
SEND = 192
BACK = 128
NARROW, DEEP, WIDE, LINES = 14, 4, 7, 4


def owner_of(p, d):
    return 4 * p + 2 * d


def adder_of(p, d):
    return owner_of(p, d) + 1


def joined(a, b):
    both = dot3(cat([b[1], b[2]], 0), cat([spread(a[1]), spread(a[0])], 1))
    return both[:HEAD, PAIR:] + b[0], both[:HEAD, :PAIR], both[HEAD:, :PAIR] + a[2]


def joined_states(a, b):
    both = dot3(b[1], cat([spread(a[1]), spread(a[0])], 1))
    return both[:, PAIR:] + b[0], both[:, :PAIR], None


def joined_adjoints(a, b):
    both = dot3(cat([b[1], b[2]], 0), spread(a[1]))
    return None, both[:HEAD], both[HEAD:] + a[2]


def copy_to(src, dst, ssem, rsem, where):
    return pltpu.make_async_remote_copy(
        src_ref=src,
        dst_ref=dst,
        send_sem=ssem,
        recv_sem=rsem,
        device_id=where,
        device_id_type=MESH,
    )


def front_kernel(*refs):
    (ins, outs, staged, scratch, sems) = refs[:8], refs[8:13], refs[13:21], refs[21:37], refs[37:]
    state, done = outs[0], outs[4]
    kept = scratch[12:], (*outs[1:4], state)
    scratch = scratch[:12]
    msg, recv, two, tot, xin, back, run, land, term, terms, sums, total = scratch
    in_sem, send_sem, recv_sem, xsend, xsem, osend, osem = sems[:7]
    tsend, tsem, ssend, ssem, gsend, gsem = sems[7:]
    d = lax.axis_index("dp")
    ctx = lax.axis_index("ctx")
    x = ctx // ROW
    z = ctx % ROW
    mine = [z == owner_of(p, d) for p in (0, 1)]
    is_owner = jnp.logical_or(*mine)
    pown = jnp.where(mine[1], 1, 0)
    adds = [z == adder_of(p, d) for p in (0, 1)]
    is_adder = jnp.logical_or(*adds)
    padd = jnp.where(adds[1], 1, 0)

    def at(xx, zz, dd=None):
        place = {"ctx": xx * ROW + zz}
        if dd is not None:
            place["dp"] = dd
        return place

    loads = [
        pltpu.make_async_copy(src, dst, in_sem.at[i])
        for i, (src, dst) in enumerate(zip(ins, staged))
    ]
    for load in loads:
        load.start()

    barrier = pltpu.get_barrier_semaphore()

    def greet(where):
        pl.semaphore_signal(barrier, inc=1, device_id=where, device_id_type=MESH)

    for p in (0, 1):
        for place in (owner_of(p, d), adder_of(p, d)):
            pl.when(z != place)(lambda place=place: greet(at(x, place)))

    @pl.when(is_owner | is_adder)
    def _():
        for j in (2, 3, 6, 7):
            greet(at(x, (2 * d + j) % ROW))

    @pl.when(is_owner)
    def _():
        for j in range(1, ROWS):
            greet(at((x + j) % ROWS, z))

    @pl.when(is_adder)
    def _():
        for j in range(1, ROWS):
            greet(at((x + j) % ROWS, z))
        for j in range(ROWS):
            greet(at((x + j) % ROWS, adder_of(padd, 1 - d), 1 - d))

    for load in loads:
        load.wait()
    def to_owner(p):
        return copy_to(
            msg.at[p], recv.at[z], send_sem.at[p], recv_sem.at[z], at(x, owner_of(p, d))
        )

    parts = []
    for p in (0, 1):
        tokens = read_tokens(staged[:6] + staged[7:], p)
        part = local_grams(*tokens, staged[6][:, PAIR * p : PAIR * p + PAIR])
        low, mid, high, bonus = local_message(part, inverse(part["lw"]))
        parts.append(part)
        msg[p, 0:64] = low
        msg[p, 64:128] = mid
        msg[p, 128:192] = high
        term[p] = jnp.broadcast_to(bonus, (8, PAIR))
        if p == 0:
            pl.when(is_owner)(lambda: pl.semaphore_wait(barrier, ROW - 1 + ROWS - 1))
            pl.when(is_adder)(lambda: pl.semaphore_wait(barrier, ROW - 1 + 2 * ROWS - 1))
            pl.when(jnp.logical_not(is_owner | is_adder))(lambda: pl.semaphore_wait(barrier, 4))
        pl.when(jnp.logical_not(mine[p]))(lambda p=p: to_owner(p).start())

    def to_adder(p):
        return copy_to(
            term.at[p], terms.at[z], tsend.at[p], tsem.at[z], at(x, adder_of(p, d))
        )

    for p in (0, 1):
        pl.when(jnp.logical_not(adds[p]))(lambda p=p: to_adder(p).start())

    for p in (0, 1):
        for ref, values in zip(kept[p], local_rest(parts[p])):
            for i, value in enumerate(values):
                if value.shape[0] == 1:
                    ref[i : i + 1] = value
                else:
                    ref[i] = value

    @pl.when(is_adder)
    def _():
        terms[z] = term[padd]
        for j in range(1, ROW):
            zz = (z + j) % ROW
            copy_to(term.at[0], terms.at[zz], tsend.at[0], tsem.at[zz], at(x, zz)).wait_recv()
        part = terms[0]
        for i in range(1, ROW):
            part = part + terms[i]
        me = d * ROWS + x
        sums[me] = part
        places = [((x + j) % ROWS, d) for j in range(1, ROWS)]
        places += [((x + j) % ROWS, 1 - d) for j in range(ROWS)]
        across = [
            copy_to(
                sums.at[me], sums.at[me], ssend.at[i], ssem.at[me], at(xx, adder_of(padd, dd), dd)
            )
            for i, (xx, dd) in enumerate(places)
        ]
        for copy in across:
            copy.start()
        for xx, dd in places:
            slot = dd * ROWS + xx
            copy_to(
                sums.at[slot], sums.at[slot], ssend.at[0], ssem.at[slot], at(xx, z)
            ).wait_recv()
        part = sums[0]
        for i in range(1, 2 * ROWS):
            part = part + sums[i]
        total[padd] = part
        gives = [
            copy_to(total.at[padd], total.at[padd], gsend.at[j], gsem.at[padd], at(x, (z + j) % ROW))
            for j in range(1, ROW)
        ]
        for give in gives:
            give.start()
        for copy in across + gives:
            copy.wait_send()

    @pl.when(is_owner)
    def _():
        recv[z] = msg[pown]
        for steps in ((0, 1, 3), (2,)):
            places = [(z // 2 + j) % (ROW // 2) for j in steps]
            for j, i in zip(steps, places):
                for zz in (2 * i, 2 * i + 1)[1 if j == 0 else 0 :]:
                    copy_to(
                        msg.at[0], recv.at[zz], send_sem.at[0], recv_sem.at[zz], at(x, zz)
                    ).wait_recv()
            blocks = [
                [(recv[zz, 0:64], recv[zz, 64:128], recv[zz, 128:192]) for zz in (2 * i, 2 * i + 1)]
                for i in places
            ]
            for i, got in zip(places, [joined(*both) for both in blocks]):
                two[i, 0:64] = got[0]
                two[i, 64:128] = got[1]
                two[i, 128:192] = got[2]
        pair = [(two[i, 0:64], two[i, 64:128], two[i, 128:192]) for i in range(ROW // 2)]
        four = [joined(pair[0], pair[1]), joined(pair[2], pair[3])]
        whole = joined(four[0], four[1])
        tot[0:64] = whole[0]
        tot[64:128] = whole[1]
        tot[128:192] = whole[2]
        cases = (
            (lambda xx: (xx > x) & (x == 0), 0, 64),
            (lambda xx: (xx > x) & (x != 0), 0, 128),
            (lambda xx: (xx < x) & (x == ROWS - 1), 128, 192),
            (lambda xx: (xx < x) & (x != ROWS - 1), 64, 192),
        )

        def across(xx, low, high, landing):
            rows = pl.ds(low, high - low)
            return copy_to(
                tot.at[rows], xin.at[landing, rows], xsend.at[xx], xsem.at[landing], at(xx, z)
            )

        for xx in range(ROWS):
            for when, low, high in cases:
                pl.when(when(xx))(
                    lambda xx=xx, low=low, high=high: across(xx, low, high, x).start()
                )
        one = [(recv[i, 0:64], recv[i, 64:128], recv[i, 128:192]) for i in range(ROW)]
        before = [None, one[0], pair[0], None, four[0], None, None, None]
        before[3] = joined_states(pair[0], one[2])
        before[5] = joined_states(four[0], one[4])
        before[6] = joined_states(four[0], pair[2])
        before[7] = joined_states(before[6], one[6])
        behind = [None, None, None, four[1], None, pair[3], one[7], None]
        behind[4] = joined_adjoints(one[5], pair[3])
        behind[2] = joined_adjoints(one[3], four[1])
        behind[1] = joined_adjoints(pair[1], four[1])
        behind[0] = joined_adjoints(one[1], behind[1])

        run[...] = jnp.zeros_like(run)
        for xx in range(ROWS - 1):
            high = 64 if xx == 0 else 128

            @pl.when(x > xx)
            def _(xx=xx, high=high):
                across(xx, 0, high, xx).wait_recv()
                if xx == 0:
                    run[0] = xin[0, 0:64]
                else:
                    run[0] = dot3(xin[xx, 64:128], spread(run[0])) + xin[xx, 0:64]

        for xx in range(ROWS - 1, 0, -1):
            low = 128 if xx == ROWS - 1 else 64

            @pl.when(x < xx)
            def _(xx=xx, low=low):
                across(xx, low, 192, xx).wait_recv()
                if xx == ROWS - 1:
                    run[1] = xin[xx, 128:192]
                else:
                    run[1] = dot3(run[1], spread(xin[xx, 64:128])) + xin[xx, 128:192]

        sg, gg = run[0], run[1]
        moved = dot3(cat([before[i][1] for i in range(1, ROW)], 0), spread(sg))
        for i in range(ROW):
            back[i, 0:64] = sg if i == 0 else moved[64 * i - 64 : 64 * i] + before[i][0]
        gs = split(gg)
        for i in range(0, ROW, 2):
            if i + 1 < ROW - 1:
                got = dot3(gs, cat([spread(behind[i][1]), spread(behind[i + 1][1])], 1))
                back[i, 64:128] = got[:, :PAIR] + behind[i][2]
                back[i + 1, 64:128] = got[:, PAIR:] + behind[i + 1][2]
            else:
                back[i, 64:128] = dot3(gs, spread(behind[i][1])) + behind[i][2]
                back[i + 1, 64:128] = gg

        gives = []
        for j in (4, 3, 5, 2, 6, 1, 7):
            zz = (z + j) % ROW
            gives.append(
                copy_to(back.at[zz], land.at[pown], osend.at[j], osem.at[pown], at(x, zz))
            )
            gives[-1].start()
        land[pown] = back[z]
        for give in gives:
            give.wait_send()
        for xx in range(ROWS):
            for when, low, high in cases:
                pl.when(when(xx))(
                    lambda xx=xx, low=low, high=high: across(xx, low, high, x).wait_send()
                )

    def state_arrives(p):
        @pl.when(jnp.logical_not(mine[p]))
        def _():
            to_owner(p).wait_send()
            copy_to(
                back.at[0], land.at[p], osend.at[0], osem.at[p], at(x, owner_of(p, d))
            ).wait_recv()

    state_arrives(0)
    held, deep_held, wide_held, lines_held = kept[0]
    got = final_part(
        *read_tokens([staged[i] for i in (0, 1, 2, 4, 5, 7)], 0),
        [held[i] for i in range(NARROW)],
        [deep_held[i] for i in range(DEEP)],
        [wide_held[i] for i in range(WIDE)],
        [lines_held[i : i + 1] for i in range(LINES)],
        land[0, 0:64],
        land[0, 64:128],
    )
    for i, value in enumerate(got):
        done[i] = value.astype(done.dtype)
    state_arrives(1)
    state[8:136] = land[1]

    for p in (0, 1):

        @pl.when(jnp.logical_not(adds[p]))
        def _(p=p):
            to_adder(p).wait_send()
            copy_to(
                total.at[p], total.at[p], gsend.at[0], gsem.at[p], at(x, adder_of(p, d))
            ).wait_recv()

    state[136:144] = total[0]
    state[144:152] = total[1]


VMEM = pl.BlockSpec(memory_space=pltpu.VMEM)
HBM = pl.BlockSpec(memory_space=pltpu.HBM)


def local(r, k, v, w, kappa, eta, extra, dy):
    rows, width = r.shape[1], r.shape[2]
    pairs = width // PAIR
    flat = [t.reshape(rows, width) for t in (r, k, v, w, kappa, eta)]
    ins = (*flat, extra.reshape(1, width), dy.reshape(rows, width))
    f32 = lambda *shape: jax.ShapeDtypeStruct(shape, F32)
    dma = lambda n: pltpu.SemaphoreType.DMA((n,))
    bf16 = lambda *shape: jax.ShapeDtypeStruct(shape, BF16)
    kept = pl.pallas_call(
        front_kernel,
        out_shape=(
            f32(BACK + 24, PAIR),
            bf16(NARROW, rows, PAIR),
            bf16(DEEP, 2 * rows, PAIR),
            f32(WIDE, rows, PAIR),
            bf16(6, rows, PAIR),
        ),
        in_specs=[HBM] * 8,
        out_specs=[VMEM] * 5,
        scratch_shapes=[
            *[pltpu.VMEM(t.shape, t.dtype) for t in ins],
            pltpu.VMEM((pairs, SEND, PAIR), F32),
            pltpu.VMEM((ROW, SEND, PAIR), F32),
            pltpu.VMEM((ROW // 2, SEND, PAIR), F32),
            pltpu.VMEM((SEND, PAIR), F32),
            pltpu.VMEM((ROWS, SEND, PAIR), F32),
            pltpu.VMEM((ROW, BACK, PAIR), F32),
            pltpu.VMEM((2, HEAD, PAIR), F32),
            pltpu.VMEM((pairs, BACK, PAIR), F32),
            pltpu.VMEM((pairs, 8, PAIR), F32),
            pltpu.VMEM((ROW, 8, PAIR), F32),
            pltpu.VMEM((2 * ROWS, 8, PAIR), F32),
            pltpu.VMEM((pairs, 8, PAIR), F32),
            pltpu.VMEM((NARROW, rows, PAIR), BF16),
            pltpu.VMEM((DEEP, 2 * rows, PAIR), BF16),
            pltpu.VMEM((WIDE, rows, PAIR), F32),
            pltpu.VMEM((8, PAIR), F32),
            *[dma(n) for n in (8, 2, ROW, ROWS, ROWS, ROW, 2)],
            *[dma(n) for n in (2, ROW, 2 * ROWS, 2 * ROWS, ROW, 2)],
        ],
        compiler_params=pltpu.CompilerParams(
            collective_id=0, has_side_effects=True, vmem_limit_bytes=48 * 1024 * 1024
        ),
    )(*[pltpu.with_memory_space_constraint(t, pltpu.HBM) for t in ins])
    *grads, bonus = pl.pallas_call(
        final_kernel,
        out_shape=(*[bf16(rows, width)] * 6, f32(1, width)),
        in_specs=[VMEM] * 11,
        out_specs=[VMEM] * 7,
        compiler_params=pltpu.CompilerParams(vmem_limit_bytes=40 * 1024 * 1024),
    )(*[ins[i] for i in (0, 1, 2, 4, 5, 7)], *kept)
    return (*[t.reshape(1, rows, width) for t in grads], bonus.reshape(width))


def solution(mesh):
    block = P("dp", "ctx", "tp")
    return jax.shard_map(
        local,
        mesh=mesh,
        in_specs=(block,) * 6 + (P("tp"), block),
        out_specs=(block,) * 6 + (P("tp"),),
        check_vma=False,
    )
```

```python
import functools

import jax
import jax.numpy as jnp
from jax import lax
from jax.experimental import pallas as pl
from jax.experimental.pallas import tpu as pltpu
from jax.sharding import PartitionSpec as P

HEAD = 64
PAIR = 128
F32 = jnp.float32
BF16 = jnp.bfloat16
MESH = pl.DeviceIdType.MESH
NN = (((1,), (0,)), ((), ()))
NT = (((1,), (1,)), ((), ()))


def split(x):
    high = x.astype(BF16)
    low = (x - high.astype(F32)).astype(BF16)
    return high, low


def mm(x, y, dims=NN):
    return lax.dot_general(x, y, dims, preferred_element_type=F32)


def cat(parts, axis):
    return jnp.concatenate(parts, axis=axis)


def dot3(x, y, dims=NN):
    xh, xl = split(x) if not isinstance(x, tuple) else x
    yh, yl = split(y) if not isinstance(y, tuple) else y
    axis = 0 if dims is NN else 1
    if yh.shape == (PAIR, PAIR):
        wide = cat([cat([yh, yl], 1 - axis)] * 2, axis)
        both = mm(cat([xh, xl], 1), wide, dims)
        return both[:, :PAIR] + both[:, PAIR:]
    return mm(cat([xh, xl], 1), cat([yh, yh], axis), dims) + mm(xh, yl, dims)


def dot2(x, y, dims=NN):
    xh, xl = split(x) if not isinstance(x, tuple) else x
    axis = 0 if dims is NN else 1
    return mm(cat([xh, xl], 1), cat([y, y], axis), dims)


def iotas(rows, cols):
    return (
        lax.broadcasted_iota(jnp.int32, (rows, cols), 0),
        lax.broadcasted_iota(jnp.int32, (rows, cols), 1),
    )


def first_half(shape):
    return (lax.broadcasted_iota(jnp.int32, shape, 1) & (PAIR - 1)) < HEAD


def by_head(stacked):
    half = stacked.shape[0] // 2
    top, bottom = stacked[:half], stacked[half:]
    return jnp.where(first_half(top.shape), top, bottom)


def own_lanes(x):
    mine = first_half(x.shape)
    return jnp.where(mine, x, 0.0), jnp.where(mine, 0.0, x)


def compact(blocks):
    return by_head(blocks)


def spread(x):
    return cat(list(own_lanes(x)), 0)


def turned_lanes(x):
    return pltpu.roll(x, HEAD, 1)


def gram_parts(x):
    high = x.astype(BF16).astype(F32)
    low = x - high
    high_t, low_t = turned_lanes(high), turned_lanes(low)
    mine = first_half(x.shape)
    pick = lambda a, b: jnp.where(mine, a, b).astype(BF16)
    return (
        (pick(high, low_t), pick(high, high_t), pick(low, low_t)),
        (pick(high_t, low), pick(high_t, high), pick(low_t, low)),
    )


def gram(lefts, rights):
    out = []
    for h in (0, 1):
        left = cat([x[h][0] for x in lefts], 0)
        right = [cat([x[h][i] for x in rights], 0) for i in (1, 2)]
        out.append(mm(cat([left, left], 1), cat(right, 1), NT))
    return out


def flip(x):
    return jnp.swapaxes(x, 0, 1)


def prepare(r, k, w, kappa, eta):
    n = w.shape[0]
    row, col = iotas(n, n)
    tri = jnp.where(row >= col, 1.0, 0.0).astype(BF16)
    wh = w.astype(BF16)
    rest = w - wh.astype(F32)
    wm = rest.astype(BF16)
    wl = (rest - wm.astype(F32)).astype(BF16)
    c = mm(cat([tri, tri], 1), cat([wh, wm], 0)) + mm(tri, wl)
    mid = c[n // 2 : n // 2 + 1]
    end = c[n - 1 : n]
    grow = jnp.exp(c - mid)
    fall = jnp.exp(mid - c)
    fall_before = jnp.exp(mid - (c - w))
    beta = kappa * eta
    out = dict(
        end=end,
        grow=grow,
        fall=fall,
        fall_before=fall_before,
        to_start=jnp.exp(-mid),
        to_end=jnp.exp(mid - end),
        beta=beta,
        rs=r * fall,
        ks=k * grow,
        bs=beta * grow,
        asc=-kappa * fall_before,
    )
    out["a0"] = out["asc"] * out["to_start"]
    out["r0"] = out["rs"] * out["to_start"]
    out["bf"] = out["bs"] * out["to_end"]
    out["kf"] = out["ks"] * out["to_end"]
    return out


def inverse(lows):
    n = lows[0].shape[0]
    row, col = iotas(n, n)
    eye = jnp.where(row == col, 1.0, 0.0)
    start = (row >> 4) == (col >> 4)
    d1 = [jnp.where(start, low, 0.0) for low in lows]
    s1 = [split(d) for d in d1]
    d2 = [dot3(s, s) for s in s1]
    s2 = [split(d) for d in d2]
    d4 = [dot3(s, s) for s in s2]
    p4 = [eye + a + b + dot3(s, t) for a, b, s, t in zip(d1, d2, s1, s2)]
    s4 = [split(d) for d in d4]
    d8 = [dot3(s, s) for s in s4]
    p8 = [p + dot3(p, s) for p, s in zip(p4, s4)]
    t = [split(p + dot3(p, d)) for p, d in zip(p8, d8)]
    rest = [jnp.where(start, 0.0, low) for low in lows]
    x1 = [split(dot3(s, r)) for s, r in zip(t, rest)]
    x2 = [split(dot3(s, s)) for s in x1]
    y1 = [a[0].astype(F32) + a[1].astype(F32) + dot3(s, a) for s, a in zip(x1, t)]
    x4 = [split(dot3(s, s)) for s in x2]
    y2 = [y + dot3(s, y) for s, y in zip(x2, y1)]
    return [y + dot3(s, y) for s, y in zip(x4, y2)]


def local_grams(r, k, v, w, kappa, eta, dy, bonus):
    n = w.shape[0]
    q = prepare(r, k, w, kappa, eta)
    q.update(r=r, k=k, v=v, dy=dy, bonus=bonus, vb=v.astype(BF16), dyb=dy.astype(BF16))
    row, col = iotas(n, n)
    pa, pr, pb, pk = [gram_parts(q[name]) for name in ("asc", "rs", "bs", "ks")]
    lower = gram([pa], [pb, pk])
    upper = gram([pb, pk], [pr, pa])
    q["lw"] = [jnp.where(row > col, t[:, :n], 0.0) for t in lower]
    q["lk"] = cat([jnp.where(row > col, t[:, n:], 0.0) for t in lower], 0)
    q["wwt"] = cat([jnp.where(col >= row, t[:n, :n], 0.0) for t in upper], 0)
    q["wkt"] = cat([jnp.where(col >= row, t[n:, :n], 0.0) for t in upper], 0)
    q["lkt"] = cat([jnp.where(col > row, t[n:, n:], 0.0) for t in upper], 0)
    q["z"] = by_head(dot2(q["lk"], q["vb"]))
    q["zd"] = by_head(dot2(q["wwt"], q["dyb"]))
    return q


def local_message(q, t):
    n = q["z"].shape[0]
    eu = by_head(dot3(cat(t, 0), cat([q["a0"], q["z"]], 1)))
    fp = by_head(dot3(cat([flip(x) for x in t], 0), cat([q["bf"], q["zd"]], 1)))
    ml = dot3(flip(q["bf"]), eu)
    row, col = iotas(HEAD, PAIR)
    decay = jnp.where(row == (col & (HEAD - 1)), jnp.exp(-q["end"]), 0.0)
    mt = decay + compact(ml[:, :n])
    lt = compact(ml[:, n:] + dot2(flip(q["kf"]), q["vb"]))
    ht = compact(flip(dot3(flip(q["a0"]), fp[:, n:]) + dot2(flip(q["r0"]), q["dyb"])))
    row, col = iotas(PAIR, PAIR)
    ones = jnp.where((row >> 6) == (col >> 6), 1.0, 0.0).astype(BF16)
    dyv = dot2(q["dy"] * q["v"], ones)
    bonus_part = jnp.sum(dyv * q["r"] * q["k"], axis=0, keepdims=True)
    q.update(eu=eu, fp=fp, ones=ones, dyv=dyv)
    return lt, mt, ht, bonus_part


def exact_parts(x):
    other = turned_lanes(x)
    mine = first_half(x.shape)
    pick = lambda a, b: jnp.where(mine, a, b).astype(BF16)
    return pick(x, 0.0), pick(x, other), pick(other, 0.0), pick(other, x)


def local_rest(q):
    n = q["z"].shape[0]
    eu, fp = q["eu"], q["fp"]
    more = by_head(dot3(q["lkt"], fp))
    kg = q["kf"] + more[:, :n]
    dv = more[:, n:] + by_head(dot2(q["wkt"], q["dyb"]))
    dv = dv + dot2(q["r"] * q["k"] * q["bonus"], q["ones"]) * q["dy"]
    narrow = [*split(eu[:, :n]), *split(fp[:, :n]), *split(kg)]
    narrow += [*exact_parts(q["v"]), *exact_parts(q["dy"])]
    deep = [*split(cat([q["bs"], q["ks"]], 0)), *split(cat([q["rs"], q["asc"]], 0))]
    wide = [eu[:, n:], fp[:, n:], dv, q["dyv"], q["fall"], q["fall_before"], q["grow"]]
    lines = [q["bonus"], q["to_start"], q["to_end"], jnp.exp(-q["end"])]
    return narrow, deep, wide, lines


def final_part(r, k, v, kappa, eta, dy, narrow, deep, wide, lines, st, g):
    n = r.shape[0]
    eh, el, fh, fl, kgh, kgl, *exact = narrow
    by, ry = deep[:2], deep[2:]
    u_own, p_own, dv_own, dyv, fall, fall_before, grow = wide
    bonus, to_start, to_end, decay = lines
    vb, dyb = v.astype(BF16), dy.astype(BF16)
    sb = split(spread(st))
    gb = split(spread(g))
    u = u_own + dot3((eh, el), sb)
    p = p_own + dot3((fh, fl), gb, NT)
    dv = dv_own + dot3((kgh, kgl), gb, NT)
    zero = jnp.zeros((n, PAIR), BF16)
    gv = ((exact[0], exact[1], zero), (exact[2], exact[3], zero))
    gy = ((exact[4], exact[5], zero), (exact[6], exact[7], zero))
    gu, gp = gram_parts(u), gram_parts(p)
    row, col = iotas(2 * n, 2 * n)
    t, s = row & (n - 1), col & (n - 1)
    fwd_mask = t >= s + jnp.where(row >= n, 1, 0)
    bwd_mask = s >= t + jnp.where(col >= n, 1, 0)
    fwd = cat([jnp.where(fwd_mask, m, 0.0) for m in gram([gy, gp], [gu, gv])], 0)
    bwd = cat([jnp.where(bwd_mask, m, 0.0) for m in gram([gu, gv], [gy, gp])], 0)

    def apply(mat, y):
        mh, ml = split(mat)
        both = mm(mh, cat(y, 1))
        return by_head(both[:, :PAIR] + both[:, PAIR:] + mm(ml, y[0]))

    ra = apply(fwd, by)
    bk = apply(bwd, ry)
    uh, ul = split(u)
    ph, pl_ = split(p)
    start = dot3((cat([dyb, ph], 0), cat([zero, pl_], 0)), sb, NT)
    behind = dot3((cat([uh, vb], 0), cat([ul, zero], 0)), gb)
    dr = (ra[:n] + start[:n] * to_start) * fall
    da = (ra[n:] + start[n:] * to_start) * fall_before
    reach = grow * to_end
    final_u = behind[:n] * reach
    final_v = behind[n:] * reach
    db = bk[:n] * grow + final_u
    dk = bk[n:] * grow + final_v
    beta = kappa * eta
    inner = beta * final_u + k * final_v
    through = r * dr - k * dk - beta * db
    behind_a = -kappa * da
    row, col = iotas(n, n)
    from_here = jnp.where(col >= row, 1.0, 0.0).astype(BF16)
    after = jnp.where(col > row, 1.0, 0.0).astype(BF16)
    tail = mm(cat([from_here, from_here], 1), cat(split(through), 0)) + mm(
        cat([after, after], 1), cat(split(behind_a), 0)
    )
    turned = compact(flip(spread(st)))
    anchor = jnp.sum(turned * g, axis=0, keepdims=True) * decay + jnp.sum(
        inner, axis=0, keepdims=True
    )
    return (
        dr + bonus * k * dyv,
        dk + bonus * r * dyv,
        dv,
        -(tail + anchor),
        eta * db - da,
        kappa * db,
    )


def read_tokens(refs, p):
    lanes = slice(PAIR * p, PAIR * p + PAIR)
    return [ref[:, lanes].astype(F32) for ref in refs]


def final_kernel(*refs):
    ins, (state, narrow, deep, wide), outs = refs[:6], refs[6:10], refs[10:]
    got = [
        final_part(
            *read_tokens(ins, p),
            [narrow[p, i] for i in range(NARROW)],
            [deep[p, i] for i in range(DEEP)],
            [wide[p, i] for i in range(WIDE)],
            [state[p, BACK + 8 + i : BACK + 9 + i] for i in range(LINES)],
            state[p, 0:64],
            state[p, 64:128],
        )
        for p in (0, 1)
    ]
    for p in (0, 1):
        lanes = slice(PAIR * p, PAIR * p + PAIR)
        for ref, value in zip(outs, got[p]):
            ref[:, lanes] = value.astype(ref.dtype)
        outs[6][:, lanes] = state[p, BACK : BACK + 1]


ROW = 8
ROWS = 4
SEND = 192
BACK = 128
NARROW, DEEP, WIDE, LINES = 14, 4, 7, 4


def owner_of(p, d):
    return 4 * p + 2 * d


def adder_of(p, d):
    return owner_of(p, d) + 1


def joined(a, b):
    both = dot3(cat([b[1], b[2]], 0), cat([spread(a[1]), spread(a[0])], 1))
    return both[:HEAD, PAIR:] + b[0], both[:HEAD, :PAIR], both[HEAD:, :PAIR] + a[2]


def joined_states(a, b):
    both = dot3(b[1], cat([spread(a[1]), spread(a[0])], 1))
    return both[:, PAIR:] + b[0], both[:, :PAIR], None


def joined_adjoints(a, b):
    both = dot3(cat([b[1], b[2]], 0), spread(a[1]))
    return None, both[:HEAD], both[HEAD:] + a[2]


def copy_to(src, dst, ssem, rsem, where):
    return pltpu.make_async_remote_copy(
        src_ref=src,
        dst_ref=dst,
        send_sem=ssem,
        recv_sem=rsem,
        device_id=where,
        device_id_type=MESH,
    )


def front_kernel(*refs):
    (ins, outs, staged, scratch, sems) = refs[:8], refs[8:12], refs[12:20], refs[20:32], refs[32:]
    state, narrow, deep, wide = outs
    msg, recv, two, tot, xin, back, run, land, term, terms, sums, total = scratch
    in_sem, send_sem, recv_sem, xsend, xsem, osend, osem = sems[:7]
    tsend, tsem, ssend, ssem, gsend, gsem = sems[7:]
    d = lax.axis_index("dp")
    ctx = lax.axis_index("ctx")
    x = ctx // ROW
    z = ctx % ROW
    mine = [z == owner_of(p, d) for p in (0, 1)]
    is_owner = jnp.logical_or(*mine)
    pown = jnp.where(mine[1], 1, 0)
    adds = [z == adder_of(p, d) for p in (0, 1)]
    is_adder = jnp.logical_or(*adds)
    padd = jnp.where(adds[1], 1, 0)

    def at(xx, zz, dd=None):
        place = {"ctx": xx * ROW + zz}
        if dd is not None:
            place["dp"] = dd
        return place

    loads = [
        pltpu.make_async_copy(src, dst, in_sem.at[i])
        for i, (src, dst) in enumerate(zip(ins, staged))
    ]
    for load in loads:
        load.start()

    barrier = pltpu.get_barrier_semaphore()

    def greet(where):
        pl.semaphore_signal(barrier, inc=1, device_id=where, device_id_type=MESH)

    for p in (0, 1):
        for place in (owner_of(p, d), adder_of(p, d)):
            pl.when(z != place)(lambda place=place: greet(at(x, place)))

    @pl.when(is_owner | is_adder)
    def _():
        for j in (2, 3, 6, 7):
            greet(at(x, (2 * d + j) % ROW))

    @pl.when(is_owner)
    def _():
        for j in range(1, ROWS):
            greet(at((x + j) % ROWS, z))

    @pl.when(is_adder)
    def _():
        for j in range(1, ROWS):
            greet(at((x + j) % ROWS, z))
        for j in range(ROWS):
            greet(at((x + j) % ROWS, adder_of(padd, 1 - d), 1 - d))

    for load in loads:
        load.wait()
    parts = []
    for p in (0, 1):
        tokens = read_tokens(staged[:6] + staged[7:], p)
        parts.append(local_grams(*tokens, staged[6][:, PAIR * p : PAIR * p + PAIR]))
    solved = inverse(parts[0]["lw"] + parts[1]["lw"])

    def to_owner(p):
        place = jnp.where(is_owner, (z + 1) % ROW, owner_of(p, d))
        return copy_to(msg.at[p], recv.at[z], send_sem.at[p], recv_sem.at[z], at(x, place))

    pmate = 1 - padd

    def from_mate(p, slot, i, place):
        return copy_to(tot, two.at[i], send_sem.at[p], recv_sem.at[slot], place)

    messages = [local_message(parts[p], solved[2 * p : 2 * p + 2]) for p in (0, 1)]
    for p, (low, mid, high, bonus) in enumerate(messages):
        msg[p, 0:64] = low
        msg[p, 64:128] = mid
        msg[p, 128:192] = high
        term[p] = jnp.broadcast_to(bonus, (8, PAIR))
    pl.when(is_owner)(lambda: pl.semaphore_wait(barrier, ROW - 1 + ROWS - 1))
    pl.when(is_adder)(lambda: pl.semaphore_wait(barrier, ROW - 1 + 2 * ROWS - 1))
    pl.when(jnp.logical_not(is_owner | is_adder))(lambda: pl.semaphore_wait(barrier, 4))
    for p in (0, 1):
        direct = jnp.logical_not(mine[p] | adds[1 - p])
        pl.when(direct)(lambda p=p: to_owner(p).start())

    def over_mate(place):
        rows = pl.ds(64, 128)
        return copy_to(
            msg.at[pmate, rows], xin.at[x, rows], xsend.at[0], xsem.at[x], at(x, place)
        )

    @pl.when(is_adder)
    def _():
        far = (z + ROW - 1) % ROW
        over_mate(far).start()
        copy_to(
            msg.at[0], recv.at[far], send_sem.at[0], recv_sem.at[far], at(x, far)
        ).wait_recv()
        got = joined(
            (recv[far, 0:64], recv[far, 64:128], recv[far, 128:192]),
            (msg[pmate, 0:64], msg[pmate, 64:128], msg[pmate, 128:192]),
        )
        tot[0:64] = got[0]
        tot[64:128] = got[1]
        tot[128:192] = got[2]
        from_mate(pmate, z, z // 2, at(x, owner_of(pmate, d))).start()

    def to_adder(p):
        return copy_to(
            term.at[p], terms.at[z], tsend.at[p], tsem.at[z], at(x, adder_of(p, d))
        )

    for p in (0, 1):
        pl.when(jnp.logical_not(adds[p]))(lambda p=p: to_adder(p).start())

    for p in (0, 1):
        got = local_rest(parts[p])
        for ref, values in zip((narrow, deep, wide), got):
            for i, value in enumerate(values):
                ref[p, i] = value
        for i, line in enumerate(got[3]):
            state[p, BACK + 8 + i : BACK + 9 + i] = line

    @pl.when(is_adder)
    def _():
        terms[z] = term[padd]
        for j in range(1, ROW):
            zz = (z + j) % ROW
            copy_to(term.at[0], terms.at[zz], tsend.at[0], tsem.at[zz], at(x, zz)).wait_recv()
        part = terms[0]
        for i in range(1, ROW):
            part = part + terms[i]
        me = d * ROWS + x
        sums[me] = part
        places = [((x + j) % ROWS, d) for j in range(1, ROWS)]
        places += [((x + j) % ROWS, 1 - d) for j in range(ROWS)]
        across = [
            copy_to(
                sums.at[me], sums.at[me], ssend.at[i], ssem.at[me], at(xx, adder_of(padd, dd), dd)
            )
            for i, (xx, dd) in enumerate(places)
        ]
        for copy in across:
            copy.start()
        for xx, dd in places:
            slot = dd * ROWS + xx
            copy_to(
                sums.at[slot], sums.at[slot], ssend.at[0], ssem.at[slot], at(xx, z)
            ).wait_recv()
        part = sums[0]
        for i in range(1, 2 * ROWS):
            part = part + sums[i]
        total[padd] = part
        gives = [
            copy_to(total.at[padd], total.at[padd], gsend.at[j], gsem.at[padd], at(x, (z + j) % ROW))
            for j in range(1, ROW)
        ]
        for give in gives:
            give.start()
        for copy in across + gives:
            copy.wait_send()

    @pl.when(is_owner)
    def _():
        recv[z] = msg[pown]
        far = (z + ROW // 2) % ROW
        for zz in (far, far + 1):
            recv[zz] = jnp.zeros((SEND, PAIR), F32)
        places = [(z // 2 + j) % (ROW // 2) for j in (0, 1, 3)]
        for j, i in zip((0, 1, 3), places):
            for zz in (2 * i + 1,) if j == 0 else (2 * i, 2 * i + 1):
                copy_to(
                    msg.at[0], recv.at[zz], send_sem.at[0], recv_sem.at[zz], at(x, zz)
                ).wait_recv()
        blocks = [
            [(recv[zz, 0:64], recv[zz, 64:128], recv[zz, 128:192]) for zz in (2 * i, 2 * i + 1)]
            for i in places
        ]
        for i, got in zip(places, [joined(*both) for both in blocks]):
            two[i, 0:64] = got[0]
            two[i, 64:128] = got[1]
            two[i, 128:192] = got[2]
        from_mate(0, far + 1, far // 2, at(x, far + 1)).wait_recv()
        pair = [(two[i, 0:64], two[i, 64:128], two[i, 128:192]) for i in range(ROW // 2)]
        four = [joined(pair[0], pair[1]), joined(pair[2], pair[3])]
        whole = joined(four[0], four[1])
        tot[0:64] = whole[0]
        tot[64:128] = whole[1]
        tot[128:192] = whole[2]
        cases = (
            (lambda xx: (xx > x) & (x == 0), 0, 64),
            (lambda xx: (xx > x) & (x != 0), 0, 128),
            (lambda xx: (xx < x) & (x == ROWS - 1), 128, 192),
            (lambda xx: (xx < x) & (x != ROWS - 1), 64, 192),
        )

        def across(xx, low, high, landing):
            rows = pl.ds(low, high - low)
            return copy_to(
                tot.at[rows], xin.at[landing, rows], xsend.at[xx], xsem.at[landing], at(xx, z)
            )

        for xx in range(ROWS):
            for when, low, high in cases:
                pl.when(when(xx))(
                    lambda xx=xx, low=low, high=high: across(xx, low, high, x).start()
                )
        one = [(recv[i, 0:64], recv[i, 64:128], recv[i, 128:192]) for i in range(ROW)]
        before = [None, one[0], pair[0], None, four[0], None, None, None]
        before[3] = joined_states(pair[0], one[2])
        before[5] = joined_states(four[0], one[4])
        before[6] = joined_states(four[0], pair[2])
        before[7] = joined_states(before[6], one[6])
        behind = [None, None, None, four[1], None, pair[3], one[7], None]
        behind[4] = joined_adjoints(one[5], pair[3])
        behind[2] = joined_adjoints(one[3], four[1])
        behind[1] = joined_adjoints(pair[1], four[1])
        behind[0] = joined_adjoints(one[1], behind[1])

        run[...] = jnp.zeros_like(run)
        for xx in range(ROWS - 1):
            high = 64 if xx == 0 else 128

            @pl.when(x > xx)
            def _(xx=xx, high=high):
                across(xx, 0, high, xx).wait_recv()
                if xx == 0:
                    run[0] = xin[0, 0:64]
                else:
                    run[0] = dot3(xin[xx, 64:128], spread(run[0])) + xin[xx, 0:64]

        for xx in range(ROWS - 1, 0, -1):
            low = 128 if xx == ROWS - 1 else 64

            @pl.when(x < xx)
            def _(xx=xx, low=low):
                across(xx, low, 192, xx).wait_recv()
                if xx == ROWS - 1:
                    run[1] = xin[xx, 128:192]
                else:
                    run[1] = dot3(run[1], spread(xin[xx, 64:128])) + xin[xx, 128:192]

        sg, gg = run[0], run[1]
        moved = dot3(cat([before[i][1] for i in range(1, ROW)], 0), spread(sg))
        for i in range(ROW):
            back[i, 0:64] = sg if i == 0 else moved[64 * i - 64 : 64 * i] + before[i][0]
        gs = split(gg)
        for i in range(0, ROW, 2):
            if i + 1 < ROW - 1:
                got = dot3(gs, cat([spread(behind[i][1]), spread(behind[i + 1][1])], 1))
                back[i, 64:128] = got[:, :PAIR] + behind[i][2]
                back[i + 1, 64:128] = got[:, PAIR:] + behind[i + 1][2]
            else:
                back[i, 64:128] = dot3(gs, spread(behind[i][1])) + behind[i][2]
                back[i + 1, 64:128] = gg

        back[far + 1, 0:64] = back[far, 0:64]
        gives = []
        for j in (4, 5, 3, 2, 6, 1, 7):
            zz = (z + j) % ROW
            source = back.at[far + 1] if j == 4 else back.at[zz]
            gives.append(
                copy_to(source, land.at[pown], osend.at[j], osem.at[pown], at(x, zz))
            )
            gives[-1].start()
        land[pown] = back[z]
        for give in gives:
            give.wait_send()
        for xx in range(ROWS):
            for when, low, high in cases:
                pl.when(when(xx))(
                    lambda xx=xx, low=low, high=high: across(xx, low, high, x).wait_send()
                )

    for p in (0, 1):

        @pl.when(jnp.logical_not(mine[p]))
        def _(p=p):
            to_owner(p).wait_send()
            copy_to(
                back.at[0], land.at[p], osend.at[0], osem.at[p], at(x, owner_of(p, d))
            ).wait_recv()

        @pl.when(adds[1 - p])
        def _(p=p):
            far = (z + ROW - 1) % ROW
            land[p, 0:64] = dot3(recv[far, 64:128], spread(land[p, 0:64])) + recv[far, 0:64]

        @pl.when(mine[1 - p])
        def _(p=p):
            over_mate(z).wait_recv()
            over = dot3(land[p, 64:128], spread(xin[x, 64:128]))
            land[p, 64:128] = over + xin[x, 128:192]

    for p in (0, 1):

        @pl.when(jnp.logical_not(adds[p]))
        def _(p=p):
            to_adder(p).wait_send()
            copy_to(
                total.at[p], total.at[p], gsend.at[0], gsem.at[p], at(x, adder_of(p, d))
            ).wait_recv()

    @pl.when(is_adder)
    def _():
        over_mate(z).wait_send()

    for p in (0, 1):
        state[p, 0:BACK] = land[p]
        state[p, BACK : BACK + 8] = total[p]


VMEM = pl.BlockSpec(memory_space=pltpu.VMEM)
HBM = pl.BlockSpec(memory_space=pltpu.HBM)


def local(r, k, v, w, kappa, eta, extra, dy):
    rows, width = r.shape[1], r.shape[2]
    pairs = width // PAIR
    flat = [t.reshape(rows, width) for t in (r, k, v, w, kappa, eta)]
    ins = (*flat, extra.reshape(1, width), dy.reshape(rows, width))
    f32 = lambda *shape: jax.ShapeDtypeStruct(shape, F32)
    dma = lambda n: pltpu.SemaphoreType.DMA((n,))
    bf16 = lambda *shape: jax.ShapeDtypeStruct(shape, BF16)
    kept = pl.pallas_call(
        front_kernel,
        out_shape=(
            f32(pairs, BACK + 16, PAIR),
            bf16(pairs, NARROW, rows, PAIR),
            bf16(pairs, DEEP, 2 * rows, PAIR),
            f32(pairs, WIDE, rows, PAIR),
        ),
        in_specs=[HBM] * 8,
        out_specs=[VMEM] * 4,
        scratch_shapes=[
            *[pltpu.VMEM(t.shape, t.dtype) for t in ins],
            pltpu.VMEM((pairs, SEND, PAIR), F32),
            pltpu.VMEM((ROW, SEND, PAIR), F32),
            pltpu.VMEM((ROW // 2, SEND, PAIR), F32),
            pltpu.VMEM((SEND, PAIR), F32),
            pltpu.VMEM((ROWS, SEND, PAIR), F32),
            pltpu.VMEM((ROW, BACK, PAIR), F32),
            pltpu.VMEM((2, HEAD, PAIR), F32),
            pltpu.VMEM((pairs, BACK, PAIR), F32),
            pltpu.VMEM((pairs, 8, PAIR), F32),
            pltpu.VMEM((ROW, 8, PAIR), F32),
            pltpu.VMEM((2 * ROWS, 8, PAIR), F32),
            pltpu.VMEM((pairs, 8, PAIR), F32),
            *[dma(n) for n in (8, 2, ROW, ROWS, ROWS, ROW, 2)],
            *[dma(n) for n in (2, ROW, 2 * ROWS, 2 * ROWS, ROW, 2)],
        ],
        compiler_params=pltpu.CompilerParams(
            collective_id=0, has_side_effects=True, vmem_limit_bytes=48 * 1024 * 1024
        ),
    )(*[pltpu.with_memory_space_constraint(t, pltpu.HBM) for t in ins])
    *grads, bonus = pl.pallas_call(
        final_kernel,
        out_shape=(*[bf16(rows, width)] * 6, f32(1, width)),
        in_specs=[VMEM] * 10,
        out_specs=[VMEM] * 7,
        compiler_params=pltpu.CompilerParams(vmem_limit_bytes=40 * 1024 * 1024),
    )(*[ins[i] for i in (0, 1, 2, 4, 5, 7)], *kept)
    return (*[t.reshape(1, rows, width) for t in grads], bonus.reshape(width))


def solution(mesh):
    block = P("dp", "ctx", "tp")
    return jax.shard_map(
        local,
        mesh=mesh,
        in_specs=(block,) * 6 + (P("tp"), block),
        out_specs=(block,) * 6 + (P("tp"),),
        check_vma=False,
    )
```

```python
import functools

import jax
import jax.numpy as jnp
from jax import lax
from jax.experimental import pallas as pl
from jax.experimental.pallas import tpu as pltpu
from jax.sharding import PartitionSpec as P

HEAD = 64
PAIR = 128
F32 = jnp.float32
BF16 = jnp.bfloat16
MESH = pl.DeviceIdType.MESH
NN = (((1,), (0,)), ((), ()))
NT = (((1,), (1,)), ((), ()))


def split(x):
    high = x.astype(BF16)
    low = (x - high.astype(F32)).astype(BF16)
    return high, low


def mm(x, y, dims=NN):
    return lax.dot_general(x, y, dims, preferred_element_type=F32)


def cat(parts, axis):
    return jnp.concatenate(parts, axis=axis)


def dot3(x, y, dims=NN):
    xh, xl = split(x) if not isinstance(x, tuple) else x
    yh, yl = split(y) if not isinstance(y, tuple) else y
    axis = 0 if dims is NN else 1
    if yh.shape == (PAIR, PAIR):
        wide = cat([cat([yh, yl], 1 - axis)] * 2, axis)
        both = mm(cat([xh, xl], 1), wide, dims)
        return both[:, :PAIR] + both[:, PAIR:]
    return mm(cat([xh, xl], 1), cat([yh, yh], axis), dims) + mm(xh, yl, dims)


def dot2(x, y, dims=NN):
    xh, xl = split(x) if not isinstance(x, tuple) else x
    axis = 0 if dims is NN else 1
    return mm(cat([xh, xl], 1), cat([y, y], axis), dims)


def iotas(rows, cols):
    return (
        lax.broadcasted_iota(jnp.int32, (rows, cols), 0),
        lax.broadcasted_iota(jnp.int32, (rows, cols), 1),
    )


def first_half(shape):
    return (lax.broadcasted_iota(jnp.int32, shape, 1) & (PAIR - 1)) < HEAD


def by_head(stacked):
    half = stacked.shape[0] // 2
    top, bottom = stacked[:half], stacked[half:]
    return jnp.where(first_half(top.shape), top, bottom)


def own_lanes(x):
    mine = first_half(x.shape)
    return jnp.where(mine, x, 0.0), jnp.where(mine, 0.0, x)


def compact(blocks):
    return by_head(blocks)


def spread(x):
    return cat(list(own_lanes(x)), 0)


def turned_lanes(x):
    return pltpu.roll(x, HEAD, 1)


def gram_parts(x):
    high = x.astype(BF16).astype(F32)
    low = x - high
    high_t, low_t = turned_lanes(high), turned_lanes(low)
    mine = first_half(x.shape)
    pick = lambda a, b: jnp.where(mine, a, b).astype(BF16)
    return (
        (pick(high, low_t), pick(high, high_t), pick(low, low_t)),
        (pick(high_t, low), pick(high_t, high), pick(low_t, low)),
    )


def gram(lefts, rights):
    out = []
    for h in (0, 1):
        left = cat([x[h][0] for x in lefts], 0)
        right = [cat([x[h][i] for x in rights], 0) for i in (1, 2)]
        out.append(mm(cat([left, left], 1), cat(right, 1), NT))
    return out


def flip(x):
    return jnp.swapaxes(x, 0, 1)


def prepare(r, k, w, kappa, eta):
    n = w.shape[0]
    row, col = iotas(n, n)
    tri = jnp.where(row >= col, 1.0, 0.0).astype(BF16)
    wh = w.astype(BF16)
    rest = w - wh.astype(F32)
    wm = rest.astype(BF16)
    wl = (rest - wm.astype(F32)).astype(BF16)
    c = mm(cat([tri, tri], 1), cat([wh, wm], 0)) + mm(tri, wl)
    mid = c[n // 2 : n // 2 + 1]
    end = c[n - 1 : n]
    grow = jnp.exp(c - mid)
    fall = jnp.exp(mid - c)
    fall_before = jnp.exp(mid - (c - w))
    beta = kappa * eta
    out = dict(
        end=end,
        grow=grow,
        fall=fall,
        fall_before=fall_before,
        to_start=jnp.exp(-mid),
        to_end=jnp.exp(mid - end),
        beta=beta,
        rs=r * fall,
        ks=k * grow,
        bs=beta * grow,
        asc=-kappa * fall_before,
    )
    out["a0"] = out["asc"] * out["to_start"]
    out["r0"] = out["rs"] * out["to_start"]
    out["bf"] = out["bs"] * out["to_end"]
    out["kf"] = out["ks"] * out["to_end"]
    return out


def inverse(lows):
    n = lows[0].shape[0]
    row, col = iotas(n, n)
    eye = jnp.where(row == col, 1.0, 0.0)
    start = (row >> 4) == (col >> 4)
    d1 = [jnp.where(start, low, 0.0) for low in lows]
    s1 = [split(d) for d in d1]
    d2 = [dot3(s, s) for s in s1]
    s2 = [split(d) for d in d2]
    d4 = [dot3(s, s) for s in s2]
    p4 = [eye + a + b + dot3(s, t) for a, b, s, t in zip(d1, d2, s1, s2)]
    s4 = [split(d) for d in d4]
    d8 = [dot3(s, s) for s in s4]
    p8 = [p + dot3(p, s) for p, s in zip(p4, s4)]
    t = [split(p + dot3(p, d)) for p, d in zip(p8, d8)]
    rest = [jnp.where(start, 0.0, low) for low in lows]
    x1 = [split(dot3(s, r)) for s, r in zip(t, rest)]
    x2 = [split(dot3(s, s)) for s in x1]
    y1 = [a[0].astype(F32) + a[1].astype(F32) + dot3(s, a) for s, a in zip(x1, t)]
    x4 = [split(dot3(s, s)) for s in x2]
    y2 = [y + dot3(s, y) for s, y in zip(x2, y1)]
    return [y + dot3(s, y) for s, y in zip(x4, y2)]


def local_grams(r, k, v, w, kappa, eta, dy, bonus):
    n = w.shape[0]
    q = prepare(r, k, w, kappa, eta)
    q.update(r=r, k=k, v=v, dy=dy, bonus=bonus, vb=v.astype(BF16), dyb=dy.astype(BF16))
    row, col = iotas(n, n)
    pa, pr, pb, pk = [gram_parts(q[name]) for name in ("asc", "rs", "bs", "ks")]
    lower = gram([pa], [pb, pk])
    upper = gram([pb], [pr])
    q["late"] = pk, pr, pa
    q["lw"] = [jnp.where(row > col, t[:, :n], 0.0) for t in lower]
    q["lk"] = cat([jnp.where(row > col, t[:, n:], 0.0) for t in lower], 0)
    q["wwt"] = cat([jnp.where(col >= row, t, 0.0) for t in upper], 0)
    q["z"] = by_head(dot2(q["lk"], q["vb"]))
    q["zd"] = by_head(dot2(q["wwt"], q["dyb"]))
    return q


def local_message(q, t):
    n = q["z"].shape[0]
    eu = by_head(dot3(cat(t, 0), cat([q["a0"], q["z"]], 1)))
    fp = by_head(dot3(cat([flip(x) for x in t], 0), cat([q["bf"], q["zd"]], 1)))
    ml = dot3(flip(q["bf"]), eu)
    row, col = iotas(HEAD, PAIR)
    decay = jnp.where(row == (col & (HEAD - 1)), jnp.exp(-q["end"]), 0.0)
    mt = decay + compact(ml[:, :n])
    lt = compact(ml[:, n:] + dot2(flip(q["kf"]), q["vb"]))
    ht = compact(flip(dot3(flip(q["a0"]), fp[:, n:]) + dot2(flip(q["r0"]), q["dyb"])))
    q.update(eu=eu, fp=fp)
    return lt, mt, ht


def bonus_terms(q):
    row, col = iotas(PAIR, PAIR)
    ones = jnp.where((row >> 6) == (col >> 6), 1.0, 0.0).astype(BF16)
    dyv = dot2(q["dy"] * q["v"], ones)
    q.update(ones=ones, dyv=dyv)
    return jnp.sum(dyv * q["r"] * q["k"], axis=0, keepdims=True)


def exact_parts(x):
    other = turned_lanes(x)
    mine = first_half(x.shape)
    pick = lambda a, b: jnp.where(mine, a, b).astype(BF16)
    return pick(x, 0.0), pick(x, other), pick(other, 0.0), pick(other, x)


def local_rest(q):
    n = q["z"].shape[0]
    eu, fp = q["eu"], q["fp"]
    pk, pr, pa = q["late"]
    upper = gram([pk], [pr, pa])
    row, col = iotas(n, n)
    wkt = cat([jnp.where(col >= row, t[:, :n], 0.0) for t in upper], 0)
    lkt = cat([jnp.where(col > row, t[:, n:], 0.0) for t in upper], 0)
    more = by_head(dot3(lkt, fp))
    kg = q["kf"] + more[:, :n]
    dv = more[:, n:] + by_head(dot2(wkt, q["dyb"]))
    dv = dv + dot2(q["r"] * q["k"] * q["bonus"], q["ones"]) * q["dy"]
    narrow = [*split(eu[:, :n]), *split(fp[:, :n]), *split(kg)]
    narrow += [*exact_parts(q["v"]), *exact_parts(q["dy"])]
    deep = [*split(cat([q["bs"], q["ks"]], 0)), *split(cat([q["rs"], q["asc"]], 0))]
    wide = [eu[:, n:], fp[:, n:], dv, q["dyv"], q["fall"], q["fall_before"], q["grow"]]
    lines = [q["bonus"], q["to_start"], q["to_end"], jnp.exp(-q["end"])]
    return narrow, deep, wide, lines


def final_part(r, k, v, kappa, eta, dy, narrow, deep, wide, lines, st, g):
    n = r.shape[0]
    eh, el, fh, fl, kgh, kgl, *exact = narrow
    by, ry = deep[:2], deep[2:]
    u_own, p_own, dv_own, dyv, fall, fall_before, grow = wide
    bonus, to_start, to_end, decay = lines
    vb, dyb = v.astype(BF16), dy.astype(BF16)
    sb = split(spread(st))
    gb = split(spread(g))
    u = u_own + dot3((eh, el), sb)
    p = p_own + dot3((fh, fl), gb, NT)
    dv = dv_own + dot3((kgh, kgl), gb, NT)
    zero = jnp.zeros((n, PAIR), BF16)
    gv = ((exact[0], exact[1], zero), (exact[2], exact[3], zero))
    gy = ((exact[4], exact[5], zero), (exact[6], exact[7], zero))
    gu, gp = gram_parts(u), gram_parts(p)
    row, col = iotas(2 * n, 2 * n)
    t, s = row & (n - 1), col & (n - 1)
    fwd_mask = t >= s + jnp.where(row >= n, 1, 0)
    bwd_mask = s >= t + jnp.where(col >= n, 1, 0)
    fwd = cat([jnp.where(fwd_mask, m, 0.0) for m in gram([gy, gp], [gu, gv])], 0)
    bwd = cat([jnp.where(bwd_mask, m, 0.0) for m in gram([gu, gv], [gy, gp])], 0)

    def apply(mat, y):
        mh, ml = split(mat)
        both = mm(mh, cat(y, 1))
        return by_head(both[:, :PAIR] + both[:, PAIR:] + mm(ml, y[0]))

    ra = apply(fwd, by)
    bk = apply(bwd, ry)
    uh, ul = split(u)
    ph, pl_ = split(p)
    start = dot3((cat([dyb, ph], 0), cat([zero, pl_], 0)), sb, NT)
    behind = dot3((cat([uh, vb], 0), cat([ul, zero], 0)), gb)
    dr = (ra[:n] + start[:n] * to_start) * fall
    da = (ra[n:] + start[n:] * to_start) * fall_before
    reach = grow * to_end
    final_u = behind[:n] * reach
    final_v = behind[n:] * reach
    db = bk[:n] * grow + final_u
    dk = bk[n:] * grow + final_v
    beta = kappa * eta
    inner = beta * final_u + k * final_v
    through = r * dr - k * dk - beta * db
    behind_a = -kappa * da
    row, col = iotas(n, n)
    from_here = jnp.where(col >= row, 1.0, 0.0).astype(BF16)
    after = jnp.where(col > row, 1.0, 0.0).astype(BF16)
    tail = mm(cat([from_here, from_here], 1), cat(split(through), 0)) + mm(
        cat([after, after], 1), cat(split(behind_a), 0)
    )
    turned = compact(flip(spread(st)))
    anchor = jnp.sum(turned * g, axis=0, keepdims=True) * decay + jnp.sum(
        inner, axis=0, keepdims=True
    )
    return (
        dr + bonus * k * dyv,
        dk + bonus * r * dyv,
        dv,
        -(tail + anchor),
        eta * db - da,
        kappa * db,
    )


def read_tokens(refs, p):
    lanes = slice(PAIR * p, PAIR * p + PAIR)
    return [ref[:, lanes].astype(F32) for ref in refs]


def final_kernel(*refs):
    ins, (state, narrow, deep, wide), outs = refs[:6], refs[6:10], refs[10:]
    got = [
        final_part(
            *read_tokens(ins, p),
            [narrow[p, i] for i in range(NARROW)],
            [deep[p, i] for i in range(DEEP)],
            [wide[p, i] for i in range(WIDE)],
            [state[p, BACK + 8 + i : BACK + 9 + i] for i in range(LINES)],
            state[p, 0:64],
            state[p, 64:128],
        )
        for p in (0, 1)
    ]
    for p in (0, 1):
        lanes = slice(PAIR * p, PAIR * p + PAIR)
        for ref, value in zip(outs, got[p]):
            ref[:, lanes] = value.astype(ref.dtype)
        outs[6][:, lanes] = state[p, BACK : BACK + 1]


ROW = 8
ROWS = 4
SEND = 192
BACK = 128
NARROW, DEEP, WIDE, LINES = 14, 4, 7, 4


def owner_of(p, d):
    return 4 * p + 2 * d


def adder_of(p, d):
    return owner_of(p, d) + 1


def joined(a, b):
    both = dot3(cat([b[1], b[2]], 0), cat([spread(a[1]), spread(a[0])], 1))
    return both[:HEAD, PAIR:] + b[0], both[:HEAD, :PAIR], both[HEAD:, :PAIR] + a[2]


def joined_states(a, b):
    both = dot3(b[1], cat([spread(a[1]), spread(a[0])], 1))
    return both[:, PAIR:] + b[0], both[:, :PAIR], None


def joined_adjoints(a, b):
    both = dot3(cat([b[1], b[2]], 0), spread(a[1]))
    return None, both[:HEAD], both[HEAD:] + a[2]


def copy_to(src, dst, ssem, rsem, where):
    return pltpu.make_async_remote_copy(
        src_ref=src,
        dst_ref=dst,
        send_sem=ssem,
        recv_sem=rsem,
        device_id=where,
        device_id_type=MESH,
    )


def front_kernel(*refs):
    (ins, outs, staged, scratch, sems) = refs[:8], refs[8:12], refs[12:20], refs[20:32], refs[32:]
    state, narrow, deep, wide = outs
    msg, recv, two, tot, xin, back, run, land, term, terms, sums, total = scratch
    in_sem, send_sem, recv_sem, xsend, xsem, osend, osem = sems[:7]
    tsend, tsem, ssend, ssem, gsend, gsem = sems[7:]
    d = lax.axis_index("dp")
    ctx = lax.axis_index("ctx")
    x = ctx // ROW
    z = ctx % ROW
    mine = [z == owner_of(p, d) for p in (0, 1)]
    is_owner = jnp.logical_or(*mine)
    pown = jnp.where(mine[1], 1, 0)
    adds = [z == adder_of(p, d) for p in (0, 1)]
    is_adder = jnp.logical_or(*adds)
    padd = jnp.where(adds[1], 1, 0)

    def at(xx, zz, dd=None):
        place = {"ctx": xx * ROW + zz}
        if dd is not None:
            place["dp"] = dd
        return place

    loads = [
        pltpu.make_async_copy(src, dst, in_sem.at[i])
        for i, (src, dst) in enumerate(zip(ins, staged))
    ]
    for load in loads:
        load.start()

    barrier = pltpu.get_barrier_semaphore()

    def greet(where):
        pl.semaphore_signal(barrier, inc=1, device_id=where, device_id_type=MESH)

    for p in (0, 1):
        for place in (owner_of(p, d), adder_of(p, d)):
            pl.when(z != place)(lambda place=place: greet(at(x, place)))

    @pl.when(is_owner | is_adder)
    def _():
        for j in (2, 3, 6, 7):
            greet(at(x, (2 * d + j) % ROW))

    @pl.when(is_owner)
    def _():
        for j in range(1, ROWS):
            greet(at((x + j) % ROWS, z))

    @pl.when(is_adder)
    def _():
        for j in range(1, ROWS):
            greet(at((x + j) % ROWS, z))
        for j in range(ROWS):
            greet(at((x + j) % ROWS, adder_of(padd, 1 - d), 1 - d))

    for load in loads:
        load.wait()
    parts = []
    for p in (0, 1):
        tokens = read_tokens(staged[:6] + staged[7:], p)
        parts.append(local_grams(*tokens, staged[6][:, PAIR * p : PAIR * p + PAIR]))
    solved = inverse(parts[0]["lw"] + parts[1]["lw"])

    def to_owner(p):
        place = jnp.where(is_owner, (z + 1) % ROW, owner_of(p, d))
        return copy_to(msg.at[p], recv.at[z], send_sem.at[p], recv_sem.at[z], at(x, place))

    pmate = 1 - padd

    def from_mate(p, slot, i, place):
        return copy_to(tot, two.at[i], send_sem.at[p], recv_sem.at[slot], place)

    messages = [local_message(parts[p], solved[2 * p : 2 * p + 2]) for p in (0, 1)]
    for p, (low, mid, high) in enumerate(messages):
        msg[p, 0:64] = low
        msg[p, 64:128] = mid
        msg[p, 128:192] = high
    pl.when(is_owner)(lambda: pl.semaphore_wait(barrier, ROW - 1 + ROWS - 1))
    pl.when(is_adder)(lambda: pl.semaphore_wait(barrier, ROW - 1 + 2 * ROWS - 1))
    pl.when(jnp.logical_not(is_owner | is_adder))(lambda: pl.semaphore_wait(barrier, 4))
    for p in (0, 1):
        direct = jnp.logical_not(mine[p] | adds[1 - p])
        pl.when(direct)(lambda p=p: to_owner(p).start())

    for p in (0, 1):
        term[p] = jnp.broadcast_to(bonus_terms(parts[p]), (8, PAIR))

    def over_mate(place):
        rows = pl.ds(64, 128)
        return copy_to(
            msg.at[pmate, rows], xin.at[x, rows], xsend.at[0], xsem.at[x], at(x, place)
        )

    @pl.when(is_adder)
    def _():
        far = (z + ROW - 1) % ROW
        over_mate(far).start()
        copy_to(
            msg.at[0], recv.at[far], send_sem.at[0], recv_sem.at[far], at(x, far)
        ).wait_recv()
        got = joined(
            (recv[far, 0:64], recv[far, 64:128], recv[far, 128:192]),
            (msg[pmate, 0:64], msg[pmate, 64:128], msg[pmate, 128:192]),
        )
        tot[0:64] = got[0]
        tot[64:128] = got[1]
        tot[128:192] = got[2]
        from_mate(pmate, z, z // 2, at(x, owner_of(pmate, d))).start()

    def to_adder(p):
        return copy_to(
            term.at[p], terms.at[z], tsend.at[p], tsem.at[z], at(x, adder_of(p, d))
        )

    for p in (0, 1):
        pl.when(jnp.logical_not(adds[p]))(lambda p=p: to_adder(p).start())

    for p in (0, 1):
        got = local_rest(parts[p])
        for ref, values in zip((narrow, deep, wide), got):
            for i, value in enumerate(values):
                ref[p, i] = value
        for i, line in enumerate(got[3]):
            state[p, BACK + 8 + i : BACK + 9 + i] = line

    @pl.when(is_adder)
    def _():
        terms[z] = term[padd]
        for j in range(1, ROW):
            zz = (z + j) % ROW
            copy_to(term.at[0], terms.at[zz], tsend.at[0], tsem.at[zz], at(x, zz)).wait_recv()
        part = terms[0]
        for i in range(1, ROW):
            part = part + terms[i]
        me = d * ROWS + x
        sums[me] = part
        places = [((x + j) % ROWS, d) for j in range(1, ROWS)]
        places += [((x + j) % ROWS, 1 - d) for j in range(ROWS)]
        across = [
            copy_to(
                sums.at[me], sums.at[me], ssend.at[i], ssem.at[me], at(xx, adder_of(padd, dd), dd)
            )
            for i, (xx, dd) in enumerate(places)
        ]
        for copy in across:
            copy.start()
        for xx, dd in places:
            slot = dd * ROWS + xx
            copy_to(
                sums.at[slot], sums.at[slot], ssend.at[0], ssem.at[slot], at(xx, z)
            ).wait_recv()
        part = sums[0]
        for i in range(1, 2 * ROWS):
            part = part + sums[i]
        total[padd] = part
        gives = [
            copy_to(total.at[padd], total.at[padd], gsend.at[j], gsem.at[padd], at(x, (z + j) % ROW))
            for j in range(1, ROW)
        ]
        for give in gives:
            give.start()
        for copy in across + gives:
            copy.wait_send()

    @pl.when(is_owner)
    def _():
        recv[z] = msg[pown]
        far = (z + ROW // 2) % ROW
        for zz in (far, far + 1):
            recv[zz] = jnp.zeros((SEND, PAIR), F32)
        places = [(z // 2 + j) % (ROW // 2) for j in (0, 1, 3)]
        for j, i in zip((0, 1, 3), places):
            for zz in (2 * i + 1,) if j == 0 else (2 * i, 2 * i + 1):
                copy_to(
                    msg.at[0], recv.at[zz], send_sem.at[0], recv_sem.at[zz], at(x, zz)
                ).wait_recv()
        blocks = [
            [(recv[zz, 0:64], recv[zz, 64:128], recv[zz, 128:192]) for zz in (2 * i, 2 * i + 1)]
            for i in places
        ]
        for i, got in zip(places, [joined(*both) for both in blocks]):
            two[i, 0:64] = got[0]
            two[i, 64:128] = got[1]
            two[i, 128:192] = got[2]
        from_mate(0, far + 1, far // 2, at(x, far + 1)).wait_recv()
        pair = [(two[i, 0:64], two[i, 64:128], two[i, 128:192]) for i in range(ROW // 2)]
        four = [joined(pair[0], pair[1]), joined(pair[2], pair[3])]
        whole = joined(four[0], four[1])
        tot[0:64] = whole[0]
        tot[64:128] = whole[1]
        tot[128:192] = whole[2]
        cases = (
            (lambda xx: (xx > x) & (x == 0), 0, 64),
            (lambda xx: (xx > x) & (x != 0), 0, 128),
            (lambda xx: (xx < x) & (x == ROWS - 1), 128, 192),
            (lambda xx: (xx < x) & (x != ROWS - 1), 64, 192),
        )

        def across(xx, low, high, landing):
            rows = pl.ds(low, high - low)
            return copy_to(
                tot.at[rows], xin.at[landing, rows], xsend.at[xx], xsem.at[landing], at(xx, z)
            )

        for xx in range(ROWS):
            for when, low, high in cases:
                pl.when(when(xx))(
                    lambda xx=xx, low=low, high=high: across(xx, low, high, x).start()
                )
        one = [(recv[i, 0:64], recv[i, 64:128], recv[i, 128:192]) for i in range(ROW)]
        before = [None, one[0], pair[0], None, four[0], None, None, None]
        before[3] = joined_states(pair[0], one[2])
        before[5] = joined_states(four[0], one[4])
        before[6] = joined_states(four[0], pair[2])
        before[7] = joined_states(before[6], one[6])
        behind = [None, None, None, four[1], None, pair[3], one[7], None]
        behind[4] = joined_adjoints(one[5], pair[3])
        behind[2] = joined_adjoints(one[3], four[1])
        behind[1] = joined_adjoints(pair[1], four[1])
        behind[0] = joined_adjoints(one[1], behind[1])

        run[...] = jnp.zeros_like(run)
        for xx in range(ROWS - 1):
            high = 64 if xx == 0 else 128

            @pl.when(x > xx)
            def _(xx=xx, high=high):
                across(xx, 0, high, xx).wait_recv()
                if xx == 0:
                    run[0] = xin[0, 0:64]
                else:
                    run[0] = dot3(xin[xx, 64:128], spread(run[0])) + xin[xx, 0:64]

        for xx in range(ROWS - 1, 0, -1):
            low = 128 if xx == ROWS - 1 else 64

            @pl.when(x < xx)
            def _(xx=xx, low=low):
                across(xx, low, 192, xx).wait_recv()
                if xx == ROWS - 1:
                    run[1] = xin[xx, 128:192]
                else:
                    run[1] = dot3(run[1], spread(xin[xx, 64:128])) + xin[xx, 128:192]

        sg, gg = run[0], run[1]
        moved = dot3(cat([before[i][1] for i in range(1, ROW)], 0), spread(sg))
        for i in range(ROW):
            back[i, 0:64] = sg if i == 0 else moved[64 * i - 64 : 64 * i] + before[i][0]
        gs = split(gg)
        for i in range(0, ROW, 2):
            if i + 1 < ROW - 1:
                got = dot3(gs, cat([spread(behind[i][1]), spread(behind[i + 1][1])], 1))
                back[i, 64:128] = got[:, :PAIR] + behind[i][2]
                back[i + 1, 64:128] = got[:, PAIR:] + behind[i + 1][2]
            else:
                back[i, 64:128] = dot3(gs, spread(behind[i][1])) + behind[i][2]
                back[i + 1, 64:128] = gg

        back[far + 1, 0:64] = back[far, 0:64]
        gives = []
        for j in (4, 5, 3, 2, 6, 1, 7):
            zz = (z + j) % ROW
            source = back.at[far + 1] if j == 4 else back.at[zz]
            gives.append(
                copy_to(source, land.at[pown], osend.at[j], osem.at[pown], at(x, zz))
            )
            gives[-1].start()
        land[pown] = back[z]
        for give in gives:
            give.wait_send()
        for xx in range(ROWS):
            for when, low, high in cases:
                pl.when(when(xx))(
                    lambda xx=xx, low=low, high=high: across(xx, low, high, x).wait_send()
                )

    for p in (0, 1):

        @pl.when(jnp.logical_not(mine[p]))
        def _(p=p):
            to_owner(p).wait_send()
            copy_to(
                back.at[0], land.at[p], osend.at[0], osem.at[p], at(x, owner_of(p, d))
            ).wait_recv()

        @pl.when(adds[1 - p])
        def _(p=p):
            far = (z + ROW - 1) % ROW
            land[p, 0:64] = dot3(recv[far, 64:128], spread(land[p, 0:64])) + recv[far, 0:64]

        @pl.when(mine[1 - p])
        def _(p=p):
            over_mate(z).wait_recv()
            over = dot3(land[p, 64:128], spread(xin[x, 64:128]))
            land[p, 64:128] = over + xin[x, 128:192]

    for p in (0, 1):

        @pl.when(jnp.logical_not(adds[p]))
        def _(p=p):
            to_adder(p).wait_send()
            copy_to(
                total.at[p], total.at[p], gsend.at[0], gsem.at[p], at(x, adder_of(p, d))
            ).wait_recv()

    @pl.when(is_adder)
    def _():
        over_mate(z).wait_send()

    for p in (0, 1):
        state[p, 0:BACK] = land[p]
        state[p, BACK : BACK + 8] = total[p]


VMEM = pl.BlockSpec(memory_space=pltpu.VMEM)
HBM = pl.BlockSpec(memory_space=pltpu.HBM)


def local(r, k, v, w, kappa, eta, extra, dy):
    rows, width = r.shape[1], r.shape[2]
    pairs = width // PAIR
    flat = [t.reshape(rows, width) for t in (r, k, v, w, kappa, eta)]
    ins = (*flat, extra.reshape(1, width), dy.reshape(rows, width))
    f32 = lambda *shape: jax.ShapeDtypeStruct(shape, F32)
    dma = lambda n: pltpu.SemaphoreType.DMA((n,))
    bf16 = lambda *shape: jax.ShapeDtypeStruct(shape, BF16)
    kept = pl.pallas_call(
        front_kernel,
        out_shape=(
            f32(pairs, BACK + 16, PAIR),
            bf16(pairs, NARROW, rows, PAIR),
            bf16(pairs, DEEP, 2 * rows, PAIR),
            f32(pairs, WIDE, rows, PAIR),
        ),
        in_specs=[HBM] * 8,
        out_specs=[VMEM] * 4,
        scratch_shapes=[
            *[pltpu.VMEM(t.shape, t.dtype) for t in ins],
            pltpu.VMEM((pairs, SEND, PAIR), F32),
            pltpu.VMEM((ROW, SEND, PAIR), F32),
            pltpu.VMEM((ROW // 2, SEND, PAIR), F32),
            pltpu.VMEM((SEND, PAIR), F32),
            pltpu.VMEM((ROWS, SEND, PAIR), F32),
            pltpu.VMEM((ROW, BACK, PAIR), F32),
            pltpu.VMEM((2, HEAD, PAIR), F32),
            pltpu.VMEM((pairs, BACK, PAIR), F32),
            pltpu.VMEM((pairs, 8, PAIR), F32),
            pltpu.VMEM((ROW, 8, PAIR), F32),
            pltpu.VMEM((2 * ROWS, 8, PAIR), F32),
            pltpu.VMEM((pairs, 8, PAIR), F32),
            *[dma(n) for n in (8, 2, ROW, ROWS, ROWS, ROW, 2)],
            *[dma(n) for n in (2, ROW, 2 * ROWS, 2 * ROWS, ROW, 2)],
        ],
        compiler_params=pltpu.CompilerParams(
            collective_id=0, has_side_effects=True, vmem_limit_bytes=48 * 1024 * 1024
        ),
    )(*[pltpu.with_memory_space_constraint(t, pltpu.HBM) for t in ins])
    *grads, bonus = pl.pallas_call(
        final_kernel,
        out_shape=(*[bf16(rows, width)] * 6, f32(1, width)),
        in_specs=[VMEM] * 10,
        out_specs=[VMEM] * 7,
        compiler_params=pltpu.CompilerParams(vmem_limit_bytes=40 * 1024 * 1024),
    )(*[ins[i] for i in (0, 1, 2, 4, 5, 7)], *kept)
    return (*[t.reshape(1, rows, width) for t in grads], bonus.reshape(width))


def solution(mesh):
    block = P("dp", "ctx", "tp")
    return jax.shard_map(
        local,
        mesh=mesh,
        in_specs=(block,) * 6 + (P("tp"), block),
        out_specs=(block,) * 6 + (P("tp"),),
        check_vma=False,
    )
```

```python
import functools

import jax
import jax.numpy as jnp
from jax import lax
from jax.experimental import pallas as pl
from jax.experimental.pallas import tpu as pltpu
from jax.sharding import PartitionSpec as P

HEAD = 64
PAIR = 128
F32 = jnp.float32
BF16 = jnp.bfloat16
MESH = pl.DeviceIdType.MESH
NN = (((1,), (0,)), ((), ()))
NT = (((1,), (1,)), ((), ()))


def split(x):
    high = x.astype(BF16)
    low = (x - high.astype(F32)).astype(BF16)
    return high, low


def mm(x, y, dims=NN):
    return lax.dot_general(x, y, dims, preferred_element_type=F32)


def cat(parts, axis):
    return jnp.concatenate(parts, axis=axis)


def dot3(x, y, dims=NN):
    xh, xl = split(x) if not isinstance(x, tuple) else x
    yh, yl = split(y) if not isinstance(y, tuple) else y
    axis = 0 if dims is NN else 1
    if yh.shape == (PAIR, PAIR):
        wide = cat([cat([yh, yl], 1 - axis)] * 2, axis)
        both = mm(cat([xh, xl], 1), wide, dims)
        return both[:, :PAIR] + both[:, PAIR:]
    return mm(cat([xh, xl], 1), cat([yh, yh], axis), dims) + mm(xh, yl, dims)


def dot2(x, y, dims=NN):
    xh, xl = split(x) if not isinstance(x, tuple) else x
    axis = 0 if dims is NN else 1
    return mm(cat([xh, xl], 1), cat([y, y], axis), dims)


def iotas(rows, cols):
    return (
        lax.broadcasted_iota(jnp.int32, (rows, cols), 0),
        lax.broadcasted_iota(jnp.int32, (rows, cols), 1),
    )


def first_half(shape):
    return (lax.broadcasted_iota(jnp.int32, shape, 1) & (PAIR - 1)) < HEAD


def by_head(stacked):
    half = stacked.shape[0] // 2
    top, bottom = stacked[:half], stacked[half:]
    return jnp.where(first_half(top.shape), top, bottom)


def own_lanes(x):
    mine = first_half(x.shape)
    return jnp.where(mine, x, 0.0), jnp.where(mine, 0.0, x)


def compact(blocks):
    return by_head(blocks)


def spread(x):
    return cat(list(own_lanes(x)), 0)


def turned_lanes(x):
    return pltpu.roll(x, HEAD, 1)


def gram_parts(x):
    high = x.astype(BF16).astype(F32)
    low = x - high
    high_t, low_t = turned_lanes(high), turned_lanes(low)
    mine = first_half(x.shape)
    pick = lambda a, b: jnp.where(mine, a, b).astype(BF16)
    return (
        (pick(high, low_t), pick(high, high_t), pick(low, low_t)),
        (pick(high_t, low), pick(high_t, high), pick(low_t, low)),
    )


def gram(lefts, rights):
    out = []
    for h in (0, 1):
        left = cat([x[h][0] for x in lefts], 0)
        right = [cat([x[h][i] for x in rights], 0) for i in (1, 2)]
        out.append(mm(cat([left, left], 1), cat(right, 1), NT))
    return out


def flip(x):
    return jnp.swapaxes(x, 0, 1)


def prepare(r, k, w, kappa, eta):
    n = w.shape[0]
    row, col = iotas(n, n)
    tri = jnp.where(row >= col, 1.0, 0.0).astype(BF16)
    wh = w.astype(BF16)
    rest = w - wh.astype(F32)
    wm = rest.astype(BF16)
    wl = (rest - wm.astype(F32)).astype(BF16)
    c = mm(cat([tri, tri], 1), cat([wh, wm], 0)) + mm(tri, wl)
    mid = c[n // 2 : n // 2 + 1]
    end = c[n - 1 : n]
    grow = jnp.exp(c - mid)
    fall = jnp.exp(mid - c)
    fall_before = jnp.exp(mid - (c - w))
    beta = kappa * eta
    out = dict(
        end=end,
        grow=grow,
        fall=fall,
        fall_before=fall_before,
        to_start=jnp.exp(-mid),
        to_end=jnp.exp(mid - end),
        beta=beta,
        rs=r * fall,
        ks=k * grow,
        bs=beta * grow,
        asc=-kappa * fall_before,
    )
    out["a0"] = out["asc"] * out["to_start"]
    out["r0"] = out["rs"] * out["to_start"]
    out["bf"] = out["bs"] * out["to_end"]
    out["kf"] = out["ks"] * out["to_end"]
    return out


def inverse(lows):
    n = lows[0].shape[0]
    row, col = iotas(n, n)
    eye = jnp.where(row == col, 1.0, 0.0)
    start = (row >> 4) == (col >> 4)
    d1 = [jnp.where(start, low, 0.0) for low in lows]
    s1 = [split(d) for d in d1]
    d2 = [dot3(s, s) for s in s1]
    s2 = [split(d) for d in d2]
    d4 = [dot3(s, s) for s in s2]
    p4 = [eye + a + b + dot3(s, t) for a, b, s, t in zip(d1, d2, s1, s2)]
    s4 = [split(d) for d in d4]
    d8 = [dot3(s, s) for s in s4]
    p8 = [p + dot3(p, s) for p, s in zip(p4, s4)]
    t = [split(p + dot3(p, d)) for p, d in zip(p8, d8)]
    rest = [jnp.where(start, 0.0, low) for low in lows]
    x1 = [split(dot3(s, r)) for s, r in zip(t, rest)]
    x2 = [split(dot3(s, s)) for s in x1]
    y1 = [a[0].astype(F32) + a[1].astype(F32) + dot3(s, a) for s, a in zip(x1, t)]
    x4 = [split(dot3(s, s)) for s in x2]
    y2 = [y + dot3(s, y) for s, y in zip(x2, y1)]
    return [y + dot3(s, y) for s, y in zip(x4, y2)]


def local_grams(r, k, v, w, kappa, eta, dy, bonus):
    n = w.shape[0]
    q = prepare(r, k, w, kappa, eta)
    q.update(r=r, k=k, v=v, dy=dy, bonus=bonus, vb=v.astype(BF16), dyb=dy.astype(BF16))
    row, col = iotas(n, n)
    pa, pr, pb, pk = [gram_parts(q[name]) for name in ("asc", "rs", "bs", "ks")]
    lower = gram([pa], [pb, pk])
    upper = gram([pb], [pr])
    q["late"] = pk, pr, pa
    q["lw"] = [jnp.where(row > col, t[:, :n], 0.0) for t in lower]
    q["lk"] = cat([jnp.where(row > col, t[:, n:], 0.0) for t in lower], 0)
    q["wwt"] = cat([jnp.where(col >= row, t, 0.0) for t in upper], 0)
    q["z"] = by_head(dot2(q["lk"], q["vb"]))
    q["zd"] = by_head(dot2(q["wwt"], q["dyb"]))
    return q


def local_message(q, t):
    n = q["z"].shape[0]
    eu = by_head(dot3(cat(t, 0), cat([q["a0"], q["z"]], 1)))
    fp = by_head(dot3(cat([flip(x) for x in t], 0), cat([q["bf"], q["zd"]], 1)))
    ml = dot3(flip(q["bf"]), eu)
    row, col = iotas(HEAD, PAIR)
    decay = jnp.where(row == (col & (HEAD - 1)), jnp.exp(-q["end"]), 0.0)
    mt = decay + compact(ml[:, :n])
    lt = compact(ml[:, n:] + dot2(flip(q["kf"]), q["vb"]))
    ht = compact(flip(dot3(flip(q["a0"]), fp[:, n:]) + dot2(flip(q["r0"]), q["dyb"])))
    q.update(eu=eu, fp=fp)
    return lt, mt, ht


def bonus_terms(q):
    row, col = iotas(PAIR, PAIR)
    ones = jnp.where((row >> 6) == (col >> 6), 1.0, 0.0).astype(BF16)
    dyv = dot2(q["dy"] * q["v"], ones)
    q.update(ones=ones, dyv=dyv)
    return jnp.sum(dyv * q["r"] * q["k"], axis=0, keepdims=True)


def exact_parts(x):
    other = turned_lanes(x)
    mine = first_half(x.shape)
    pick = lambda a, b: jnp.where(mine, a, b).astype(BF16)
    return pick(x, 0.0), pick(x, other), pick(other, 0.0), pick(other, x)


def local_rest(q):
    n = q["z"].shape[0]
    eu, fp = q["eu"], q["fp"]
    pk, pr, pa = q["late"]
    upper = gram([pk], [pr, pa])
    row, col = iotas(n, n)
    wkt = cat([jnp.where(col >= row, t[:, :n], 0.0) for t in upper], 0)
    lkt = cat([jnp.where(col > row, t[:, n:], 0.0) for t in upper], 0)
    more = by_head(dot3(lkt, fp))
    kg = q["kf"] + more[:, :n]
    dv = more[:, n:] + by_head(dot2(wkt, q["dyb"]))
    dv = dv + dot2(q["r"] * q["k"] * q["bonus"], q["ones"]) * q["dy"]
    narrow = [*split(eu[:, :n]), *split(fp[:, :n]), *split(kg)]
    narrow += [*exact_parts(q["v"]), *exact_parts(q["dy"])]
    deep = [*split(cat([q["bs"], q["ks"]], 0)), *split(cat([q["rs"], q["asc"]], 0))]
    wide = [eu[:, n:], fp[:, n:], dv, q["dyv"], q["fall"], q["fall_before"], q["grow"]]
    lines = [q["bonus"], q["to_start"], q["to_end"], jnp.exp(-q["end"])]
    return narrow, deep, wide, lines


def final_part(r, k, v, kappa, eta, dy, narrow, deep, wide, lines, st, g):
    n = r.shape[0]
    eh, el, fh, fl, kgh, kgl, *exact = narrow
    by, ry = deep[:2], deep[2:]
    u_own, p_own, dv_own, dyv, fall, fall_before, grow = wide
    bonus, to_start, to_end, decay = lines
    vb, dyb = v.astype(BF16), dy.astype(BF16)
    sb = split(spread(st))
    gb = split(spread(g))
    u = u_own + dot3((eh, el), sb)
    p = p_own + dot3((fh, fl), gb, NT)
    dv = dv_own + dot3((kgh, kgl), gb, NT)
    zero = jnp.zeros((n, PAIR), BF16)
    gv = ((exact[0], exact[1], zero), (exact[2], exact[3], zero))
    gy = ((exact[4], exact[5], zero), (exact[6], exact[7], zero))
    gu, gp = gram_parts(u), gram_parts(p)
    row, col = iotas(2 * n, 2 * n)
    t, s = row & (n - 1), col & (n - 1)
    fwd_mask = t >= s + jnp.where(row >= n, 1, 0)
    bwd_mask = s >= t + jnp.where(col >= n, 1, 0)
    fwd = cat([jnp.where(fwd_mask, m, 0.0) for m in gram([gy, gp], [gu, gv])], 0)
    bwd = cat([jnp.where(bwd_mask, m, 0.0) for m in gram([gu, gv], [gy, gp])], 0)

    def apply(mat, y):
        mh, ml = split(mat)
        both = mm(mh, cat(y, 1))
        return by_head(both[:, :PAIR] + both[:, PAIR:] + mm(ml, y[0]))

    ra = apply(fwd, by)
    bk = apply(bwd, ry)
    uh, ul = split(u)
    ph, pl_ = split(p)
    start = dot3((cat([dyb, ph], 0), cat([zero, pl_], 0)), sb, NT)
    behind = dot3((cat([uh, vb], 0), cat([ul, zero], 0)), gb)
    dr = (ra[:n] + start[:n] * to_start) * fall
    da = (ra[n:] + start[n:] * to_start) * fall_before
    reach = grow * to_end
    final_u = behind[:n] * reach
    final_v = behind[n:] * reach
    db = bk[:n] * grow + final_u
    dk = bk[n:] * grow + final_v
    beta = kappa * eta
    inner = beta * final_u + k * final_v
    through = r * dr - k * dk - beta * db
    behind_a = -kappa * da
    row, col = iotas(n, n)
    from_here = jnp.where(col >= row, 1.0, 0.0).astype(BF16)
    after = jnp.where(col > row, 1.0, 0.0).astype(BF16)
    tail = mm(cat([from_here, from_here], 1), cat(split(through), 0)) + mm(
        cat([after, after], 1), cat(split(behind_a), 0)
    )
    turned = compact(flip(spread(st)))
    anchor = jnp.sum(turned * g, axis=0, keepdims=True) * decay + jnp.sum(
        inner, axis=0, keepdims=True
    )
    return (
        dr + bonus * k * dyv,
        dk + bonus * r * dyv,
        dv,
        -(tail + anchor),
        eta * db - da,
        kappa * db,
    )


def read_tokens(refs, p):
    lanes = slice(PAIR * p, PAIR * p + PAIR)
    return [ref[:, lanes].astype(F32) for ref in refs]


def final_kernel(*refs):
    ins, (state, narrow, deep, wide), outs = refs[:6], refs[6:10], refs[10:]
    got = [
        final_part(
            *read_tokens(ins, p),
            [narrow[p, i] for i in range(NARROW)],
            [deep[p, i] for i in range(DEEP)],
            [wide[p, i] for i in range(WIDE)],
            [state[p, BACK + 8 + i : BACK + 9 + i] for i in range(LINES)],
            state[p, 0:64],
            state[p, 64:128],
        )
        for p in (0, 1)
    ]
    for p in (0, 1):
        lanes = slice(PAIR * p, PAIR * p + PAIR)
        for ref, value in zip(outs, got[p]):
            ref[:, lanes] = value.astype(ref.dtype)
        outs[6][:, lanes] = state[p, BACK : BACK + 1]


ROW = 8
ROWS = 4
SEND = 192
BACK = 128
NARROW, DEEP, WIDE, LINES = 14, 4, 7, 4


def owner_of(p, d):
    return 4 * p + 2 * d


def adder_of(p, d):
    return owner_of(p, d) + 1


def joined(a, b):
    both = dot3(cat([b[1], b[2]], 0), cat([spread(a[1]), spread(a[0])], 1))
    return both[:HEAD, PAIR:] + b[0], both[:HEAD, :PAIR], both[HEAD:, :PAIR] + a[2]


def joined_states(a, b):
    both = dot3(b[1], cat([spread(a[1]), spread(a[0])], 1))
    return both[:, PAIR:] + b[0], both[:, :PAIR], None


def joined_adjoints(a, b):
    both = dot3(cat([b[1], b[2]], 0), spread(a[1]))
    return None, both[:HEAD], both[HEAD:] + a[2]


def copy_to(src, dst, ssem, rsem, where):
    return pltpu.make_async_remote_copy(
        src_ref=src,
        dst_ref=dst,
        send_sem=ssem,
        recv_sem=rsem,
        device_id=where,
        device_id_type=MESH,
    )


def front_kernel(*refs):
    (ins, outs, staged, scratch, sems) = refs[:8], refs[8:12], refs[12:20], refs[20:32], refs[32:]
    state, narrow, deep, wide = outs
    msg, recv, two, tot, xin, back, run, land, term, terms, sums, total = scratch
    in_sem, send_sem, recv_sem, xsend, xsem, osend, osem = sems[:7]
    tsend, tsem, ssend, ssem, gsend, gsem = sems[7:]
    d = lax.axis_index("dp")
    ctx = lax.axis_index("ctx")
    x = ctx // ROW
    z = ctx % ROW
    mine = [z == owner_of(p, d) for p in (0, 1)]
    is_owner = jnp.logical_or(*mine)
    pown = jnp.where(mine[1], 1, 0)
    adds = [z == adder_of(p, d) for p in (0, 1)]
    is_adder = jnp.logical_or(*adds)
    padd = jnp.where(adds[1], 1, 0)

    def at(xx, zz, dd=None):
        place = {"ctx": xx * ROW + zz}
        if dd is not None:
            place["dp"] = dd
        return place

    loads = [
        pltpu.make_async_copy(src, dst, in_sem.at[i])
        for i, (src, dst) in enumerate(zip(ins, staged))
    ]
    for load in loads:
        load.start()

    barrier = pltpu.get_barrier_semaphore()

    def greet(where):
        pl.semaphore_signal(barrier, inc=1, device_id=where, device_id_type=MESH)

    for p in (0, 1):
        for place in (owner_of(p, d), adder_of(p, d)):
            pl.when(z != place)(lambda place=place: greet(at(x, place)))

    @pl.when(is_owner | is_adder)
    def _():
        for j in (2, 3, 6, 7):
            greet(at(x, (2 * d + j) % ROW))

    @pl.when(is_owner)
    def _():
        for j in range(1, ROWS):
            greet(at((x + j) % ROWS, z))

    @pl.when(is_adder)
    def _():
        for j in range(1, ROWS):
            greet(at((x + j) % ROWS, z))
        for j in range(ROWS):
            greet(at((x + j) % ROWS, adder_of(padd, 1 - d), 1 - d))

    for load in loads:
        load.wait()
    parts = []
    for p in (0, 1):
        tokens = read_tokens(staged[:6] + staged[7:], p)
        parts.append(local_grams(*tokens, staged[6][:, PAIR * p : PAIR * p + PAIR]))
    solved = inverse(parts[0]["lw"] + parts[1]["lw"])

    def to_owner(p):
        place = jnp.where(is_owner, (z + 1) % ROW, owner_of(p, d))
        return copy_to(msg.at[p], recv.at[z], send_sem.at[p], recv_sem.at[z], at(x, place))

    pmate = 1 - padd

    def from_mate(p, slot, i, place):
        return copy_to(tot, two.at[i], send_sem.at[p], recv_sem.at[slot], place)

    messages = [local_message(parts[p], solved[2 * p : 2 * p + 2]) for p in (0, 1)]
    for p, (low, mid, high) in enumerate(messages):
        msg[p, 0:64] = low
        msg[p, 64:128] = mid
        msg[p, 128:192] = high
    pl.when(is_owner)(lambda: pl.semaphore_wait(barrier, ROW - 1 + ROWS - 1))
    pl.when(is_adder)(lambda: pl.semaphore_wait(barrier, ROW - 1 + 2 * ROWS - 1))
    pl.when(jnp.logical_not(is_owner | is_adder))(lambda: pl.semaphore_wait(barrier, 4))
    direct = [jnp.logical_not(mine[p] | adds[1 - p]) for p in (0, 1)]
    waits = (d == 1) & jnp.logical_not(is_owner)
    pl.when(direct[0])(lambda: to_owner(0).start())
    pl.when(direct[1] & jnp.logical_not(waits))(lambda: to_owner(1).start())

    for p in (0, 1):
        term[p] = jnp.broadcast_to(bonus_terms(parts[p]), (8, PAIR))

    def over_mate(place):
        rows = pl.ds(64, 128)
        return copy_to(
            msg.at[pmate, rows], xin.at[x, rows], xsend.at[0], xsem.at[x], at(x, place)
        )

    @pl.when(is_adder)
    def _():
        far = (z + ROW - 1) % ROW
        over_mate(far).start()
        copy_to(
            msg.at[0], recv.at[far], send_sem.at[0], recv_sem.at[far], at(x, far)
        ).wait_recv()
        got = joined(
            (recv[far, 0:64], recv[far, 64:128], recv[far, 128:192]),
            (msg[pmate, 0:64], msg[pmate, 64:128], msg[pmate, 128:192]),
        )
        tot[0:64] = got[0]
        tot[64:128] = got[1]
        tot[128:192] = got[2]
        from_mate(pmate, z, z // 2, at(x, owner_of(pmate, d))).start()

    def to_adder(p):
        return copy_to(
            term.at[p], terms.at[z], tsend.at[p], tsem.at[z], at(x, adder_of(p, d))
        )

    for p in (0, 1):
        pl.when(jnp.logical_not(adds[p]))(lambda p=p: to_adder(p).start())

    rests = [local_rest(parts[p]) for p in (0, 1)]
    for p, got in enumerate(rests):
        for ref, values in zip((narrow, deep, wide), got):
            for i, value in enumerate(values):
                ref[p, i] = value
        for i, line in enumerate(got[3]):
            state[p, BACK + 8 + i : BACK + 9 + i] = line

    pl.when(direct[1] & waits)(lambda: to_owner(1).start())

    @pl.when(is_adder)
    def _():
        terms[z] = term[padd]
        for j in range(1, ROW):
            zz = (z + j) % ROW
            copy_to(term.at[0], terms.at[zz], tsend.at[0], tsem.at[zz], at(x, zz)).wait_recv()
        part = terms[0]
        for i in range(1, ROW):
            part = part + terms[i]
        me = d * ROWS + x
        sums[me] = part
        places = [((x + j) % ROWS, d) for j in range(1, ROWS)]
        places += [((x + j) % ROWS, 1 - d) for j in range(ROWS)]
        across = [
            copy_to(
                sums.at[me], sums.at[me], ssend.at[i], ssem.at[me], at(xx, adder_of(padd, dd), dd)
            )
            for i, (xx, dd) in enumerate(places)
        ]
        for copy in across:
            copy.start()
        for xx, dd in places:
            slot = dd * ROWS + xx
            copy_to(
                sums.at[slot], sums.at[slot], ssend.at[0], ssem.at[slot], at(xx, z)
            ).wait_recv()
        part = sums[0]
        for i in range(1, 2 * ROWS):
            part = part + sums[i]
        total[padd] = part
        gives = [
            copy_to(total.at[padd], total.at[padd], gsend.at[j], gsem.at[padd], at(x, (z + j) % ROW))
            for j in range(1, ROW)
        ]
        for give in gives:
            give.start()
        for copy in across + gives:
            copy.wait_send()

    @pl.when(is_owner)
    def _():
        recv[z] = msg[pown]
        far = (z + ROW // 2) % ROW
        for zz in (far, far + 1):
            recv[zz] = jnp.zeros((SEND, PAIR), F32)
        places = [(z // 2 + j) % (ROW // 2) for j in (0, 1, 3)]
        for j, i in zip((0, 1, 3), places):
            for zz in (2 * i + 1,) if j == 0 else (2 * i, 2 * i + 1):
                copy_to(
                    msg.at[0], recv.at[zz], send_sem.at[0], recv_sem.at[zz], at(x, zz)
                ).wait_recv()
        blocks = [
            [(recv[zz, 0:64], recv[zz, 64:128], recv[zz, 128:192]) for zz in (2 * i, 2 * i + 1)]
            for i in places
        ]
        for i, got in zip(places, [joined(*both) for both in blocks]):
            two[i, 0:64] = got[0]
            two[i, 64:128] = got[1]
            two[i, 128:192] = got[2]
        from_mate(0, far + 1, far // 2, at(x, far + 1)).wait_recv()
        pair = [(two[i, 0:64], two[i, 64:128], two[i, 128:192]) for i in range(ROW // 2)]
        four = [joined(pair[0], pair[1]), joined(pair[2], pair[3])]
        whole = joined(four[0], four[1])
        tot[0:64] = whole[0]
        tot[64:128] = whole[1]
        tot[128:192] = whole[2]
        cases = (
            (lambda xx: (xx > x) & (x == 0), 0, 64),
            (lambda xx: (xx > x) & (x != 0), 0, 128),
            (lambda xx: (xx < x) & (x == ROWS - 1), 128, 192),
            (lambda xx: (xx < x) & (x != ROWS - 1), 64, 192),
        )

        def across(xx, low, high, landing):
            rows = pl.ds(low, high - low)
            return copy_to(
                tot.at[rows], xin.at[landing, rows], xsend.at[xx], xsem.at[landing], at(xx, z)
            )

        for xx in range(ROWS):
            for when, low, high in cases:
                pl.when(when(xx))(
                    lambda xx=xx, low=low, high=high: across(xx, low, high, x).start()
                )
        one = [(recv[i, 0:64], recv[i, 64:128], recv[i, 128:192]) for i in range(ROW)]
        before = [None, one[0], pair[0], None, four[0], None, None, None]
        before[3] = joined_states(pair[0], one[2])
        before[5] = joined_states(four[0], one[4])
        before[6] = joined_states(four[0], pair[2])
        before[7] = joined_states(before[6], one[6])
        behind = [None, None, None, four[1], None, pair[3], one[7], None]
        behind[4] = joined_adjoints(one[5], pair[3])
        behind[2] = joined_adjoints(one[3], four[1])
        behind[1] = joined_adjoints(pair[1], four[1])
        behind[0] = joined_adjoints(one[1], behind[1])

        run[...] = jnp.zeros_like(run)
        for xx in range(ROWS - 1):
            high = 64 if xx == 0 else 128

            @pl.when(x > xx)
            def _(xx=xx, high=high):
                across(xx, 0, high, xx).wait_recv()
                if xx == 0:
                    run[0] = xin[0, 0:64]
                else:
                    run[0] = dot3(xin[xx, 64:128], spread(run[0])) + xin[xx, 0:64]

        for xx in range(ROWS - 1, 0, -1):
            low = 128 if xx == ROWS - 1 else 64

            @pl.when(x < xx)
            def _(xx=xx, low=low):
                across(xx, low, 192, xx).wait_recv()
                if xx == ROWS - 1:
                    run[1] = xin[xx, 128:192]
                else:
                    run[1] = dot3(run[1], spread(xin[xx, 64:128])) + xin[xx, 128:192]

        sg, gg = run[0], run[1]
        moved = dot3(cat([before[i][1] for i in range(1, ROW)], 0), spread(sg))
        for i in range(ROW):
            back[i, 0:64] = sg if i == 0 else moved[64 * i - 64 : 64 * i] + before[i][0]
        gs = split(gg)
        for i in range(0, ROW, 2):
            if i + 1 < ROW - 1:
                got = dot3(gs, cat([spread(behind[i][1]), spread(behind[i + 1][1])], 1))
                back[i, 64:128] = got[:, :PAIR] + behind[i][2]
                back[i + 1, 64:128] = got[:, PAIR:] + behind[i + 1][2]
            else:
                back[i, 64:128] = dot3(gs, spread(behind[i][1])) + behind[i][2]
                back[i + 1, 64:128] = gg

        back[far + 1, 0:64] = back[far, 0:64]
        gives = []
        for j in (4, 5, 3, 2, 6, 1, 7):
            zz = (z + j) % ROW
            source = back.at[far + 1] if j == 4 else back.at[zz]
            gives.append(
                copy_to(source, land.at[pown], osend.at[j], osem.at[pown], at(x, zz))
            )
            gives[-1].start()
        land[pown] = back[z]
        for give in gives:
            give.wait_send()
        for xx in range(ROWS):
            for when, low, high in cases:
                pl.when(when(xx))(
                    lambda xx=xx, low=low, high=high: across(xx, low, high, x).wait_send()
                )

    for p in (0, 1):

        @pl.when(jnp.logical_not(mine[p]))
        def _(p=p):
            to_owner(p).wait_send()
            copy_to(
                back.at[0], land.at[p], osend.at[0], osem.at[p], at(x, owner_of(p, d))
            ).wait_recv()

        @pl.when(adds[1 - p])
        def _(p=p):
            far = (z + ROW - 1) % ROW
            land[p, 0:64] = dot3(recv[far, 64:128], spread(land[p, 0:64])) + recv[far, 0:64]

        @pl.when(mine[1 - p])
        def _(p=p):
            over_mate(z).wait_recv()
            over = dot3(land[p, 64:128], spread(xin[x, 64:128]))
            land[p, 64:128] = over + xin[x, 128:192]

    for p in (0, 1):

        @pl.when(jnp.logical_not(adds[p]))
        def _(p=p):
            to_adder(p).wait_send()
            copy_to(
                total.at[p], total.at[p], gsend.at[0], gsem.at[p], at(x, adder_of(p, d))
            ).wait_recv()

    @pl.when(is_adder)
    def _():
        over_mate(z).wait_send()

    for p in (0, 1):
        state[p, 0:BACK] = land[p]
        state[p, BACK : BACK + 8] = total[p]


VMEM = pl.BlockSpec(memory_space=pltpu.VMEM)
HBM = pl.BlockSpec(memory_space=pltpu.HBM)


def local(r, k, v, w, kappa, eta, extra, dy):
    rows, width = r.shape[1], r.shape[2]
    pairs = width // PAIR
    flat = [t.reshape(rows, width) for t in (r, k, v, w, kappa, eta)]
    ins = (*flat, extra.reshape(1, width), dy.reshape(rows, width))
    f32 = lambda *shape: jax.ShapeDtypeStruct(shape, F32)
    dma = lambda n: pltpu.SemaphoreType.DMA((n,))
    bf16 = lambda *shape: jax.ShapeDtypeStruct(shape, BF16)
    kept = pl.pallas_call(
        front_kernel,
        out_shape=(
            f32(pairs, BACK + 16, PAIR),
            bf16(pairs, NARROW, rows, PAIR),
            bf16(pairs, DEEP, 2 * rows, PAIR),
            f32(pairs, WIDE, rows, PAIR),
        ),
        in_specs=[HBM] * 8,
        out_specs=[VMEM] * 4,
        scratch_shapes=[
            *[pltpu.VMEM(t.shape, t.dtype) for t in ins],
            pltpu.VMEM((pairs, SEND, PAIR), F32),
            pltpu.VMEM((ROW, SEND, PAIR), F32),
            pltpu.VMEM((ROW // 2, SEND, PAIR), F32),
            pltpu.VMEM((SEND, PAIR), F32),
            pltpu.VMEM((ROWS, SEND, PAIR), F32),
            pltpu.VMEM((ROW, BACK, PAIR), F32),
            pltpu.VMEM((2, HEAD, PAIR), F32),
            pltpu.VMEM((pairs, BACK, PAIR), F32),
            pltpu.VMEM((pairs, 8, PAIR), F32),
            pltpu.VMEM((ROW, 8, PAIR), F32),
            pltpu.VMEM((2 * ROWS, 8, PAIR), F32),
            pltpu.VMEM((pairs, 8, PAIR), F32),
            *[dma(n) for n in (8, 2, ROW, ROWS, ROWS, ROW, 2)],
            *[dma(n) for n in (2, ROW, 2 * ROWS, 2 * ROWS, ROW, 2)],
        ],
        compiler_params=pltpu.CompilerParams(
            collective_id=0, has_side_effects=True, vmem_limit_bytes=48 * 1024 * 1024
        ),
    )(*[pltpu.with_memory_space_constraint(t, pltpu.HBM) for t in ins])
    *grads, bonus = pl.pallas_call(
        final_kernel,
        out_shape=(*[bf16(rows, width)] * 6, f32(1, width)),
        in_specs=[VMEM] * 10,
        out_specs=[VMEM] * 7,
        compiler_params=pltpu.CompilerParams(vmem_limit_bytes=40 * 1024 * 1024),
    )(*[ins[i] for i in (0, 1, 2, 4, 5, 7)], *kept)
    return (*[t.reshape(1, rows, width) for t in grads], bonus.reshape(width))


def solution(mesh):
    block = P("dp", "ctx", "tp")
    return jax.shard_map(
        local,
        mesh=mesh,
        in_specs=(block,) * 6 + (P("tp"), block),
        out_specs=(block,) * 6 + (P("tp"),),
        check_vma=False,
    )
```

```python
import functools

import jax
import jax.numpy as jnp
from jax import lax
from jax.experimental import pallas as pl
from jax.experimental.pallas import tpu as pltpu
from jax.sharding import PartitionSpec as P

HEAD = 64
PAIR = 128
F32 = jnp.float32
BF16 = jnp.bfloat16
MESH = pl.DeviceIdType.MESH
NN = (((1,), (0,)), ((), ()))
NT = (((1,), (1,)), ((), ()))


def split(x):
    high = x.astype(BF16)
    low = (x - high.astype(F32)).astype(BF16)
    return high, low


def mm(x, y, dims=NN):
    return lax.dot_general(x, y, dims, preferred_element_type=F32)


def cat(parts, axis):
    return jnp.concatenate(parts, axis=axis)


def dot3(x, y, dims=NN):
    xh, xl = split(x) if not isinstance(x, tuple) else x
    yh, yl = split(y) if not isinstance(y, tuple) else y
    axis = 0 if dims is NN else 1
    if yh.shape == (PAIR, PAIR):
        wide = cat([cat([yh, yl], 1 - axis)] * 2, axis)
        both = mm(cat([xh, xl], 1), wide, dims)
        return both[:, :PAIR] + both[:, PAIR:]
    return mm(cat([xh, xl], 1), cat([yh, yh], axis), dims) + mm(xh, yl, dims)


def dot2(x, y, dims=NN):
    xh, xl = split(x) if not isinstance(x, tuple) else x
    axis = 0 if dims is NN else 1
    return mm(cat([xh, xl], 1), cat([y, y], axis), dims)


def iotas(rows, cols):
    return (
        lax.broadcasted_iota(jnp.int32, (rows, cols), 0),
        lax.broadcasted_iota(jnp.int32, (rows, cols), 1),
    )


def first_half(shape):
    return (lax.broadcasted_iota(jnp.int32, shape, 1) & (PAIR - 1)) < HEAD


def by_head(stacked):
    half = stacked.shape[0] // 2
    top, bottom = stacked[:half], stacked[half:]
    return jnp.where(first_half(top.shape), top, bottom)


def own_lanes(x):
    mine = first_half(x.shape)
    return jnp.where(mine, x, 0.0), jnp.where(mine, 0.0, x)


def compact(blocks):
    return by_head(blocks)


def spread(x):
    return cat(list(own_lanes(x)), 0)


def turned_lanes(x):
    return pltpu.roll(x, HEAD, 1)


def gram_parts(x):
    high = x.astype(BF16).astype(F32)
    low = x - high
    high_t, low_t = turned_lanes(high), turned_lanes(low)
    mine = first_half(x.shape)
    pick = lambda a, b: jnp.where(mine, a, b).astype(BF16)
    return (
        (pick(high, low_t), pick(high, high_t), pick(low, low_t)),
        (pick(high_t, low), pick(high_t, high), pick(low_t, low)),
    )


def gram(lefts, rights):
    out = []
    for h in (0, 1):
        left = cat([x[h][0] for x in lefts], 0)
        right = [cat([x[h][i] for x in rights], 0) for i in (1, 2)]
        out.append(mm(cat([left, left], 1), cat(right, 1), NT))
    return out


def flip(x):
    return jnp.swapaxes(x, 0, 1)


def prepare(r, k, w, kappa, eta):
    n = w.shape[0]
    row, col = iotas(n, n)
    tri = jnp.where(row >= col, 1.0, 0.0).astype(BF16)
    wh = w.astype(BF16)
    rest = w - wh.astype(F32)
    wm = rest.astype(BF16)
    wl = (rest - wm.astype(F32)).astype(BF16)
    c = mm(cat([tri, tri], 1), cat([wh, wm], 0)) + mm(tri, wl)
    mid = c[n // 2 : n // 2 + 1]
    end = c[n - 1 : n]
    grow = jnp.exp(c - mid)
    fall = jnp.exp(mid - c)
    fall_before = jnp.exp(mid - (c - w))
    beta = kappa * eta
    out = dict(
        end=end,
        grow=grow,
        fall=fall,
        fall_before=fall_before,
        to_start=jnp.exp(-mid),
        to_end=jnp.exp(mid - end),
        beta=beta,
        rs=r * fall,
        ks=k * grow,
        bs=beta * grow,
        asc=-kappa * fall_before,
    )
    out["a0"] = out["asc"] * out["to_start"]
    out["r0"] = out["rs"] * out["to_start"]
    out["bf"] = out["bs"] * out["to_end"]
    out["kf"] = out["ks"] * out["to_end"]
    return out


def inverse(lows):
    n = lows[0].shape[0]
    row, col = iotas(n, n)
    eye = jnp.where(row == col, 1.0, 0.0)
    start = (row >> 4) == (col >> 4)
    d1 = [jnp.where(start, low, 0.0) for low in lows]
    s1 = [split(d) for d in d1]
    d2 = [dot3(s, s) for s in s1]
    s2 = [split(d) for d in d2]
    d4 = [dot3(s, s) for s in s2]
    p4 = [eye + a + b + dot3(s, t) for a, b, s, t in zip(d1, d2, s1, s2)]
    s4 = [split(d) for d in d4]
    d8 = [dot3(s, s) for s in s4]
    p8 = [p + dot3(p, s) for p, s in zip(p4, s4)]
    t = [split(p + dot3(p, d)) for p, d in zip(p8, d8)]
    rest = [jnp.where(start, 0.0, low) for low in lows]
    x1 = [split(dot3(s, r)) for s, r in zip(t, rest)]
    x2 = [split(dot3(s, s)) for s in x1]
    y1 = [a[0].astype(F32) + a[1].astype(F32) + dot3(s, a) for s, a in zip(x1, t)]
    x4 = [split(dot3(s, s)) for s in x2]
    y2 = [y + dot3(s, y) for s, y in zip(x2, y1)]
    return [y + dot3(s, y) for s, y in zip(x4, y2)]


def local_grams(r, k, v, w, kappa, eta, dy, bonus):
    n = w.shape[0]
    q = prepare(r, k, w, kappa, eta)
    q.update(r=r, k=k, v=v, dy=dy, bonus=bonus, vb=v.astype(BF16), dyb=dy.astype(BF16))
    row, col = iotas(n, n)
    pa, pr, pb, pk = [gram_parts(q[name]) for name in ("asc", "rs", "bs", "ks")]
    lower = gram([pa], [pb, pk])
    upper = gram([pb], [pr])
    q["late"] = pk, pr, pa
    q["lw"] = [jnp.where(row > col, t[:, :n], 0.0) for t in lower]
    q["lk"] = cat([jnp.where(row > col, t[:, n:], 0.0) for t in lower], 0)
    q["wwt"] = cat([jnp.where(col >= row, t, 0.0) for t in upper], 0)
    q["z"] = by_head(dot2(q["lk"], q["vb"]))
    q["zd"] = by_head(dot2(q["wwt"], q["dyb"]))
    return q


def local_message(q, t):
    n = q["z"].shape[0]
    eu = by_head(dot3(cat(t, 0), cat([q["a0"], q["z"]], 1)))
    turned = split(cat([flip(x) for x in t], 0))
    p_own = by_head(dot3(turned, q["zd"]))
    ml = dot3(flip(q["bf"]), eu)
    row, col = iotas(HEAD, PAIR)
    decay = jnp.where(row == (col & (HEAD - 1)), jnp.exp(-q["end"]), 0.0)
    mt = decay + compact(ml[:, :n])
    lt = compact(ml[:, n:] + dot2(flip(q["kf"]), q["vb"]))
    ht = compact(flip(dot3(flip(q["a0"]), p_own) + dot2(flip(q["r0"]), q["dyb"])))
    q.update(eu=eu, turned=turned, p_own=p_own)
    return lt, mt, ht


def bonus_terms(q):
    row, col = iotas(PAIR, PAIR)
    ones = jnp.where((row >> 6) == (col >> 6), 1.0, 0.0).astype(BF16)
    dyv = dot2(q["dy"] * q["v"], ones)
    q.update(ones=ones, dyv=dyv)
    return jnp.sum(dyv * q["r"] * q["k"], axis=0, keepdims=True)


def exact_parts(x):
    other = turned_lanes(x)
    mine = first_half(x.shape)
    pick = lambda a, b: jnp.where(mine, a, b).astype(BF16)
    return pick(x, 0.0), pick(x, other), pick(other, 0.0), pick(other, x)


def local_rest(q):
    n = q["z"].shape[0]
    eu = q["eu"]
    fp = cat([by_head(dot3(q["turned"], q["bf"])), q["p_own"]], 1)
    pk, pr, pa = q["late"]
    upper = gram([pk], [pr, pa])
    row, col = iotas(n, n)
    wkt = cat([jnp.where(col >= row, t[:, :n], 0.0) for t in upper], 0)
    lkt = cat([jnp.where(col > row, t[:, n:], 0.0) for t in upper], 0)
    more = by_head(dot3(lkt, fp))
    kg = q["kf"] + more[:, :n]
    dv = more[:, n:] + by_head(dot2(wkt, q["dyb"]))
    dv = dv + dot2(q["r"] * q["k"] * q["bonus"], q["ones"]) * q["dy"]
    narrow = [*split(eu[:, :n]), *split(fp[:, :n]), *split(kg)]
    narrow += [*exact_parts(q["v"]), *exact_parts(q["dy"])]
    deep = [*split(cat([q["bs"], q["ks"]], 0)), *split(cat([q["rs"], q["asc"]], 0))]
    wide = [eu[:, n:], fp[:, n:], dv, q["dyv"], q["fall"], q["fall_before"], q["grow"]]
    lines = [q["bonus"], q["to_start"], q["to_end"], jnp.exp(-q["end"])]
    return narrow, deep, wide, lines


def final_part(r, k, v, kappa, eta, dy, narrow, deep, wide, lines, st, g):
    n = r.shape[0]
    eh, el, fh, fl, kgh, kgl, *exact = narrow
    by, ry = deep[:2], deep[2:]
    u_own, p_own, dv_own, dyv, fall, fall_before, grow = wide
    bonus, to_start, to_end, decay = lines
    vb, dyb = v.astype(BF16), dy.astype(BF16)
    sb = split(spread(st))
    gb = split(spread(g))
    u = u_own + dot3((eh, el), sb)
    p = p_own + dot3((fh, fl), gb, NT)
    dv = dv_own + dot3((kgh, kgl), gb, NT)
    zero = jnp.zeros((n, PAIR), BF16)
    gv = ((exact[0], exact[1], zero), (exact[2], exact[3], zero))
    gy = ((exact[4], exact[5], zero), (exact[6], exact[7], zero))
    gu, gp = gram_parts(u), gram_parts(p)
    row, col = iotas(2 * n, 2 * n)
    t, s = row & (n - 1), col & (n - 1)
    fwd_mask = t >= s + jnp.where(row >= n, 1, 0)
    bwd_mask = s >= t + jnp.where(col >= n, 1, 0)
    fwd = cat([jnp.where(fwd_mask, m, 0.0) for m in gram([gy, gp], [gu, gv])], 0)
    bwd = cat([jnp.where(bwd_mask, m, 0.0) for m in gram([gu, gv], [gy, gp])], 0)

    def apply(mat, y):
        mh, ml = split(mat)
        both = mm(mh, cat(y, 1))
        return by_head(both[:, :PAIR] + both[:, PAIR:] + mm(ml, y[0]))

    ra = apply(fwd, by)
    bk = apply(bwd, ry)
    uh, ul = split(u)
    ph, pl_ = split(p)
    start = dot3((cat([dyb, ph], 0), cat([zero, pl_], 0)), sb, NT)
    behind = dot3((cat([uh, vb], 0), cat([ul, zero], 0)), gb)
    dr = (ra[:n] + start[:n] * to_start) * fall
    da = (ra[n:] + start[n:] * to_start) * fall_before
    reach = grow * to_end
    final_u = behind[:n] * reach
    final_v = behind[n:] * reach
    db = bk[:n] * grow + final_u
    dk = bk[n:] * grow + final_v
    beta = kappa * eta
    inner = beta * final_u + k * final_v
    through = r * dr - k * dk - beta * db
    behind_a = -kappa * da
    row, col = iotas(n, n)
    from_here = jnp.where(col >= row, 1.0, 0.0).astype(BF16)
    after = jnp.where(col > row, 1.0, 0.0).astype(BF16)
    tail = mm(cat([from_here, from_here], 1), cat(split(through), 0)) + mm(
        cat([after, after], 1), cat(split(behind_a), 0)
    )
    turned = compact(flip(spread(st)))
    anchor = jnp.sum(turned * g, axis=0, keepdims=True) * decay + jnp.sum(
        inner, axis=0, keepdims=True
    )
    return (
        dr + bonus * k * dyv,
        dk + bonus * r * dyv,
        dv,
        -(tail + anchor),
        eta * db - da,
        kappa * db,
    )


def read_tokens(refs, p):
    lanes = slice(PAIR * p, PAIR * p + PAIR)
    return [ref[:, lanes].astype(F32) for ref in refs]


def final_kernel(*refs):
    ins, (state, narrow, deep, wide), outs = refs[:6], refs[6:10], refs[10:]
    got = [
        final_part(
            *read_tokens(ins, p),
            [narrow[p, i] for i in range(NARROW)],
            [deep[p, i] for i in range(DEEP)],
            [wide[p, i] for i in range(WIDE)],
            [state[p, BACK + 8 + i : BACK + 9 + i] for i in range(LINES)],
            state[p, 0:64],
            state[p, 64:128],
        )
        for p in (0, 1)
    ]
    for p in (0, 1):
        lanes = slice(PAIR * p, PAIR * p + PAIR)
        for ref, value in zip(outs, got[p]):
            ref[:, lanes] = value.astype(ref.dtype)
        outs[6][:, lanes] = state[p, BACK : BACK + 1]


ROW = 8
ROWS = 4
SEND = 192
BACK = 128
NARROW, DEEP, WIDE, LINES = 14, 4, 7, 4


def owner_of(p, d):
    return 4 * p + 2 * d


def adder_of(p, d):
    return owner_of(p, d) + 1


def joined(a, b):
    both = dot3(cat([b[1], b[2]], 0), cat([spread(a[1]), spread(a[0])], 1))
    return both[:HEAD, PAIR:] + b[0], both[:HEAD, :PAIR], both[HEAD:, :PAIR] + a[2]


def joined_states(a, b):
    both = dot3(b[1], cat([spread(a[1]), spread(a[0])], 1))
    return both[:, PAIR:] + b[0], both[:, :PAIR], None


def joined_adjoints(a, b):
    both = dot3(cat([b[1], b[2]], 0), spread(a[1]))
    return None, both[:HEAD], both[HEAD:] + a[2]


def copy_to(src, dst, ssem, rsem, where):
    return pltpu.make_async_remote_copy(
        src_ref=src,
        dst_ref=dst,
        send_sem=ssem,
        recv_sem=rsem,
        device_id=where,
        device_id_type=MESH,
    )


def front_kernel(*refs):
    (ins, outs, staged, scratch, sems) = refs[:8], refs[8:12], refs[12:20], refs[20:32], refs[32:]
    state, narrow, deep, wide = outs
    msg, recv, two, tot, xin, back, run, land, term, terms, sums, total = scratch
    in_sem, send_sem, recv_sem, xsend, xsem, osend, osem = sems[:7]
    tsend, tsem, ssend, ssem, gsend, gsem = sems[7:]
    d = lax.axis_index("dp")
    ctx = lax.axis_index("ctx")
    x = ctx // ROW
    z = ctx % ROW
    mine = [z == owner_of(p, d) for p in (0, 1)]
    is_owner = jnp.logical_or(*mine)
    pown = jnp.where(mine[1], 1, 0)
    adds = [z == adder_of(p, d) for p in (0, 1)]
    is_adder = jnp.logical_or(*adds)
    padd = jnp.where(adds[1], 1, 0)

    def at(xx, zz, dd=None):
        place = {"ctx": xx * ROW + zz}
        if dd is not None:
            place["dp"] = dd
        return place

    loads = [
        pltpu.make_async_copy(src, dst, in_sem.at[i])
        for i, (src, dst) in enumerate(zip(ins, staged))
    ]
    for load in loads:
        load.start()

    barrier = pltpu.get_barrier_semaphore()

    def greet(where):
        pl.semaphore_signal(barrier, inc=1, device_id=where, device_id_type=MESH)

    for p in (0, 1):
        for place in (owner_of(p, d), adder_of(p, d)):
            pl.when(z != place)(lambda place=place: greet(at(x, place)))

    @pl.when(is_owner | is_adder)
    def _():
        for j in (2, 3, 6, 7):
            greet(at(x, (2 * d + j) % ROW))

    @pl.when(is_owner)
    def _():
        for j in range(1, ROWS):
            greet(at((x + j) % ROWS, z))

    @pl.when(is_adder)
    def _():
        for j in range(1, ROWS):
            greet(at((x + j) % ROWS, z))
        for j in range(ROWS):
            greet(at((x + j) % ROWS, adder_of(padd, 1 - d), 1 - d))

    for load in loads:
        load.wait()
    parts = []
    for p in (0, 1):
        tokens = read_tokens(staged[:6] + staged[7:], p)
        parts.append(local_grams(*tokens, staged[6][:, PAIR * p : PAIR * p + PAIR]))
    solved = inverse(parts[0]["lw"] + parts[1]["lw"])

    def to_owner(p):
        place = jnp.where(is_owner, (z + 1) % ROW, owner_of(p, d))
        return copy_to(msg.at[p], recv.at[z], send_sem.at[p], recv_sem.at[z], at(x, place))

    pmate = 1 - padd

    def from_mate(p, slot, i, place):
        return copy_to(tot, two.at[i], send_sem.at[p], recv_sem.at[slot], place)

    messages = [local_message(parts[p], solved[2 * p : 2 * p + 2]) for p in (0, 1)]
    for p, (low, mid, high) in enumerate(messages):
        msg[p, 0:64] = low
        msg[p, 64:128] = mid
        msg[p, 128:192] = high
    pl.when(is_owner)(lambda: pl.semaphore_wait(barrier, ROW - 1 + ROWS - 1))
    pl.when(is_adder)(lambda: pl.semaphore_wait(barrier, ROW - 1 + 2 * ROWS - 1))
    pl.when(jnp.logical_not(is_owner | is_adder))(lambda: pl.semaphore_wait(barrier, 4))
    for p in (0, 1):
        direct = jnp.logical_not(mine[p] | adds[1 - p])
        pl.when(direct)(lambda p=p: to_owner(p).start())

    for p in (0, 1):
        term[p] = jnp.broadcast_to(bonus_terms(parts[p]), (8, PAIR))

    def over_mate(place):
        rows = pl.ds(64, 128)
        return copy_to(
            msg.at[pmate, rows], xin.at[x, rows], xsend.at[0], xsem.at[x], at(x, place)
        )

    @pl.when(is_adder)
    def _():
        far = (z + ROW - 1) % ROW
        over_mate(far).start()
        copy_to(
            msg.at[0], recv.at[far], send_sem.at[0], recv_sem.at[far], at(x, far)
        ).wait_recv()
        got = joined(
            (recv[far, 0:64], recv[far, 64:128], recv[far, 128:192]),
            (msg[pmate, 0:64], msg[pmate, 64:128], msg[pmate, 128:192]),
        )
        tot[0:64] = got[0]
        tot[64:128] = got[1]
        tot[128:192] = got[2]
        from_mate(pmate, z, z // 2, at(x, owner_of(pmate, d))).start()

    def to_adder(p):
        return copy_to(
            term.at[p], terms.at[z], tsend.at[p], tsem.at[z], at(x, adder_of(p, d))
        )

    for p in (0, 1):
        pl.when(jnp.logical_not(adds[p]))(lambda p=p: to_adder(p).start())

    for p in (0, 1):
        got = local_rest(parts[p])
        for ref, values in zip((narrow, deep, wide), got):
            for i, value in enumerate(values):
                ref[p, i] = value
        for i, line in enumerate(got[3]):
            state[p, BACK + 8 + i : BACK + 9 + i] = line

    @pl.when(is_adder)
    def _():
        terms[z] = term[padd]
        for j in range(1, ROW):
            zz = (z + j) % ROW
            copy_to(term.at[0], terms.at[zz], tsend.at[0], tsem.at[zz], at(x, zz)).wait_recv()
        part = terms[0]
        for i in range(1, ROW):
            part = part + terms[i]
        me = d * ROWS + x
        sums[me] = part
        places = [((x + j) % ROWS, d) for j in range(1, ROWS)]
        places += [((x + j) % ROWS, 1 - d) for j in range(ROWS)]
        across = [
            copy_to(
                sums.at[me], sums.at[me], ssend.at[i], ssem.at[me], at(xx, adder_of(padd, dd), dd)
            )
            for i, (xx, dd) in enumerate(places)
        ]
        for copy in across:
            copy.start()
        for xx, dd in places:
            slot = dd * ROWS + xx
            copy_to(
                sums.at[slot], sums.at[slot], ssend.at[0], ssem.at[slot], at(xx, z)
            ).wait_recv()
        part = sums[0]
        for i in range(1, 2 * ROWS):
            part = part + sums[i]
        total[padd] = part
        gives = [
            copy_to(total.at[padd], total.at[padd], gsend.at[j], gsem.at[padd], at(x, (z + j) % ROW))
            for j in range(1, ROW)
        ]
        for give in gives:
            give.start()
        for copy in across + gives:
            copy.wait_send()

    @pl.when(is_owner)
    def _():
        recv[z] = msg[pown]
        far = (z + ROW // 2) % ROW
        for zz in (far, far + 1):
            recv[zz] = jnp.zeros((SEND, PAIR), F32)
        places = [(z // 2 + j) % (ROW // 2) for j in (0, 1, 3)]
        for j, i in zip((0, 1, 3), places):
            for zz in (2 * i + 1,) if j == 0 else (2 * i, 2 * i + 1):
                copy_to(
                    msg.at[0], recv.at[zz], send_sem.at[0], recv_sem.at[zz], at(x, zz)
                ).wait_recv()
        blocks = [
            [(recv[zz, 0:64], recv[zz, 64:128], recv[zz, 128:192]) for zz in (2 * i, 2 * i + 1)]
            for i in places
        ]
        for i, got in zip(places, [joined(*both) for both in blocks]):
            two[i, 0:64] = got[0]
            two[i, 64:128] = got[1]
            two[i, 128:192] = got[2]
        from_mate(0, far + 1, far // 2, at(x, far + 1)).wait_recv()
        pair = [(two[i, 0:64], two[i, 64:128], two[i, 128:192]) for i in range(ROW // 2)]
        four = [joined(pair[0], pair[1]), joined(pair[2], pair[3])]
        whole = joined(four[0], four[1])
        tot[0:64] = whole[0]
        tot[64:128] = whole[1]
        tot[128:192] = whole[2]
        def rows_for(here, there):
            if there > here:
                return (0, 64) if here == 0 else (0, 128)
            return (128, 192) if here == ROWS - 1 else (64, 192)

        def rows_cases(act):
            for here in range(ROWS):

                @pl.when(x == here)
                def _(here=here):
                    for there in sorted(range(ROWS), key=lambda r: -abs(r - here)):
                        if there != here:
                            act(across(there, *rows_for(here, there), here))

        def across(xx, low, high, landing):
            rows = pl.ds(low, high - low)
            return copy_to(
                tot.at[rows], xin.at[landing, rows], xsend.at[xx], xsem.at[landing], at(xx, z)
            )

        rows_cases(lambda copy: copy.start())

        one = [(recv[i, 0:64], recv[i, 64:128], recv[i, 128:192]) for i in range(ROW)]
        before = [None, one[0], pair[0], None, four[0], None, None, None]
        before[3] = joined_states(pair[0], one[2])
        before[5] = joined_states(four[0], one[4])
        before[6] = joined_states(four[0], pair[2])
        before[7] = joined_states(before[6], one[6])
        behind = [None, None, None, four[1], None, pair[3], one[7], None]
        behind[4] = joined_adjoints(one[5], pair[3])
        behind[2] = joined_adjoints(one[3], four[1])
        behind[1] = joined_adjoints(pair[1], four[1])
        behind[0] = joined_adjoints(one[1], behind[1])

        for here in range(ROWS):

            @pl.when(x == here)
            def _(here=here):
                for there in range(ROWS):
                    if there != here:
                        across(there, *rows_for(there, here), there).wait_recv()
                start = end = jnp.zeros((HEAD, PAIR), F32)
                for there in range(here):
                    if there:
                        start = dot3(xin[there, 64:128], spread(start)) + xin[there, 0:64]
                    else:
                        start = xin[0, 0:64]
                for there in range(ROWS - 1, here, -1):
                    if there < ROWS - 1:
                        end = dot3(end, spread(xin[there, 64:128])) + xin[there, 128:192]
                    else:
                        end = xin[there, 128:192]
                run[0] = start
                run[1] = end

        sg, gg = run[0], run[1]
        moved = dot3(cat([before[i][1] for i in range(1, ROW)], 0), spread(sg))
        for i in range(ROW):
            back[i, 0:64] = sg if i == 0 else moved[64 * i - 64 : 64 * i] + before[i][0]
        gs = split(gg)
        for i in range(0, ROW, 2):
            if i + 1 < ROW - 1:
                got = dot3(gs, cat([spread(behind[i][1]), spread(behind[i + 1][1])], 1))
                back[i, 64:128] = got[:, :PAIR] + behind[i][2]
                back[i + 1, 64:128] = got[:, PAIR:] + behind[i + 1][2]
            else:
                back[i, 64:128] = dot3(gs, spread(behind[i][1])) + behind[i][2]
                back[i + 1, 64:128] = gg

        back[far + 1, 0:64] = back[far, 0:64]
        gives = []
        for j in (4, 5, 3, 2, 6, 1, 7):
            zz = (z + j) % ROW
            source = back.at[far + 1] if j == 4 else back.at[zz]
            gives.append(
                copy_to(source, land.at[pown], osend.at[j], osem.at[pown], at(x, zz))
            )
            gives[-1].start()
        land[pown] = back[z]
        for give in gives:
            give.wait_send()
        rows_cases(lambda copy: copy.wait_send())

    for p in (0, 1):

        @pl.when(jnp.logical_not(mine[p]))
        def _(p=p):
            to_owner(p).wait_send()
            copy_to(
                back.at[0], land.at[p], osend.at[0], osem.at[p], at(x, owner_of(p, d))
            ).wait_recv()

        @pl.when(adds[1 - p])
        def _(p=p):
            far = (z + ROW - 1) % ROW
            land[p, 0:64] = dot3(recv[far, 64:128], spread(land[p, 0:64])) + recv[far, 0:64]

        @pl.when(mine[1 - p])
        def _(p=p):
            over_mate(z).wait_recv()
            over = dot3(land[p, 64:128], spread(xin[x, 64:128]))
            land[p, 64:128] = over + xin[x, 128:192]

    for p in (0, 1):

        @pl.when(jnp.logical_not(adds[p]))
        def _(p=p):
            to_adder(p).wait_send()
            copy_to(
                total.at[p], total.at[p], gsend.at[0], gsem.at[p], at(x, adder_of(p, d))
            ).wait_recv()

    @pl.when(is_adder)
    def _():
        over_mate(z).wait_send()

    for p in (0, 1):
        state[p, 0:BACK] = land[p]
        state[p, BACK : BACK + 8] = total[p]


VMEM = pl.BlockSpec(memory_space=pltpu.VMEM)
HBM = pl.BlockSpec(memory_space=pltpu.HBM)


def local(r, k, v, w, kappa, eta, extra, dy):
    rows, width = r.shape[1], r.shape[2]
    pairs = width // PAIR
    flat = [t.reshape(rows, width) for t in (r, k, v, w, kappa, eta)]
    ins = (*flat, extra.reshape(1, width), dy.reshape(rows, width))
    f32 = lambda *shape: jax.ShapeDtypeStruct(shape, F32)
    dma = lambda n: pltpu.SemaphoreType.DMA((n,))
    bf16 = lambda *shape: jax.ShapeDtypeStruct(shape, BF16)
    kept = pl.pallas_call(
        front_kernel,
        out_shape=(
            f32(pairs, BACK + 16, PAIR),
            bf16(pairs, NARROW, rows, PAIR),
            bf16(pairs, DEEP, 2 * rows, PAIR),
            f32(pairs, WIDE, rows, PAIR),
        ),
        in_specs=[HBM] * 8,
        out_specs=[VMEM] * 4,
        scratch_shapes=[
            *[pltpu.VMEM(t.shape, t.dtype) for t in ins],
            pltpu.VMEM((pairs, SEND, PAIR), F32),
            pltpu.VMEM((ROW, SEND, PAIR), F32),
            pltpu.VMEM((ROW // 2, SEND, PAIR), F32),
            pltpu.VMEM((SEND, PAIR), F32),
            pltpu.VMEM((ROWS, SEND, PAIR), F32),
            pltpu.VMEM((ROW, BACK, PAIR), F32),
            pltpu.VMEM((2, HEAD, PAIR), F32),
            pltpu.VMEM((pairs, BACK, PAIR), F32),
            pltpu.VMEM((pairs, 8, PAIR), F32),
            pltpu.VMEM((ROW, 8, PAIR), F32),
            pltpu.VMEM((2 * ROWS, 8, PAIR), F32),
            pltpu.VMEM((pairs, 8, PAIR), F32),
            *[dma(n) for n in (8, 2, ROW, ROWS, ROWS, ROW, 2)],
            *[dma(n) for n in (2, ROW, 2 * ROWS, 2 * ROWS, ROW, 2)],
        ],
        compiler_params=pltpu.CompilerParams(
            collective_id=0, has_side_effects=True, vmem_limit_bytes=48 * 1024 * 1024
        ),
    )(*[pltpu.with_memory_space_constraint(t, pltpu.HBM) for t in ins])
    *grads, bonus = pl.pallas_call(
        final_kernel,
        out_shape=(*[bf16(rows, width)] * 6, f32(1, width)),
        in_specs=[VMEM] * 10,
        out_specs=[VMEM] * 7,
        compiler_params=pltpu.CompilerParams(vmem_limit_bytes=40 * 1024 * 1024),
    )(*[ins[i] for i in (0, 1, 2, 4, 5, 7)], *kept)
    return (*[t.reshape(1, rows, width) for t in grads], bonus.reshape(width))


def solution(mesh):
    block = P("dp", "ctx", "tp")
    return jax.shard_map(
        local,
        mesh=mesh,
        in_specs=(block,) * 6 + (P("tp"), block),
        out_specs=(block,) * 6 + (P("tp"),),
        check_vma=False,
    )
```

```python
import functools

import jax
import jax.numpy as jnp
from jax import lax
from jax.experimental import pallas as pl
from jax.experimental.pallas import tpu as pltpu
from jax.sharding import PartitionSpec as P

HEAD = 64
PAIR = 128
F32 = jnp.float32
BF16 = jnp.bfloat16
MESH = pl.DeviceIdType.MESH
NN = (((1,), (0,)), ((), ()))
NT = (((1,), (1,)), ((), ()))


def split(x):
    high = x.astype(BF16)
    low = (x - high.astype(F32)).astype(BF16)
    return high, low


def mm(x, y, dims=NN):
    return lax.dot_general(x, y, dims, preferred_element_type=F32)


def cat(parts, axis):
    return jnp.concatenate(parts, axis=axis)


def dot3(x, y, dims=NN):
    xh, xl = split(x) if not isinstance(x, tuple) else x
    yh, yl = split(y) if not isinstance(y, tuple) else y
    axis = 0 if dims is NN else 1
    if yh.shape == (PAIR, PAIR):
        wide = cat([cat([yh, yl], 1 - axis)] * 2, axis)
        both = mm(cat([xh, xl], 1), wide, dims)
        return both[:, :PAIR] + both[:, PAIR:]
    return mm(cat([xh, xl, xh], 1), cat([yh, yh, yl], axis), dims)


def dot2(x, y, dims=NN):
    xh, xl = split(x) if not isinstance(x, tuple) else x
    axis = 0 if dims is NN else 1
    return mm(cat([xh, xl], 1), cat([y, y], axis), dims)


def iotas(rows, cols):
    return (
        lax.broadcasted_iota(jnp.int32, (rows, cols), 0),
        lax.broadcasted_iota(jnp.int32, (rows, cols), 1),
    )


def first_half(shape):
    return (lax.broadcasted_iota(jnp.int32, shape, 1) & (PAIR - 1)) < HEAD


def by_head(stacked):
    half = stacked.shape[0] // 2
    top, bottom = stacked[:half], stacked[half:]
    return jnp.where(first_half(top.shape), top, bottom)


def own_lanes(x):
    mine = first_half(x.shape)
    return jnp.where(mine, x, 0.0), jnp.where(mine, 0.0, x)


def compact(blocks):
    return by_head(blocks)


def spread(x):
    return cat(list(own_lanes(x)), 0)


def turned_lanes(x):
    return pltpu.roll(x, HEAD, 1)


def gram_parts(x):
    high = x.astype(BF16).astype(F32)
    low = x - high
    high_t, low_t = turned_lanes(high), turned_lanes(low)
    mine = first_half(x.shape)
    pick = lambda a, b: jnp.where(mine, a, b).astype(BF16)
    return (
        (pick(high, low_t), pick(high, high_t), pick(low, low_t)),
        (pick(high_t, low), pick(high_t, high), pick(low_t, low)),
    )


def gram(lefts, rights):
    out = []
    for h in (0, 1):
        left = cat([x[h][0] for x in lefts], 0)
        right = [cat([x[h][i] for x in rights], 0) for i in (1, 2)]
        out.append(mm(cat([left, left], 1), cat(right, 1), NT))
    return out


def flip(x):
    return jnp.swapaxes(x, 0, 1)


def prepare(r, k, w, kappa, eta):
    n = w.shape[0]
    row, col = iotas(n, n)
    tri = jnp.where(row >= col, 1.0, 0.0).astype(BF16)
    wh = w.astype(BF16)
    rest = w - wh.astype(F32)
    wm = rest.astype(BF16)
    wl = (rest - wm.astype(F32)).astype(BF16)
    c = mm(cat([tri, tri], 1), cat([wh, wm], 0)) + mm(tri, wl)
    mid = c[n // 2 : n // 2 + 1]
    end = c[n - 1 : n]
    grow = jnp.exp(c - mid)
    fall = jnp.exp(mid - c)
    fall_before = jnp.exp(mid - (c - w))
    beta = kappa * eta
    out = dict(
        end=end,
        grow=grow,
        fall=fall,
        fall_before=fall_before,
        to_start=jnp.exp(-mid),
        to_end=jnp.exp(mid - end),
        beta=beta,
        rs=r * fall,
        ks=k * grow,
        bs=beta * grow,
        asc=-kappa * fall_before,
    )
    out["a0"] = out["asc"] * out["to_start"]
    out["r0"] = out["rs"] * out["to_start"]
    out["bf"] = out["bs"] * out["to_end"]
    out["kf"] = out["ks"] * out["to_end"]
    return out


def inverse(lows):
    n = lows[0].shape[0]
    row, col = iotas(n, n)
    eye = jnp.where(row == col, 1.0, 0.0)
    start = (row >> 4) == (col >> 4)
    d1 = [jnp.where(start, low, 0.0) for low in lows]
    s1 = [split(d) for d in d1]
    d2 = [dot3(s, s) for s in s1]
    s2 = [split(d) for d in d2]
    d4 = [dot3(s, s) for s in s2]
    p4 = [eye + a + b + dot3(s, t) for a, b, s, t in zip(d1, d2, s1, s2)]
    s4 = [split(d) for d in d4]
    d8 = [dot3(s, s) for s in s4]
    p8 = [p + dot3(p, s) for p, s in zip(p4, s4)]
    t = [split(p + dot3(p, d)) for p, d in zip(p8, d8)]
    rest = [jnp.where(start, 0.0, low) for low in lows]
    x1 = [split(dot3(s, r)) for s, r in zip(t, rest)]
    x2 = [split(dot3(s, s)) for s in x1]
    y1 = [a[0].astype(F32) + a[1].astype(F32) + dot3(s, a) for s, a in zip(x1, t)]
    x4 = [split(dot3(s, s)) for s in x2]
    y2 = [y + dot3(s, y) for s, y in zip(x2, y1)]
    return [y + dot3(s, y) for s, y in zip(x4, y2)]


def local_grams(r, k, v, w, kappa, eta, dy, bonus):
    n = w.shape[0]
    q = prepare(r, k, w, kappa, eta)
    q.update(r=r, k=k, v=v, dy=dy, bonus=bonus, vb=v.astype(BF16), dyb=dy.astype(BF16))
    row, col = iotas(n, n)
    pa, pr, pb, pk = [gram_parts(q[name]) for name in ("asc", "rs", "bs", "ks")]
    lower = gram([pa], [pb, pk])
    upper = gram([pb], [pr])
    q["late"] = pk, pr, pa
    q["lw"] = [jnp.where(row > col, t[:, :n], 0.0) for t in lower]
    q["lk"] = cat([jnp.where(row > col, t[:, n:], 0.0) for t in lower], 0)
    q["wwt"] = cat([jnp.where(col >= row, t, 0.0) for t in upper], 0)
    q["z"] = by_head(dot2(q["lk"], q["vb"]))
    q["zd"] = by_head(dot2(q["wwt"], q["dyb"]))
    return q


def local_message(q, t):
    n = q["z"].shape[0]
    eu = by_head(dot3(cat(t, 0), cat([q["a0"], q["z"]], 1)))
    turned = split(cat([flip(x) for x in t], 0))
    p_own = by_head(dot3(turned, q["zd"]))
    ml = dot3(flip(q["bf"]), eu)
    row, col = iotas(HEAD, PAIR)
    decay = jnp.where(row == (col & (HEAD - 1)), jnp.exp(-q["end"]), 0.0)
    mt = decay + compact(ml[:, :n])
    lt = compact(ml[:, n:] + dot2(flip(q["kf"]), q["vb"]))
    ht = compact(flip(dot3(flip(q["a0"]), p_own) + dot2(flip(q["r0"]), q["dyb"])))
    q.update(eu=eu, turned=turned, p_own=p_own)
    return lt, mt, ht


def bonus_terms(q):
    row, col = iotas(PAIR, PAIR)
    ones = jnp.where((row >> 6) == (col >> 6), 1.0, 0.0).astype(BF16)
    dyv = dot2(q["dy"] * q["v"], ones)
    q.update(ones=ones, dyv=dyv)
    return jnp.sum(dyv * q["r"] * q["k"], axis=0, keepdims=True)


def exact_parts(x):
    other = turned_lanes(x)
    mine = first_half(x.shape)
    pick = lambda a, b: jnp.where(mine, a, b).astype(BF16)
    return pick(x, 0.0), pick(x, other), pick(other, 0.0), pick(other, x)


def local_rest(q):
    n = q["z"].shape[0]
    eu = q["eu"]
    fp = cat([by_head(dot3(q["turned"], q["bf"])), q["p_own"]], 1)
    pk, pr, pa = q["late"]
    upper = gram([pk], [pr, pa])
    row, col = iotas(n, n)
    wkt = cat([jnp.where(col >= row, t[:, :n], 0.0) for t in upper], 0)
    lkt = cat([jnp.where(col > row, t[:, n:], 0.0) for t in upper], 0)
    more = by_head(dot3(lkt, fp))
    kg = q["kf"] + more[:, :n]
    dv = more[:, n:] + by_head(dot2(wkt, q["dyb"]))
    dv = dv + dot2(q["r"] * q["k"] * q["bonus"], q["ones"]) * q["dy"]
    narrow = [*split(eu[:, :n]), *split(fp[:, :n]), *split(kg)]
    narrow += [*exact_parts(q["v"]), *exact_parts(q["dy"])]
    deep = [*split(cat([q["bs"], q["ks"]], 0)), *split(cat([q["rs"], q["asc"]], 0))]
    wide = [eu[:, n:], fp[:, n:], dv, q["dyv"], q["fall"], q["fall_before"], q["grow"]]
    lines = [q["bonus"], q["to_start"], q["to_end"], jnp.exp(-q["end"])]
    return narrow, deep, wide, lines


def final_part(r, k, v, kappa, eta, dy, narrow, deep, wide, lines, st, g):
    n = r.shape[0]
    eh, el, fh, fl, kgh, kgl, *exact = narrow
    by, ry = deep[:2], deep[2:]
    u_own, p_own, dv_own, dyv, fall, fall_before, grow = wide
    bonus, to_start, to_end, decay = lines
    vb, dyb = v.astype(BF16), dy.astype(BF16)
    sb = split(spread(st))
    gb = split(spread(g))
    u = u_own + dot3((eh, el), sb)
    p = p_own + dot3((fh, fl), gb, NT)
    dv = dv_own + dot3((kgh, kgl), gb, NT)
    zero = jnp.zeros((n, PAIR), BF16)
    gv = ((exact[0], exact[1], zero), (exact[2], exact[3], zero))
    gy = ((exact[4], exact[5], zero), (exact[6], exact[7], zero))
    gu, gp = gram_parts(u), gram_parts(p)
    row, col = iotas(2 * n, 2 * n)
    t, s = row & (n - 1), col & (n - 1)
    fwd_mask = t >= s + jnp.where(row >= n, 1, 0)
    bwd_mask = s >= t + jnp.where(col >= n, 1, 0)
    fwd = cat([jnp.where(fwd_mask, m, 0.0) for m in gram([gy, gp], [gu, gv])], 0)
    bwd = cat([jnp.where(bwd_mask, m, 0.0) for m in gram([gu, gv], [gy, gp])], 0)

    def apply(mat, y):
        mh, ml = split(mat)
        both = mm(mh, cat(y, 1))
        return by_head(both[:, :PAIR] + both[:, PAIR:] + mm(ml, y[0]))

    ra = apply(fwd, by)
    bk = apply(bwd, ry)
    uh, ul = split(u)
    ph, pl_ = split(p)
    start = dot3((cat([dyb, ph], 0), cat([zero, pl_], 0)), sb, NT)
    behind = dot3((cat([uh, vb], 0), cat([ul, zero], 0)), gb)
    dr = (ra[:n] + start[:n] * to_start) * fall
    da = (ra[n:] + start[n:] * to_start) * fall_before
    reach = grow * to_end
    final_u = behind[:n] * reach
    final_v = behind[n:] * reach
    db = bk[:n] * grow + final_u
    dk = bk[n:] * grow + final_v
    beta = kappa * eta
    inner = beta * final_u + k * final_v
    through = r * dr - k * dk - beta * db
    behind_a = -kappa * da
    row, col = iotas(n, n)
    from_here = jnp.where(col >= row, 1.0, 0.0).astype(BF16)
    after = jnp.where(col > row, 1.0, 0.0).astype(BF16)
    tail = mm(cat([from_here, from_here], 1), cat(split(through), 0)) + mm(
        cat([after, after], 1), cat(split(behind_a), 0)
    )
    turned = compact(flip(spread(st)))
    anchor = jnp.sum(turned * g, axis=0, keepdims=True) * decay + jnp.sum(
        inner, axis=0, keepdims=True
    )
    return (
        dr + bonus * k * dyv,
        dk + bonus * r * dyv,
        dv,
        -(tail + anchor),
        eta * db - da,
        kappa * db,
    )


def read_tokens(refs, p):
    lanes = slice(PAIR * p, PAIR * p + PAIR)
    return [ref[:, lanes].astype(F32) for ref in refs]


def final_kernel(*refs):
    ins, (state, narrow, deep, wide), outs = refs[:6], refs[6:10], refs[10:]
    got = [
        final_part(
            *read_tokens(ins, p),
            [narrow[p, i] for i in range(NARROW)],
            [deep[p, i] for i in range(DEEP)],
            [wide[p, i] for i in range(WIDE)],
            [state[p, BACK + 8 + i : BACK + 9 + i] for i in range(LINES)],
            state[p, 0:64],
            state[p, 64:128],
        )
        for p in (0, 1)
    ]
    for p in (0, 1):
        lanes = slice(PAIR * p, PAIR * p + PAIR)
        for ref, value in zip(outs, got[p]):
            ref[:, lanes] = value.astype(ref.dtype)
        outs[6][:, lanes] = state[p, BACK : BACK + 1]


ROW = 8
ROWS = 4
SEND = 192
BACK = 128
NARROW, DEEP, WIDE, LINES = 14, 4, 7, 4


def owner_of(p, d):
    return 4 * p + 2 * d


def adder_of(p, d):
    return owner_of(p, d) + 1


def joined(a, b):
    both = dot3(cat([b[1], b[2]], 0), cat([spread(a[1]), spread(a[0])], 1))
    return both[:HEAD, PAIR:] + b[0], both[:HEAD, :PAIR], both[HEAD:, :PAIR] + a[2]


def joined_states(a, b):
    both = dot3(b[1], cat([spread(a[1]), spread(a[0])], 1))
    return both[:, PAIR:] + b[0], both[:, :PAIR], None


def joined_adjoints(a, b):
    both = dot3(cat([b[1], b[2]], 0), spread(a[1]))
    return None, both[:HEAD], both[HEAD:] + a[2]


def copy_to(src, dst, ssem, rsem, where):
    return pltpu.make_async_remote_copy(
        src_ref=src,
        dst_ref=dst,
        send_sem=ssem,
        recv_sem=rsem,
        device_id=where,
        device_id_type=MESH,
    )


def front_kernel(*refs):
    (ins, outs, staged, scratch, sems) = refs[:8], refs[8:12], refs[12:20], refs[20:32], refs[32:]
    state, narrow, deep, wide = outs
    msg, recv, two, tot, xin, back, run, land, term, terms, sums, total = scratch
    in_sem, send_sem, recv_sem, xsend, xsem, osend, osem = sems[:7]
    tsend, tsem, ssend, ssem, gsend, gsem = sems[7:]
    d = lax.axis_index("dp")
    ctx = lax.axis_index("ctx")
    x = ctx // ROW
    z = ctx % ROW
    mine = [z == owner_of(p, d) for p in (0, 1)]
    is_owner = jnp.logical_or(*mine)
    pown = jnp.where(mine[1], 1, 0)
    adds = [z == adder_of(p, d) for p in (0, 1)]
    is_adder = jnp.logical_or(*adds)
    padd = jnp.where(adds[1], 1, 0)

    def at(xx, zz, dd=None):
        place = {"ctx": xx * ROW + zz}
        if dd is not None:
            place["dp"] = dd
        return place

    loads = [
        pltpu.make_async_copy(src, dst, in_sem.at[i])
        for i, (src, dst) in enumerate(zip(ins, staged))
    ]
    for load in loads:
        load.start()

    barrier = pltpu.get_barrier_semaphore()

    def greet(where):
        pl.semaphore_signal(barrier, inc=1, device_id=where, device_id_type=MESH)

    for p in (0, 1):
        for place in (owner_of(p, d), adder_of(p, d)):
            pl.when(z != place)(lambda place=place: greet(at(x, place)))

    @pl.when(is_owner | is_adder)
    def _():
        for j in (2, 3, 6, 7):
            greet(at(x, (2 * d + j) % ROW))

    @pl.when(is_owner)
    def _():
        for j in range(1, ROWS):
            greet(at((x + j) % ROWS, z))

    @pl.when(is_adder)
    def _():
        for j in range(1, ROWS):
            greet(at((x + j) % ROWS, z))
        for j in range(ROWS):
            greet(at((x + j) % ROWS, adder_of(padd, 1 - d), 1 - d))

    for load in loads:
        load.wait()
    parts = []
    for p in (0, 1):
        tokens = read_tokens(staged[:6] + staged[7:], p)
        parts.append(local_grams(*tokens, staged[6][:, PAIR * p : PAIR * p + PAIR]))
    solved = inverse(parts[0]["lw"] + parts[1]["lw"])

    def to_owner(p):
        place = jnp.where(is_owner, (z + 1) % ROW, owner_of(p, d))
        return copy_to(msg.at[p], recv.at[z], send_sem.at[p], recv_sem.at[z], at(x, place))

    pmate = 1 - padd

    def from_mate(p, slot, i, place):
        return copy_to(tot, two.at[i], send_sem.at[p], recv_sem.at[slot], place)

    messages = [local_message(parts[p], solved[2 * p : 2 * p + 2]) for p in (0, 1)]
    for p, (low, mid, high) in enumerate(messages):
        msg[p, 0:64] = low
        msg[p, 64:128] = mid
        msg[p, 128:192] = high
    pl.when(is_owner)(lambda: pl.semaphore_wait(barrier, ROW - 1 + ROWS - 1))
    pl.when(is_adder)(lambda: pl.semaphore_wait(barrier, ROW - 1 + 2 * ROWS - 1))
    pl.when(jnp.logical_not(is_owner | is_adder))(lambda: pl.semaphore_wait(barrier, 4))
    for p in (0, 1):
        direct = jnp.logical_not(mine[p] | adds[1 - p])
        pl.when(direct)(lambda p=p: to_owner(p).start())

    for p in (0, 1):
        term[p] = jnp.broadcast_to(bonus_terms(parts[p]), (8, PAIR))

    def over_mate(place):
        rows = pl.ds(64, 128)
        return copy_to(
            msg.at[pmate, rows], xin.at[x, rows], xsend.at[0], xsem.at[x], at(x, place)
        )

    @pl.when(is_adder)
    def _():
        far = (z + ROW - 1) % ROW
        over_mate(far).start()
        copy_to(
            msg.at[0], recv.at[far], send_sem.at[0], recv_sem.at[far], at(x, far)
        ).wait_recv()
        got = joined(
            (recv[far, 0:64], recv[far, 64:128], recv[far, 128:192]),
            (msg[pmate, 0:64], msg[pmate, 64:128], msg[pmate, 128:192]),
        )
        tot[0:64] = got[0]
        tot[64:128] = got[1]
        tot[128:192] = got[2]
        from_mate(pmate, z, z // 2, at(x, owner_of(pmate, d))).start()

    def to_adder(p):
        return copy_to(
            term.at[p], terms.at[z], tsend.at[p], tsem.at[z], at(x, adder_of(p, d))
        )

    for p in (0, 1):
        pl.when(jnp.logical_not(adds[p]))(lambda p=p: to_adder(p).start())

    for p in (0, 1):
        got = local_rest(parts[p])
        for ref, values in zip((narrow, deep, wide), got):
            for i, value in enumerate(values):
                ref[p, i] = value
        for i, line in enumerate(got[3]):
            state[p, BACK + 8 + i : BACK + 9 + i] = line

    @pl.when(is_adder)
    def _():
        terms[z] = term[padd]
        for j in range(1, ROW):
            zz = (z + j) % ROW
            copy_to(term.at[0], terms.at[zz], tsend.at[0], tsem.at[zz], at(x, zz)).wait_recv()
        part = terms[0]
        for i in range(1, ROW):
            part = part + terms[i]
        me = d * ROWS + x
        sums[me] = part
        places = [((x + j) % ROWS, d) for j in range(1, ROWS)]
        places += [((x + j) % ROWS, 1 - d) for j in range(ROWS)]
        across = [
            copy_to(
                sums.at[me], sums.at[me], ssend.at[i], ssem.at[me], at(xx, adder_of(padd, dd), dd)
            )
            for i, (xx, dd) in enumerate(places)
        ]
        for copy in across:
            copy.start()
        for xx, dd in places:
            slot = dd * ROWS + xx
            copy_to(
                sums.at[slot], sums.at[slot], ssend.at[0], ssem.at[slot], at(xx, z)
            ).wait_recv()
        part = sums[0]
        for i in range(1, 2 * ROWS):
            part = part + sums[i]
        total[padd] = part
        gives = [
            copy_to(total.at[padd], total.at[padd], gsend.at[j], gsem.at[padd], at(x, (z + j) % ROW))
            for j in range(1, ROW)
        ]
        for give in gives:
            give.start()
        for copy in across + gives:
            copy.wait_send()

    @pl.when(is_owner)
    def _():
        recv[z] = msg[pown]
        far = (z + ROW // 2) % ROW
        for zz in (far, far + 1):
            recv[zz] = jnp.zeros((SEND, PAIR), F32)
        places = [(z // 2 + j) % (ROW // 2) for j in (0, 1, 3)]
        for j, i in zip((0, 1, 3), places):
            for zz in (2 * i + 1,) if j == 0 else (2 * i, 2 * i + 1):
                copy_to(
                    msg.at[0], recv.at[zz], send_sem.at[0], recv_sem.at[zz], at(x, zz)
                ).wait_recv()
        blocks = [
            [(recv[zz, 0:64], recv[zz, 64:128], recv[zz, 128:192]) for zz in (2 * i, 2 * i + 1)]
            for i in places
        ]
        for i, got in zip(places, [joined(*both) for both in blocks]):
            two[i, 0:64] = got[0]
            two[i, 64:128] = got[1]
            two[i, 128:192] = got[2]
        from_mate(0, far + 1, far // 2, at(x, far + 1)).wait_recv()
        pair = [(two[i, 0:64], two[i, 64:128], two[i, 128:192]) for i in range(ROW // 2)]
        four = [joined(pair[0], pair[1]), joined(pair[2], pair[3])]
        whole = joined(four[0], four[1])
        tot[0:64] = whole[0]
        tot[64:128] = whole[1]
        tot[128:192] = whole[2]
        def rows_for(here, there):
            if there > here:
                return (0, 64) if here == 0 else (0, 128)
            return (128, 192) if here == ROWS - 1 else (64, 192)

        def rows_cases(act):
            for here in range(ROWS):

                @pl.when(x == here)
                def _(here=here):
                    for there in sorted(range(ROWS), key=lambda r: -abs(r - here)):
                        if there != here:
                            act(across(there, *rows_for(here, there), here))

        def across(xx, low, high, landing):
            rows = pl.ds(low, high - low)
            return copy_to(
                tot.at[rows], xin.at[landing, rows], xsend.at[xx], xsem.at[landing], at(xx, z)
            )

        rows_cases(lambda copy: copy.start())

        one = [(recv[i, 0:64], recv[i, 64:128], recv[i, 128:192]) for i in range(ROW)]
        before = [None, one[0], pair[0], None, four[0], None, None, None]
        before[3] = joined_states(pair[0], one[2])
        before[5] = joined_states(four[0], one[4])
        before[6] = joined_states(four[0], pair[2])
        before[7] = joined_states(before[6], one[6])
        behind = [None, None, None, four[1], None, pair[3], one[7], None]
        behind[4] = joined_adjoints(one[5], pair[3])
        behind[2] = joined_adjoints(one[3], four[1])
        behind[1] = joined_adjoints(pair[1], four[1])
        behind[0] = joined_adjoints(one[1], behind[1])

        for here in range(ROWS):

            @pl.when(x == here)
            def _(here=here):
                for there in range(ROWS):
                    if there != here:
                        across(there, *rows_for(there, here), there).wait_recv()
                start = end = jnp.zeros((HEAD, PAIR), F32)
                for there in range(here):
                    if there:
                        start = dot3(xin[there, 64:128], spread(start)) + xin[there, 0:64]
                    else:
                        start = xin[0, 0:64]
                for there in range(ROWS - 1, here, -1):
                    if there < ROWS - 1:
                        end = dot3(end, spread(xin[there, 64:128])) + xin[there, 128:192]
                    else:
                        end = xin[there, 128:192]
                run[0] = start
                run[1] = end

        sg, gg = run[0], run[1]
        moved = dot3(cat([before[i][1] for i in range(1, ROW)], 0), spread(sg))
        for i in range(ROW):
            back[i, 0:64] = sg if i == 0 else moved[64 * i - 64 : 64 * i] + before[i][0]
        gs = split(gg)
        for i in range(0, ROW, 2):
            if i + 1 < ROW - 1:
                got = dot3(gs, cat([spread(behind[i][1]), spread(behind[i + 1][1])], 1))
                back[i, 64:128] = got[:, :PAIR] + behind[i][2]
                back[i + 1, 64:128] = got[:, PAIR:] + behind[i + 1][2]
            else:
                back[i, 64:128] = dot3(gs, spread(behind[i][1])) + behind[i][2]
                back[i + 1, 64:128] = gg

        back[far + 1, 0:64] = back[far, 0:64]
        gives = []
        for j in (4, 5, 3, 2, 6, 1, 7):
            zz = (z + j) % ROW
            source = back.at[far + 1] if j == 4 else back.at[zz]
            gives.append(
                copy_to(source, land.at[pown], osend.at[j], osem.at[pown], at(x, zz))
            )
            gives[-1].start()
        land[pown] = back[z]
        for give in gives:
            give.wait_send()
        rows_cases(lambda copy: copy.wait_send())

    for p in (0, 1):

        @pl.when(jnp.logical_not(mine[p]))
        def _(p=p):
            to_owner(p).wait_send()
            copy_to(
                back.at[0], land.at[p], osend.at[0], osem.at[p], at(x, owner_of(p, d))
            ).wait_recv()

        @pl.when(adds[1 - p])
        def _(p=p):
            far = (z + ROW - 1) % ROW
            land[p, 0:64] = dot3(recv[far, 64:128], spread(land[p, 0:64])) + recv[far, 0:64]

        @pl.when(mine[1 - p])
        def _(p=p):
            over_mate(z).wait_recv()
            over = dot3(land[p, 64:128], spread(xin[x, 64:128]))
            land[p, 64:128] = over + xin[x, 128:192]

    for p in (0, 1):

        @pl.when(jnp.logical_not(adds[p]))
        def _(p=p):
            to_adder(p).wait_send()
            copy_to(
                total.at[p], total.at[p], gsend.at[0], gsem.at[p], at(x, adder_of(p, d))
            ).wait_recv()

    @pl.when(is_adder)
    def _():
        over_mate(z).wait_send()

    for p in (0, 1):
        state[p, 0:BACK] = land[p]
        state[p, BACK : BACK + 8] = total[p]


VMEM = pl.BlockSpec(memory_space=pltpu.VMEM)
HBM = pl.BlockSpec(memory_space=pltpu.HBM)


def local(r, k, v, w, kappa, eta, extra, dy):
    rows, width = r.shape[1], r.shape[2]
    pairs = width // PAIR
    flat = [t.reshape(rows, width) for t in (r, k, v, w, kappa, eta)]
    ins = (*flat, extra.reshape(1, width), dy.reshape(rows, width))
    f32 = lambda *shape: jax.ShapeDtypeStruct(shape, F32)
    dma = lambda n: pltpu.SemaphoreType.DMA((n,))
    bf16 = lambda *shape: jax.ShapeDtypeStruct(shape, BF16)
    kept = pl.pallas_call(
        front_kernel,
        out_shape=(
            f32(pairs, BACK + 16, PAIR),
            bf16(pairs, NARROW, rows, PAIR),
            bf16(pairs, DEEP, 2 * rows, PAIR),
            f32(pairs, WIDE, rows, PAIR),
        ),
        in_specs=[HBM] * 8,
        out_specs=[VMEM] * 4,
        scratch_shapes=[
            *[pltpu.VMEM(t.shape, t.dtype) for t in ins],
            pltpu.VMEM((pairs, SEND, PAIR), F32),
            pltpu.VMEM((ROW, SEND, PAIR), F32),
            pltpu.VMEM((ROW // 2, SEND, PAIR), F32),
            pltpu.VMEM((SEND, PAIR), F32),
            pltpu.VMEM((ROWS, SEND, PAIR), F32),
            pltpu.VMEM((ROW, BACK, PAIR), F32),
            pltpu.VMEM((2, HEAD, PAIR), F32),
            pltpu.VMEM((pairs, BACK, PAIR), F32),
            pltpu.VMEM((pairs, 8, PAIR), F32),
            pltpu.VMEM((ROW, 8, PAIR), F32),
            pltpu.VMEM((2 * ROWS, 8, PAIR), F32),
            pltpu.VMEM((pairs, 8, PAIR), F32),
            *[dma(n) for n in (8, 2, ROW, ROWS, ROWS, ROW, 2)],
            *[dma(n) for n in (2, ROW, 2 * ROWS, 2 * ROWS, ROW, 2)],
        ],
        compiler_params=pltpu.CompilerParams(
            collective_id=0, has_side_effects=True, vmem_limit_bytes=48 * 1024 * 1024
        ),
    )(*[pltpu.with_memory_space_constraint(t, pltpu.HBM) for t in ins])
    *grads, bonus = pl.pallas_call(
        final_kernel,
        out_shape=(*[bf16(rows, width)] * 6, f32(1, width)),
        in_specs=[VMEM] * 10,
        out_specs=[VMEM] * 7,
        compiler_params=pltpu.CompilerParams(vmem_limit_bytes=40 * 1024 * 1024),
    )(*[ins[i] for i in (0, 1, 2, 4, 5, 7)], *kept)
    return (*[t.reshape(1, rows, width) for t in grads], bonus.reshape(width))


def solution(mesh):
    block = P("dp", "ctx", "tp")
    return jax.shard_map(
        local,
        mesh=mesh,
        in_specs=(block,) * 6 + (P("tp"), block),
        out_specs=(block,) * 6 + (P("tp"),),
        check_vma=False,
    )
```

```python
import functools

import jax
import jax.numpy as jnp
from jax import lax
from jax.experimental import pallas as pl
from jax.experimental.pallas import tpu as pltpu
from jax.sharding import PartitionSpec as P

HEAD = 64
PAIR = 128
F32 = jnp.float32
BF16 = jnp.bfloat16
MESH = pl.DeviceIdType.MESH
NN = (((1,), (0,)), ((), ()))
NT = (((1,), (1,)), ((), ()))


def split(x):
    high = x.astype(BF16)
    low = (x - high.astype(F32)).astype(BF16)
    return high, low


def mm(x, y, dims=NN):
    return lax.dot_general(x, y, dims, preferred_element_type=F32)


def cat(parts, axis):
    return jnp.concatenate(parts, axis=axis)


def dot3(x, y, dims=NN):
    xh, xl = split(x) if not isinstance(x, tuple) else x
    yh, yl = split(y) if not isinstance(y, tuple) else y
    axis = 0 if dims is NN else 1
    if yh.shape == (PAIR, PAIR):
        wide = cat([cat([yh, yl], 1 - axis)] * 2, axis)
        both = mm(cat([xh, xl], 1), wide, dims)
        return both[:, :PAIR] + both[:, PAIR:]
    return mm(cat([xh, xl], 1), cat([yh, yh], axis), dims) + mm(xh, yl, dims)


def dot2(x, y, dims=NN):
    xh, xl = split(x) if not isinstance(x, tuple) else x
    axis = 0 if dims is NN else 1
    return mm(cat([xh, xl], 1), cat([y, y], axis), dims)


def iotas(rows, cols):
    return (
        lax.broadcasted_iota(jnp.int32, (rows, cols), 0),
        lax.broadcasted_iota(jnp.int32, (rows, cols), 1),
    )


def first_half(shape):
    return (lax.broadcasted_iota(jnp.int32, shape, 1) & (PAIR - 1)) < HEAD


def by_head(stacked):
    half = stacked.shape[0] // 2
    top, bottom = stacked[:half], stacked[half:]
    return jnp.where(first_half(top.shape), top, bottom)


def own_lanes(x):
    mine = first_half(x.shape)
    return jnp.where(mine, x, 0.0), jnp.where(mine, 0.0, x)


def compact(blocks):
    return by_head(blocks)


def spread(x):
    return cat(list(own_lanes(x)), 0)


def turned_lanes(x):
    return pltpu.roll(x, HEAD, 1)


def gram_parts(x):
    high = x.astype(BF16).astype(F32)
    low = x - high
    high_t, low_t = turned_lanes(high), turned_lanes(low)
    mine = first_half(x.shape)
    pick = lambda a, b: jnp.where(mine, a, b).astype(BF16)
    return (
        (pick(high, low_t), pick(high, high_t), pick(low, low_t)),
        (pick(high_t, low), pick(high_t, high), pick(low_t, low)),
    )


def gram(lefts, rights):
    out = []
    for h in (0, 1):
        left = cat([x[h][0] for x in lefts], 0)
        right = [cat([x[h][i] for x in rights], 0) for i in (1, 2)]
        out.append(mm(cat([left, left], 1), cat(right, 1), NT))
    return out


def flip(x):
    return jnp.swapaxes(x, 0, 1)


def prepare(r, k, w, kappa, eta):
    n = w.shape[0]
    row, col = iotas(n, n)
    tri = jnp.where(row >= col, 1.0, 0.0).astype(BF16)
    wh = w.astype(BF16)
    rest = w - wh.astype(F32)
    wm = rest.astype(BF16)
    wl = (rest - wm.astype(F32)).astype(BF16)
    c = mm(cat([tri, tri], 1), cat([wh, wm], 0)) + mm(tri, wl)
    mid = c[n // 2 : n // 2 + 1]
    end = c[n - 1 : n]
    grow = jnp.exp(c - mid)
    fall = jnp.exp(mid - c)
    fall_before = jnp.exp(mid - (c - w))
    beta = kappa * eta
    out = dict(
        end=end,
        grow=grow,
        fall=fall,
        fall_before=fall_before,
        to_start=jnp.exp(-mid),
        to_end=jnp.exp(mid - end),
        beta=beta,
        rs=r * fall,
        ks=k * grow,
        bs=beta * grow,
        asc=-kappa * fall_before,
    )
    out["a0"] = out["asc"] * out["to_start"]
    out["r0"] = out["rs"] * out["to_start"]
    out["bf"] = out["bs"] * out["to_end"]
    out["kf"] = out["ks"] * out["to_end"]
    return out


def inverse(lows):
    n = lows[0].shape[0]
    row, col = iotas(n, n)
    eye = jnp.where(row == col, 1.0, 0.0)
    start = (row >> 4) == (col >> 4)
    d1 = [jnp.where(start, low, 0.0) for low in lows]
    s1 = [split(d) for d in d1]
    d2 = [dot3(s, s) for s in s1]
    s2 = [split(d) for d in d2]
    d4 = [dot3(s, s) for s in s2]
    p4 = [eye + a + b + dot3(s, t) for a, b, s, t in zip(d1, d2, s1, s2)]
    s4 = [split(d) for d in d4]
    d8 = [dot3(s, s) for s in s4]
    p8 = [p + dot3(p, s) for p, s in zip(p4, s4)]
    t = [split(p + dot3(p, d)) for p, d in zip(p8, d8)]
    rest = [jnp.where(start, 0.0, low) for low in lows]
    x1 = [split(dot3(s, r)) for s, r in zip(t, rest)]
    x2 = [split(dot3(s, s)) for s in x1]
    y1 = [a[0].astype(F32) + a[1].astype(F32) + dot3(s, a) for s, a in zip(x1, t)]
    x4 = [split(dot3(s, s)) for s in x2]
    y2 = [y + dot3(s, y) for s, y in zip(x2, y1)]
    return [y + dot3(s, y) for s, y in zip(x4, y2)]


def local_grams(r, k, v, w, kappa, eta, dy, bonus):
    n = w.shape[0]
    q = prepare(r, k, w, kappa, eta)
    q.update(r=r, k=k, v=v, dy=dy, bonus=bonus, vb=v.astype(BF16), dyb=dy.astype(BF16))
    row, col = iotas(n, n)
    pa, pr, pb, pk = [gram_parts(q[name]) for name in ("asc", "rs", "bs", "ks")]
    lower = gram([pa], [pb, pk])
    upper = gram([pb], [pr])
    q["late"] = pk, pr, pa
    q["lw"] = [jnp.where(row > col, t[:, :n], 0.0) for t in lower]
    q["lk"] = cat([jnp.where(row > col, t[:, n:], 0.0) for t in lower], 0)
    q["wwt"] = cat([jnp.where(col >= row, t, 0.0) for t in upper], 0)
    q["z"] = by_head(dot2(q["lk"], q["vb"]))
    q["zd"] = by_head(dot2(q["wwt"], q["dyb"]))
    return q


def local_message(q, t):
    n = q["z"].shape[0]
    eu = by_head(dot3(cat(t, 0), cat([q["a0"], q["z"]], 1)))
    fp = by_head(dot3(cat([flip(x) for x in t], 0), cat([q["bf"], q["zd"]], 1)))
    ml = dot3(flip(q["bf"]), eu)
    row, col = iotas(HEAD, PAIR)
    decay = jnp.where(row == (col & (HEAD - 1)), jnp.exp(-q["end"]), 0.0)
    mt = decay + compact(ml[:, :n])
    lt = compact(ml[:, n:] + dot2(flip(q["kf"]), q["vb"]))
    ht = compact(flip(dot3(flip(q["a0"]), fp[:, n:]) + dot2(flip(q["r0"]), q["dyb"])))
    q.update(eu=eu, fp=fp)
    return lt, mt, ht


def bonus_terms(q):
    row, col = iotas(PAIR, PAIR)
    ones = jnp.where((row >> 6) == (col >> 6), 1.0, 0.0).astype(BF16)
    dyv = dot2(q["dy"] * q["v"], ones)
    q.update(ones=ones, dyv=dyv)
    return jnp.sum(dyv * q["r"] * q["k"], axis=0, keepdims=True)


def exact_parts(x):
    other = turned_lanes(x)
    mine = first_half(x.shape)
    pick = lambda a, b: jnp.where(mine, a, b).astype(BF16)
    return pick(x, 0.0), pick(x, other), pick(other, 0.0), pick(other, x)


def local_rest(q):
    n = q["z"].shape[0]
    eu, fp = q["eu"], q["fp"]
    pk, pr, pa = q["late"]
    upper = gram([pk], [pr, pa])
    row, col = iotas(n, n)
    wkt = cat([jnp.where(col >= row, t[:, :n], 0.0) for t in upper], 0)
    lkt = cat([jnp.where(col > row, t[:, n:], 0.0) for t in upper], 0)
    more = by_head(dot3(lkt, fp))
    kg = q["kf"] + more[:, :n]
    dv = more[:, n:] + by_head(dot2(wkt, q["dyb"]))
    dv = dv + dot2(q["r"] * q["k"] * q["bonus"], q["ones"]) * q["dy"]
    narrow = [*split(eu[:, :n]), *split(fp[:, :n]), *split(kg)]
    narrow += [*exact_parts(q["v"]), *exact_parts(q["dy"])]
    deep = [*split(cat([q["bs"], q["ks"]], 0)), *split(cat([q["rs"], q["asc"]], 0))]
    wide = [eu[:, n:], fp[:, n:], dv, q["dyv"], q["fall"], q["fall_before"], q["grow"]]
    lines = [q["bonus"], q["to_start"], q["to_end"], jnp.exp(-q["end"])]
    return narrow, deep, wide, lines


def final_part(r, k, v, kappa, eta, dy, narrow, deep, wide, lines, st, g):
    n = r.shape[0]
    eh, el, fh, fl, kgh, kgl, *exact = narrow
    by, ry = deep[:2], deep[2:]
    u_own, p_own, dv_own, dyv, fall, fall_before, grow = wide
    bonus, to_start, to_end, decay = lines
    vb, dyb = v.astype(BF16), dy.astype(BF16)
    sb = split(spread(st))
    gb = split(spread(g))
    u = u_own + dot3((eh, el), sb)
    p = p_own + dot3((fh, fl), gb, NT)
    dv = dv_own + dot3((kgh, kgl), gb, NT)
    zero = jnp.zeros((n, PAIR), BF16)
    gv = ((exact[0], exact[1], zero), (exact[2], exact[3], zero))
    gy = ((exact[4], exact[5], zero), (exact[6], exact[7], zero))
    gu, gp = gram_parts(u), gram_parts(p)
    row, col = iotas(2 * n, 2 * n)
    t, s = row & (n - 1), col & (n - 1)
    fwd_mask = t >= s + jnp.where(row >= n, 1, 0)
    bwd_mask = s >= t + jnp.where(col >= n, 1, 0)
    fwd = cat([jnp.where(fwd_mask, m, 0.0) for m in gram([gy, gp], [gu, gv])], 0)
    bwd = cat([jnp.where(bwd_mask, m, 0.0) for m in gram([gu, gv], [gy, gp])], 0)

    def apply(mat, y):
        mh, ml = split(mat)
        return by_head(mm(cat([mh, ml, mh], 1), cat([y[0], y[0], y[1]], 0)))

    ra = apply(fwd, by)
    bk = apply(bwd, ry)
    uh, ul = split(u)
    ph, pl_ = split(p)
    start = dot3((cat([dyb, ph], 0), cat([zero, pl_], 0)), sb, NT)
    behind = dot3((cat([uh, vb], 0), cat([ul, zero], 0)), gb)
    dr = (ra[:n] + start[:n] * to_start) * fall
    da = (ra[n:] + start[n:] * to_start) * fall_before
    reach = grow * to_end
    final_u = behind[:n] * reach
    final_v = behind[n:] * reach
    db = bk[:n] * grow + final_u
    dk = bk[n:] * grow + final_v
    beta = kappa * eta
    inner = beta * final_u + k * final_v
    through = r * dr - k * dk - beta * db
    behind_a = -kappa * da
    row, col = iotas(n, n)
    from_here = jnp.where(col >= row, 1.0, 0.0).astype(BF16)
    after = jnp.where(col > row, 1.0, 0.0).astype(BF16)
    tail = mm(cat([from_here, from_here], 1), cat(split(through), 0)) + mm(
        cat([after, after], 1), cat(split(behind_a), 0)
    )
    turned = compact(flip(spread(st)))
    anchor = jnp.sum(turned * g, axis=0, keepdims=True) * decay + jnp.sum(
        inner, axis=0, keepdims=True
    )
    return (
        dr + bonus * k * dyv,
        dk + bonus * r * dyv,
        dv,
        -(tail + anchor),
        eta * db - da,
        kappa * db,
    )


def read_tokens(refs, p):
    lanes = slice(PAIR * p, PAIR * p + PAIR)
    return [ref[:, lanes].astype(F32) for ref in refs]


def final_kernel(*refs):
    ins, (state, narrow, deep, wide), outs = refs[:6], refs[6:10], refs[10:]
    got = [
        final_part(
            *read_tokens(ins, p),
            [narrow[p, i] for i in range(NARROW)],
            [deep[p, i] for i in range(DEEP)],
            [wide[p, i] for i in range(WIDE)],
            [state[p, BACK + 8 + i : BACK + 9 + i] for i in range(LINES)],
            state[p, 0:64],
            state[p, 64:128],
        )
        for p in (0, 1)
    ]
    for p in (0, 1):
        lanes = slice(PAIR * p, PAIR * p + PAIR)
        for ref, value in zip(outs, got[p]):
            ref[:, lanes] = value.astype(ref.dtype)
        outs[6][:, lanes] = state[p, BACK : BACK + 1]


ROW = 8
ROWS = 4
SEND = 192
BACK = 128
NARROW, DEEP, WIDE, LINES = 14, 4, 7, 4


def owner_of(p, d):
    return 4 * p + 2 * d


def adder_of(p, d):
    return owner_of(p, d) + 1


def joined(a, b):
    both = dot3(cat([b[1], b[2]], 0), cat([spread(a[1]), spread(a[0])], 1))
    return both[:HEAD, PAIR:] + b[0], both[:HEAD, :PAIR], both[HEAD:, :PAIR] + a[2]


def joined_states(a, b):
    both = dot3(b[1], cat([spread(a[1]), spread(a[0])], 1))
    return both[:, PAIR:] + b[0], both[:, :PAIR], None


def joined_adjoints(a, b):
    both = dot3(cat([b[1], b[2]], 0), spread(a[1]))
    return None, both[:HEAD], both[HEAD:] + a[2]


def copy_to(src, dst, ssem, rsem, where):
    return pltpu.make_async_remote_copy(
        src_ref=src,
        dst_ref=dst,
        send_sem=ssem,
        recv_sem=rsem,
        device_id=where,
        device_id_type=MESH,
    )


def front_kernel(*refs):
    (ins, outs, staged, scratch, sems) = refs[:8], refs[8:12], refs[12:20], refs[20:32], refs[32:]
    state, narrow, deep, wide = outs
    msg, recv, two, tot, xin, back, run, land, term, terms, sums, total = scratch
    in_sem, send_sem, recv_sem, xsend, xsem, osend, osem = sems[:7]
    tsend, tsem, ssend, ssem, gsend, gsem = sems[7:]
    d = lax.axis_index("dp")
    ctx = lax.axis_index("ctx")
    x = ctx // ROW
    z = ctx % ROW
    mine = [z == owner_of(p, d) for p in (0, 1)]
    is_owner = jnp.logical_or(*mine)
    pown = jnp.where(mine[1], 1, 0)
    adds = [z == adder_of(p, d) for p in (0, 1)]
    is_adder = jnp.logical_or(*adds)
    padd = jnp.where(adds[1], 1, 0)

    def at(xx, zz, dd=None):
        place = {"ctx": xx * ROW + zz}
        if dd is not None:
            place["dp"] = dd
        return place

    loads = [
        pltpu.make_async_copy(src, dst, in_sem.at[i])
        for i, (src, dst) in enumerate(zip(ins, staged))
    ]
    for load in loads:
        load.start()

    barrier = pltpu.get_barrier_semaphore()

    def greet(where):
        pl.semaphore_signal(barrier, inc=1, device_id=where, device_id_type=MESH)

    for p in (0, 1):
        for place in (owner_of(p, d), adder_of(p, d)):
            pl.when(z != place)(lambda place=place: greet(at(x, place)))

    @pl.when(is_owner | is_adder)
    def _():
        for j in (2, 3, 6, 7):
            greet(at(x, (2 * d + j) % ROW))

    @pl.when(is_owner)
    def _():
        for j in range(1, ROWS):
            greet(at((x + j) % ROWS, z))

    @pl.when(is_adder)
    def _():
        for j in range(1, ROWS):
            greet(at((x + j) % ROWS, z))
        for j in range(ROWS):
            greet(at((x + j) % ROWS, adder_of(padd, 1 - d), 1 - d))

    for load in loads:
        load.wait()
    parts = []
    for p in (0, 1):
        tokens = read_tokens(staged[:6] + staged[7:], p)
        parts.append(local_grams(*tokens, staged[6][:, PAIR * p : PAIR * p + PAIR]))
    solved = inverse(parts[0]["lw"] + parts[1]["lw"])

    def to_owner(p):
        place = jnp.where(is_owner, (z + 1) % ROW, owner_of(p, d))
        return copy_to(msg.at[p], recv.at[z], send_sem.at[p], recv_sem.at[z], at(x, place))

    pmate = 1 - padd

    def from_mate(p, slot, i, place):
        return copy_to(tot, two.at[i], send_sem.at[p], recv_sem.at[slot], place)

    messages = [local_message(parts[p], solved[2 * p : 2 * p + 2]) for p in (0, 1)]
    for p, (low, mid, high) in enumerate(messages):
        msg[p, 0:64] = low
        msg[p, 64:128] = mid
        msg[p, 128:192] = high
    pl.when(is_owner)(lambda: pl.semaphore_wait(barrier, ROW - 1 + ROWS - 1))
    pl.when(is_adder)(lambda: pl.semaphore_wait(barrier, ROW - 1 + 2 * ROWS - 1))
    pl.when(jnp.logical_not(is_owner | is_adder))(lambda: pl.semaphore_wait(barrier, 4))
    for p in (0, 1):
        direct = jnp.logical_not(mine[p] | adds[1 - p])
        pl.when(direct)(lambda p=p: to_owner(p).start())

    for p in (0, 1):
        term[p] = jnp.broadcast_to(bonus_terms(parts[p]), (8, PAIR))

    def over_mate(place):
        rows = pl.ds(64, 128)
        return copy_to(
            msg.at[pmate, rows], xin.at[x, rows], xsend.at[0], xsem.at[x], at(x, place)
        )

    @pl.when(is_adder)
    def _():
        far = (z + ROW - 1) % ROW
        over_mate(far).start()
        copy_to(
            msg.at[0], recv.at[far], send_sem.at[0], recv_sem.at[far], at(x, far)
        ).wait_recv()
        got = joined(
            (recv[far, 0:64], recv[far, 64:128], recv[far, 128:192]),
            (msg[pmate, 0:64], msg[pmate, 64:128], msg[pmate, 128:192]),
        )
        tot[0:64] = got[0]
        tot[64:128] = got[1]
        tot[128:192] = got[2]
        from_mate(pmate, z, z // 2, at(x, owner_of(pmate, d))).start()

    def to_adder(p):
        return copy_to(
            term.at[p], terms.at[z], tsend.at[p], tsem.at[z], at(x, adder_of(p, d))
        )

    for p in (0, 1):
        pl.when(jnp.logical_not(adds[p]))(lambda p=p: to_adder(p).start())

    for p in (0, 1):
        got = local_rest(parts[p])
        for ref, values in zip((narrow, deep, wide), got):
            for i, value in enumerate(values):
                ref[p, i] = value
        for i, line in enumerate(got[3]):
            state[p, BACK + 8 + i : BACK + 9 + i] = line

    @pl.when(is_adder)
    def _():
        terms[z] = term[padd]
        for j in range(1, ROW):
            zz = (z + j) % ROW
            copy_to(term.at[0], terms.at[zz], tsend.at[0], tsem.at[zz], at(x, zz)).wait_recv()
        part = terms[0]
        for i in range(1, ROW):
            part = part + terms[i]
        me = d * ROWS + x
        sums[me] = part
        places = [((x + j) % ROWS, d) for j in range(1, ROWS)]
        places += [((x + j) % ROWS, 1 - d) for j in range(ROWS)]
        across = [
            copy_to(
                sums.at[me], sums.at[me], ssend.at[i], ssem.at[me], at(xx, adder_of(padd, dd), dd)
            )
            for i, (xx, dd) in enumerate(places)
        ]
        for copy in across:
            copy.start()
        for xx, dd in places:
            slot = dd * ROWS + xx
            copy_to(
                sums.at[slot], sums.at[slot], ssend.at[0], ssem.at[slot], at(xx, z)
            ).wait_recv()
        part = sums[0]
        for i in range(1, 2 * ROWS):
            part = part + sums[i]
        total[padd] = part
        gives = [
            copy_to(total.at[padd], total.at[padd], gsend.at[j], gsem.at[padd], at(x, (z + j) % ROW))
            for j in range(1, ROW)
        ]
        for give in gives:
            give.start()
        for copy in across + gives:
            copy.wait_send()

    @pl.when(is_owner)
    def _():
        recv[z] = msg[pown]
        far = (z + ROW // 2) % ROW
        for zz in (far, far + 1):
            recv[zz] = jnp.zeros((SEND, PAIR), F32)
        places = [(z // 2 + j) % (ROW // 2) for j in (0, 1, 3)]
        for j, i in zip((0, 1, 3), places):
            for zz in (2 * i + 1,) if j == 0 else (2 * i, 2 * i + 1):
                copy_to(
                    msg.at[0], recv.at[zz], send_sem.at[0], recv_sem.at[zz], at(x, zz)
                ).wait_recv()
        blocks = [
            [(recv[zz, 0:64], recv[zz, 64:128], recv[zz, 128:192]) for zz in (2 * i, 2 * i + 1)]
            for i in places
        ]
        for i, got in zip(places, [joined(*both) for both in blocks]):
            two[i, 0:64] = got[0]
            two[i, 64:128] = got[1]
            two[i, 128:192] = got[2]
        from_mate(0, far + 1, far // 2, at(x, far + 1)).wait_recv()
        pair = [(two[i, 0:64], two[i, 64:128], two[i, 128:192]) for i in range(ROW // 2)]
        four = [joined(pair[0], pair[1]), joined(pair[2], pair[3])]
        whole = joined(four[0], four[1])
        tot[0:64] = whole[0]
        tot[64:128] = whole[1]
        tot[128:192] = whole[2]
        cases = (
            (lambda xx: (xx > x) & (x == 0), 0, 64),
            (lambda xx: (xx > x) & (x != 0), 0, 128),
            (lambda xx: (xx < x) & (x == ROWS - 1), 128, 192),
            (lambda xx: (xx < x) & (x != ROWS - 1), 64, 192),
        )

        def across(xx, low, high, landing):
            rows = pl.ds(low, high - low)
            return copy_to(
                tot.at[rows], xin.at[landing, rows], xsend.at[xx], xsem.at[landing], at(xx, z)
            )

        for xx in range(ROWS):
            for when, low, high in cases:
                pl.when(when(xx))(
                    lambda xx=xx, low=low, high=high: across(xx, low, high, x).start()
                )
        one = [(recv[i, 0:64], recv[i, 64:128], recv[i, 128:192]) for i in range(ROW)]
        before = [None, one[0], pair[0], None, four[0], None, None, None]
        before[3] = joined_states(pair[0], one[2])
        before[5] = joined_states(four[0], one[4])
        before[6] = joined_states(four[0], pair[2])
        before[7] = joined_states(before[6], one[6])
        behind = [None, None, None, four[1], None, pair[3], one[7], None]
        behind[4] = joined_adjoints(one[5], pair[3])
        behind[2] = joined_adjoints(one[3], four[1])
        behind[1] = joined_adjoints(pair[1], four[1])
        behind[0] = joined_adjoints(one[1], behind[1])

        run[...] = jnp.zeros_like(run)
        for xx in range(ROWS - 1):
            high = 64 if xx == 0 else 128

            @pl.when(x > xx)
            def _(xx=xx, high=high):
                across(xx, 0, high, xx).wait_recv()
                if xx == 0:
                    run[0] = xin[0, 0:64]
                else:
                    run[0] = dot3(xin[xx, 64:128], spread(run[0])) + xin[xx, 0:64]

        for xx in range(ROWS - 1, 0, -1):
            low = 128 if xx == ROWS - 1 else 64

            @pl.when(x < xx)
            def _(xx=xx, low=low):
                across(xx, low, 192, xx).wait_recv()
                if xx == ROWS - 1:
                    run[1] = xin[xx, 128:192]
                else:
                    run[1] = dot3(run[1], spread(xin[xx, 64:128])) + xin[xx, 128:192]

        sg, gg = run[0], run[1]
        moved = dot3(cat([before[i][1] for i in range(1, ROW)], 0), spread(sg))
        for i in range(ROW):
            back[i, 0:64] = sg if i == 0 else moved[64 * i - 64 : 64 * i] + before[i][0]
        gs = split(gg)
        for i in range(0, ROW, 2):
            if i + 1 < ROW - 1:
                got = dot3(gs, cat([spread(behind[i][1]), spread(behind[i + 1][1])], 1))
                back[i, 64:128] = got[:, :PAIR] + behind[i][2]
                back[i + 1, 64:128] = got[:, PAIR:] + behind[i + 1][2]
            else:
                back[i, 64:128] = dot3(gs, spread(behind[i][1])) + behind[i][2]
                back[i + 1, 64:128] = gg

        back[far + 1, 0:64] = back[far, 0:64]
        gives = []
        for j in (4, 5, 3, 2, 6, 1, 7):
            zz = (z + j) % ROW
            source = back.at[far + 1] if j == 4 else back.at[zz]
            gives.append(
                copy_to(source, land.at[pown], osend.at[j], osem.at[pown], at(x, zz))
            )
            gives[-1].start()
        land[pown] = back[z]
        for give in gives:
            give.wait_send()
        for xx in range(ROWS):
            for when, low, high in cases:
                pl.when(when(xx))(
                    lambda xx=xx, low=low, high=high: across(xx, low, high, x).wait_send()
                )

    for p in (0, 1):

        @pl.when(jnp.logical_not(mine[p]))
        def _(p=p):
            to_owner(p).wait_send()
            copy_to(
                back.at[0], land.at[p], osend.at[0], osem.at[p], at(x, owner_of(p, d))
            ).wait_recv()

        @pl.when(adds[1 - p])
        def _(p=p):
            far = (z + ROW - 1) % ROW
            land[p, 0:64] = dot3(recv[far, 64:128], spread(land[p, 0:64])) + recv[far, 0:64]

        @pl.when(mine[1 - p])
        def _(p=p):
            over_mate(z).wait_recv()
            over = dot3(land[p, 64:128], spread(xin[x, 64:128]))
            land[p, 64:128] = over + xin[x, 128:192]

    for p in (0, 1):

        @pl.when(jnp.logical_not(adds[p]))
        def _(p=p):
            to_adder(p).wait_send()
            copy_to(
                total.at[p], total.at[p], gsend.at[0], gsem.at[p], at(x, adder_of(p, d))
            ).wait_recv()

    @pl.when(is_adder)
    def _():
        over_mate(z).wait_send()

    for p in (0, 1):
        state[p, 0:BACK] = land[p]
        state[p, BACK : BACK + 8] = total[p]


VMEM = pl.BlockSpec(memory_space=pltpu.VMEM)
HBM = pl.BlockSpec(memory_space=pltpu.HBM)


def local(r, k, v, w, kappa, eta, extra, dy):
    rows, width = r.shape[1], r.shape[2]
    pairs = width // PAIR
    flat = [t.reshape(rows, width) for t in (r, k, v, w, kappa, eta)]
    ins = (*flat, extra.reshape(1, width), dy.reshape(rows, width))
    f32 = lambda *shape: jax.ShapeDtypeStruct(shape, F32)
    dma = lambda n: pltpu.SemaphoreType.DMA((n,))
    bf16 = lambda *shape: jax.ShapeDtypeStruct(shape, BF16)
    kept = pl.pallas_call(
        front_kernel,
        out_shape=(
            f32(pairs, BACK + 16, PAIR),
            bf16(pairs, NARROW, rows, PAIR),
            bf16(pairs, DEEP, 2 * rows, PAIR),
            f32(pairs, WIDE, rows, PAIR),
        ),
        in_specs=[HBM] * 8,
        out_specs=[VMEM] * 4,
        scratch_shapes=[
            *[pltpu.VMEM(t.shape, t.dtype) for t in ins],
            pltpu.VMEM((pairs, SEND, PAIR), F32),
            pltpu.VMEM((ROW, SEND, PAIR), F32),
            pltpu.VMEM((ROW // 2, SEND, PAIR), F32),
            pltpu.VMEM((SEND, PAIR), F32),
            pltpu.VMEM((ROWS, SEND, PAIR), F32),
            pltpu.VMEM((ROW, BACK, PAIR), F32),
            pltpu.VMEM((2, HEAD, PAIR), F32),
            pltpu.VMEM((pairs, BACK, PAIR), F32),
            pltpu.VMEM((pairs, 8, PAIR), F32),
            pltpu.VMEM((ROW, 8, PAIR), F32),
            pltpu.VMEM((2 * ROWS, 8, PAIR), F32),
            pltpu.VMEM((pairs, 8, PAIR), F32),
            *[dma(n) for n in (8, 2, ROW, ROWS, ROWS, ROW, 2)],
            *[dma(n) for n in (2, ROW, 2 * ROWS, 2 * ROWS, ROW, 2)],
        ],
        compiler_params=pltpu.CompilerParams(
            collective_id=0, has_side_effects=True, vmem_limit_bytes=48 * 1024 * 1024
        ),
    )(*[pltpu.with_memory_space_constraint(t, pltpu.HBM) for t in ins])
    *grads, bonus = pl.pallas_call(
        final_kernel,
        out_shape=(*[bf16(rows, width)] * 6, f32(1, width)),
        in_specs=[VMEM] * 10,
        out_specs=[VMEM] * 7,
        compiler_params=pltpu.CompilerParams(vmem_limit_bytes=40 * 1024 * 1024),
    )(*[ins[i] for i in (0, 1, 2, 4, 5, 7)], *kept)
    return (*[t.reshape(1, rows, width) for t in grads], bonus.reshape(width))


def solution(mesh):
    block = P("dp", "ctx", "tp")
    return jax.shard_map(
        local,
        mesh=mesh,
        in_specs=(block,) * 6 + (P("tp"), block),
        out_specs=(block,) * 6 + (P("tp"),),
        check_vma=False,
    )
```
